512 devices in a mesh: replica: 32 (over y, x), tensor: 16 (over z, core).
Axes of the slice: x: 4, y: 8, z: 8, core: 2. Of those that a mesh axis runs over, the one named last changes fastest.
Arguments:
- tokens_x: bfloat16 [4096, 8192], P('replica', 'tensor'), may hold values from -6 to 6
- cotangent: bfloat16 [256, 4096], P('tensor', 'replica'), may hold values from -6 to 6
- weight: bfloat16 [256, 8192], P('tensor'), may hold values from -0.375 to 0.375
- error_fb: float32 [32, 256, 8192], P('replica', 'tensor'), may hold values from -420 to 420, as said below
- momentum: float32 [256, 8192], P('tensor'), may hold values from -1.2 to 1.2
- q_prev: float32 [32, 8192], replicated, may hold values from -6 to 6
Outputs:
- input_grad: bfloat16 [4096, 8192], P('replica', 'tensor')
- error_new: float32 [32, 256, 8192], P('replica', 'tensor')
- momentum_new: float32 [256, 8192], P('tensor')
- q_new: float32 [32, 8192], replicated
The draws below stay inside these ranges and needn't reach their ends.
Inputs may be any that keep to these rules, and one draw needn't show every extreme that they name: `error_fb`: finite values.
All inputs are finite; a program needn't handle non-finite values.
Results may differ from the reference program's by a relative error of at most 0.0011.
Values may be sent and summed in bfloat16 or wider, within the bound.
No kernel may reach another device: no remote copies, remote signals or barrier semaphores. Data moves between devices by JAX's collectives and lax.ppermute only.
A program may use at most 64 MiB of HBM per device.

```python
import math
import jax
import jax.numpy as jnp
from jax import lax

D = 8192
RANK = 32
TOK_DEV = 128
FF_WIN = 256
TOKENS = 4096
N_REPLICA = 32


def draw_error_fb(key, part):
    key = jax.random.fold_in(key, 11)
    k_base, k_rows, k_cols = jax.random.split(key, 3)
    ramp = jnp.exp(0.5 * math.log(3.0) * jnp.arange(FF_WIN, dtype=jnp.float32) / FF_WIN)
    row_scale = jnp.exp(jax.random.uniform(k_rows, (FF_WIN,), jnp.float32, 0.0, math.log(10.0))) * ramp
    col_scale = jnp.exp(jax.random.uniform(k_cols, (D,), jnp.float32, math.log(0.5), math.log(2.0)))
    base = jax.random.normal(k_base, (N_REPLICA, FF_WIN, D), jnp.float32)
    base = jnp.clip(base, -6.0, 6.0)
    return (2.0 * base * row_scale[None, :, None] * col_scale[None, None, :]).astype(jnp.float32)


def levels(key, shape, cuts, smallest, high):
    level, own = 1.0, jax.random.fold_in(key, 6)
    for position, parts in cuts:
        draws = jnp.exp(jax.random.uniform(jax.random.fold_in(own, position), (parts,), jnp.float32, smallest / len(cuts), high / len(cuts)))
        level = level * jnp.repeat(draws, shape[position] // parts).reshape([-1 if axis == position else 1 for axis in range(len(shape))])
    return level


def centred(rng, dims, width, most, pieces=(), held_as=jnp.bfloat16):
    result = width * jax.random.normal(rng, dims, jnp.float32)
    if pieces:
        result = result * levels(rng, dims, pieces, -0.22, 0.18)
    return jnp.clip(result, -most, most).astype(held_as)


def setup_inputs(seed: int = 0) -> dict:
    key_of = jax.random.split(jax.random.key(seed), 7)
    return {
        "tokens_x": centred(key_of[0], (TOKENS, D), 1.0, 6.0, ((0, 32), (1, 16))),
        "cotangent": centred(key_of[1], (FF_WIN, TOKENS), 1.0, 6.0, ((0, 16), (1, 32))),
        "weight": centred(key_of[2], (FF_WIN, D), FF_WIN ** -0.5, 0.375, ((0, 16),)),
        "error_fb": draw_error_fb(jax.random.fold_in(key_of[6], 71), 0),
        "momentum": centred(key_of[4], (FF_WIN, D), 0.2, 1.2, ((0, 16),), jnp.float32),
        "q_prev": centred(key_of[5], (RANK, D), 1.0, 6.0, (), jnp.float32),
    }


CLIPPING = 0.2
BETA = 0.9

def reference(tokens_x, cotangent, weight, error_fb, momentum, q_prev):
    highest = lax.Precision.HIGHEST
    input_grad = jnp.dot(cotangent.T.astype(jnp.float32), weight.astype(jnp.float32), preferred_element_type=jnp.float32).astype(jnp.bfloat16)

    def one_replica(index):
        start = index * TOK_DEV
        inputs = lax.dynamic_slice_in_dim(tokens_x, start, TOK_DEV, 0)
        grads = lax.dynamic_slice_in_dim(cotangent, start, TOK_DEV, 1)
        return jnp.dot(grads.astype(jnp.float32), inputs.astype(jnp.float32), preferred_element_type=jnp.float32) + error_fb[index]
    merged = lax.map(one_replica, jnp.arange(N_REPLICA, dtype=jnp.int32))
    p_sum = jnp.einsum('rfd,kd->fk', merged, q_prev, precision=highest)
    gram = jnp.dot(p_sum.T, p_sum, precision=highest)
    lower = jnp.linalg.cholesky(gram)
    basis_t = lax.linalg.triangular_solve(lower, p_sum.T, left_side=True, lower=True)
    q_new = jnp.einsum('kf,rfd->kd', basis_t, merged, precision=highest) / N_REPLICA
    approx = jnp.dot(basis_t.T, q_new, precision=highest)
    error_new = merged - approx[None]
    total = jnp.sum(approx * approx)
    scale = jnp.minimum(1.0, CLIPPING * jnp.sqrt(jnp.float32(FF_WIN * D)) / jnp.sqrt(total))
    momentum_new = BETA * momentum + scale * approx
    return (input_grad, error_new, momentum_new, q_new)
```

```python
import jax
import jax.numpy as jnp
from jax import lax
from jax.sharding import Mesh, PartitionSpec as P

CLIPPING = 0.2
BETA = 0.9
HIGHEST = lax.Precision.HIGHEST
LANES = 128

T = ("z", "core")
R = ("y", "x")


def exchange(parts, axes):
    return lax.all_to_all(parts, axes, 0, 0, tiled=True)


def spread(block, axes):
    return exchange(jnp.broadcast_to(block[None], (lax.axis_size(axes), *block.shape)), axes)


def body(tokens_x, cotangent, weight, error_fb, momentum, q_prev):
    n_t, n_r = lax.axis_size(T), lax.axis_size(R)
    t = lax.axis_index(T)
    core = lax.axis_index("core")
    tokens, wide = tokens_x.shape
    rows, width = weight.shape
    rank = q_prev.shape[0]
    ff_win = rows * n_t
    own = wide // n_r
    error = error_fb[0]

    x_all = lax.all_gather(tokens_x, T, axis=1, tiled=True)
    w_all = lax.all_gather(weight, T, axis=0, tiled=True)

    q_mine = lax.dynamic_slice_in_dim(q_prev, t * wide, wide, 1)
    y_t = lax.dot_general(
        q_mine, tokens_x.astype(jnp.float32), (((1,), (1,)), ((), ())), precision=HIGHEST
    )
    p_error = lax.dot_general(error, q_prev, (((1,), (1,)), ((), ())), precision=HIGHEST)
    fold = rank // rows
    y_fold = y_t.reshape(fold, rows, tokens).transpose(1, 0, 2).reshape(rows, fold * tokens)
    same = jnp.concatenate([cotangent.astype(jnp.float32), y_fold], 1)
    first = jnp.concatenate(
        [
            error.reshape(rows, n_t, wide).transpose(1, 0, 2),
            jnp.broadcast_to(same[None], (n_t, *same.shape)),
        ],
        2,
    )
    first = exchange(first, T)
    error_cols = first[:, :, :wide].reshape(ff_win, wide)
    cot_all = first[:, :, wide : wide + tokens].reshape(ff_win, tokens).astype(jnp.bfloat16)
    y_sum = jnp.sum(first[:, :, wide + tokens :], 0)
    y_sum = y_sum.reshape(rows, fold, tokens).transpose(1, 0, 2).reshape(rank, tokens)
    p_mine = p_error + lax.dot_general(
        cotangent.astype(jnp.float32), y_sum, (((1,), (1,)), ((), ())), precision=HIGHEST
    )

    merged_t = error_cols.T + lax.dot_general(
        tokens_x, cot_all, (((0,), (1,)), ((), ())), preferred_element_type=jnp.float32
    )
    flat = rows * rank // LANES
    second = jnp.concatenate(
        [
            merged_t.reshape(n_r, own * ff_win // LANES, LANES),
            jnp.broadcast_to(p_mine.reshape(1, flat, LANES), (n_r, flat, LANES)),
        ],
        1,
    )
    second = jnp.sum(exchange(second, R), 0)
    total_t = second[: own * ff_win // LANES].reshape(own, ff_win)
    p_sum = spread(second[own * ff_win // LANES :], T).reshape(ff_win, rank)

    gram = lax.dot_general(p_sum, p_sum, (((0,), (0,)), ((), ())), precision=HIGHEST)
    lower = jnp.linalg.cholesky(gram)
    basis_t = lax.linalg.triangular_solve(lower, p_sum.T, left_side=True, lower=True)
    q_own = lax.dot_general(total_t, basis_t, (((1,), (1,)), ((), ())), precision=HIGHEST) / n_r

    q_cols = spread(q_own.reshape(own * rank // LANES, LANES), R).reshape(wide, rank).T
    q_z = spread(q_cols, "z")
    q_other = lax.ppermute(q_z, "core", [(0, 1), (1, 0)])
    q_pair = jnp.where(core == 0, jnp.stack([q_z, q_other], 1), jnp.stack([q_other, q_z], 1))
    q_new = q_pair.reshape(n_t, rank, wide).transpose(1, 0, 2).reshape(rank, width)

    basis_mine = lax.dynamic_slice_in_dim(basis_t, t * rows, rows, 1)
    approx = lax.dot_general(basis_mine, q_new, (((0,), (0,)), ((), ())), precision=HIGHEST)
    merged = error + jnp.dot(cotangent, x_all, preferred_element_type=jnp.float32)
    error_new = (merged - approx)[None]
    basis_gram = lax.dot_general(basis_t, basis_t, (((1,), (1,)), ((), ())), precision=HIGHEST)
    q_gram = lax.dot_general(q_new, q_new, (((1,), (1,)), ((), ())), precision=HIGHEST)
    total = jnp.sum(basis_gram * q_gram)
    scale = jnp.minimum(1.0, CLIPPING * jnp.sqrt(jnp.float32(ff_win * width)) / jnp.sqrt(total))
    momentum_new = BETA * momentum + scale * approx

    w_cols = lax.dynamic_slice_in_dim(w_all, t * wide, wide, 1)
    input_grad = lax.dot_general(
        cot_all, w_cols, (((0,), (0,)), ((), ())), preferred_element_type=jnp.float32
    ).astype(jnp.bfloat16)
    return (input_grad, error_new, momentum_new, q_new)


def solution(mesh):
    n_r, n_t = mesh.devices.shape
    x = 4 if n_r % 4 == 0 and n_r > 4 else 2
    split = Mesh(mesh.devices.reshape(n_r // x, x, n_t // 2, 2), ("y", "x", "z", "core"))
    placed = (P(R, T), P(T, R), P(T, None), P(R, T, None), P(T, None), P())
    return jax.shard_map(
        body,
        mesh=split,
        in_specs=placed,
        out_specs=(P(R, T), P(R, T, None), P(T, None), P()),
        check_vma=False,
    )
```

```python
import jax
import jax.numpy as jnp
from jax import lax
from jax.sharding import Mesh, PartitionSpec as P

CLIPPING = 0.2
BETA = 0.9
HIGHEST = lax.Precision.HIGHEST
LANES = 128

T = ("z", "core")
R = ("y", "x")


def exchange(parts, axes):
    return lax.all_to_all(parts, axes, 0, 0, tiled=True)


def spread(block, axes):
    return exchange(jnp.broadcast_to(block[None], (lax.axis_size(axes), *block.shape)), axes)


def body(tokens_x, cotangent, weight, error_fb, momentum, q_prev):
    n_t, n_r = lax.axis_size(T), lax.axis_size(R)
    t = lax.axis_index(T)
    core = lax.axis_index("core")
    tokens, wide = tokens_x.shape
    rows, width = weight.shape
    rank = q_prev.shape[0]
    ff_win = rows * n_t
    own = wide // n_r
    error = error_fb[0]

    q_mine = lax.dynamic_slice_in_dim(q_prev, t * wide, wide, 1)
    y_t = lax.dot_general(
        q_mine, tokens_x.astype(jnp.float32), (((1,), (1,)), ((), ())), precision=HIGHEST
    )
    p_error = lax.dot_general(error, q_prev, (((1,), (1,)), ((), ())), precision=HIGHEST)
    fold = rank // rows
    y_fold = y_t.reshape(fold, rows, tokens).transpose(1, 0, 2).reshape(rows, fold * tokens)
    same = jnp.concatenate([cotangent.astype(jnp.float32), y_fold], 1)
    first = jnp.concatenate(
        [
            error.reshape(rows, n_t, wide).transpose(1, 0, 2),
            weight.astype(jnp.float32).reshape(rows, n_t, wide).transpose(1, 0, 2),
            jnp.broadcast_to(same[None], (n_t, *same.shape)),
        ],
        2,
    )
    first = exchange(first, T)
    error_cols = first[:, :, :wide].reshape(ff_win, wide)
    w_cols = first[:, :, wide : 2 * wide].reshape(ff_win, wide).astype(jnp.bfloat16)
    cot_all = first[:, :, 2 * wide : 2 * wide + tokens].reshape(ff_win, tokens).astype(jnp.bfloat16)
    y_sum = jnp.sum(first[:, :, 2 * wide + tokens :], 0)
    y_sum = y_sum.reshape(rows, fold, tokens).transpose(1, 0, 2).reshape(rank, tokens)
    p_mine = p_error + lax.dot_general(
        cotangent.astype(jnp.float32), y_sum, (((1,), (1,)), ((), ())), precision=HIGHEST
    )

    merged_t = error_cols.T + lax.dot_general(
        tokens_x, cot_all, (((0,), (1,)), ((), ())), preferred_element_type=jnp.float32
    )
    flat = rows * rank // LANES
    second = jnp.concatenate(
        [
            merged_t.reshape(n_r, own * ff_win // LANES, LANES),
            jnp.broadcast_to(p_mine.reshape(1, flat, LANES), (n_r, flat, LANES)),
        ],
        1,
    )
    second = jnp.sum(exchange(second, R), 0)
    total_t = second[: own * ff_win // LANES].reshape(own, ff_win)

    grad_cols = jnp.dot(cot_all, tokens_x, preferred_element_type=jnp.float32)
    tiles = wide // LANES
    third = jnp.concatenate(
        [
            grad_cols.reshape(n_t, rows, tiles, LANES).transpose(0, 2, 1, 3).reshape(n_t, tiles * rows, LANES),
            jnp.broadcast_to(second[None, own * ff_win // LANES :], (n_t, flat, LANES)),
        ],
        1,
    )
    third = exchange(third, T)
    p_sum = third[:, tiles * rows :].reshape(ff_win, rank)
    grad_rows = third[:, : tiles * rows].reshape(n_t, tiles, rows, LANES)
    grad_rows = grad_rows.transpose(2, 0, 1, 3).reshape(rows, width)

    gram = lax.dot_general(p_sum, p_sum, (((0,), (0,)), ((), ())), precision=HIGHEST)
    lower = jnp.linalg.cholesky(gram)
    basis_t = lax.linalg.triangular_solve(lower, p_sum.T, left_side=True, lower=True)
    q_own = lax.dot_general(total_t, basis_t, (((1,), (1,)), ((), ())), precision=HIGHEST) / n_r

    q_cols = spread(q_own.reshape(own * rank // LANES, LANES), R).reshape(wide, rank).T
    q_z = spread(q_cols, "z")
    q_other = lax.ppermute(q_z, "core", [(0, 1), (1, 0)])
    q_pair = jnp.where(core == 0, jnp.stack([q_z, q_other], 1), jnp.stack([q_other, q_z], 1))
    q_new = q_pair.reshape(n_t, rank, wide).transpose(1, 0, 2).reshape(rank, width)

    basis_mine = lax.dynamic_slice_in_dim(basis_t, t * rows, rows, 1)
    approx = lax.dot_general(basis_mine, q_new, (((0,), (0,)), ((), ())), precision=HIGHEST)
    error_new = (error + grad_rows - approx)[None]
    basis_gram = lax.dot_general(basis_t, basis_t, (((1,), (1,)), ((), ())), precision=HIGHEST)
    q_gram = lax.dot_general(q_new, q_new, (((1,), (1,)), ((), ())), precision=HIGHEST)
    total = jnp.sum(basis_gram * q_gram)
    scale = jnp.minimum(1.0, CLIPPING * jnp.sqrt(jnp.float32(ff_win * width)) / jnp.sqrt(total))
    momentum_new = BETA * momentum + scale * approx

    input_grad = lax.dot_general(
        cot_all, w_cols, (((0,), (0,)), ((), ())), preferred_element_type=jnp.float32
    ).astype(jnp.bfloat16)
    return (input_grad, error_new, momentum_new, q_new)


def solution(mesh):
    n_r, n_t = mesh.devices.shape
    x = 4 if n_r % 4 == 0 and n_r > 4 else 2
    split = Mesh(mesh.devices.reshape(n_r // x, x, n_t // 2, 2), ("y", "x", "z", "core"))
    placed = (P(R, T), P(T, R), P(T, None), P(R, T, None), P(T, None), P())
    return jax.shard_map(
        body,
        mesh=split,
        in_specs=placed,
        out_specs=(P(R, T), P(R, T, None), P(T, None), P()),
        check_vma=False,
    )
```

```python
import functools
import math

import jax
import jax.numpy as jnp
from jax import lax
from jax.experimental import pallas as pl
from jax.experimental.pallas import tpu as pltpu
from jax.sharding import Mesh, PartitionSpec as P

CLIPPING = 0.2
BETA = 0.9
HIGHEST = lax.Precision.HIGHEST
LANES = 128
SUB = 8
F32 = jnp.float32
BF16 = jnp.bfloat16

T = ("z", "core")
R = ("y", "x")
CHIPS = ("z", "y", "x")

VMEM = pl.BlockSpec(memory_space=pltpu.VMEM)
SMEM = pl.BlockSpec(memory_space=pltpu.SMEM)


def exchange(parts, axes):
    return lax.all_to_all(parts, axes, 0, 0, tiled=True)


def call(kernel, outs, in_specs=None, out_specs=None, flops=0, moved=0, **more):
    outs = [jax.ShapeDtypeStruct(*o) for o in outs]
    return functools.partial(
        pl.pallas_call,
        kernel,
        out_shape=outs,
        out_specs=out_specs or [VMEM] * len(outs),
        cost_estimate=pl.CostEstimate(flops=flops, bytes_accessed=moved, transcendentals=0),
        compiler_params=pltpu.CompilerParams(vmem_limit_bytes=48 * 2**20),
        **more,
    )(in_specs=in_specs)


def iota(shape, axis):
    return lax.broadcasted_iota(jnp.int32, shape, axis)


def nt(a, b, precision=HIGHEST):
    return lax.dot_general(a, b, (((1,), (1,)), ((), ())), precision=precision, preferred_element_type=F32)


def tn(a, b, precision=HIGHEST):
    return lax.dot_general(a, b, (((0,), (0,)), ((), ())), precision=precision, preferred_element_type=F32)


def dot(a, b, precision=HIGHEST):
    return jnp.dot(a, b, precision=precision, preferred_element_type=F32)


def fold_rows(tiled, group):
    n = tiled.shape[0]
    kept = jnp.where(iota(tiled.shape, 0) // group == iota(tiled.shape, 1) // 32, tiled, 0.0)
    out = max(group, SUB)
    pick = (iota((out, n), 1) % group == iota((out, n), 0)).astype(F32)
    return dot(pick, kept)


def first_kernel(t_ref, x_ref, c_ref, e_ref, q_ref, send_ref, pe_ref):
    n_t, rows, _ = send_ref.shape
    tokens, wide = x_ref.shape
    start = pl.multiple_of(t_ref[0] * wide, wide)
    y = nt(q_ref[:, pl.ds(start, wide)], x_ref[...].astype(F32))
    c = c_ref[...].astype(F32)
    for k in range(n_t):
        send_ref[k, :, :wide] = e_ref[:, k * wide : (k + 1) * wide]
        send_ref[k, :, wide : wide + tokens] = c
        for g in range(y.shape[0] // rows):
            at = wide + tokens + g * tokens
            send_ref[k, :, at : at + tokens] = y[g * rows : (g + 1) * rows]
    pe_ref[...] = nt(e_ref[...], q_ref[...])


def merge_kernel(got_ref, x_ref, c_ref, pe_ref, send_ref, cot_ref):
    n_t, rows, _ = got_ref.shape
    tokens, wide = x_ref.shape
    n_r = send_ref.shape[0]
    group = LANES // n_r
    ff_win = n_t * rows
    cot = got_ref[:, :, wide : wide + tokens].reshape(ff_win, tokens).astype(BF16)
    cot_ref[...] = cot
    y = jnp.sum(got_ref[:, :, wide + tokens :], 0)
    folds = y.shape[1] // tokens
    y = jnp.concatenate([y[:, g * tokens : (g + 1) * tokens] for g in range(folds)], 0)
    rank = y.shape[0]
    y4 = jnp.concatenate([y] * (LANES // rank), 0)
    tile = (iota((rank, LANES), 1) % rank == iota((rank, LANES), 0)).astype(F32)
    p4 = nt(c_ref[...].astype(F32), y4) + dot(pe_ref[...], tile)
    p_pack = fold_rows(p4, rows // 4)

    merged = got_ref[:, :, :wide].reshape(ff_win, wide) + dot(cot, x_ref[...], None)
    out, col = iota((wide, wide), 0), iota((wide, wide), 1)
    own = wide // n_r
    r, b, a = out // own, out % own // group, out % group
    turn = (col == b * LANES + r * group + a).astype(BF16)
    turned = jnp.zeros((wide, ff_win), F32)
    rest = merged
    for _ in range(3):
        piece = rest.astype(BF16)
        turned += nt(turn, piece, None)
        rest -= piece.astype(F32)
    halves = ff_win // LANES if ff_win >= LANES else 1
    width = ff_win // halves
    for k in range(n_r):
        for h in range(halves):
            send_ref[k, h * own : (h + 1) * own, :width] = turned[
                k * own : (k + 1) * own, h * width : (h + 1) * width
            ]
        send_ref[k, halves * own :, :] = p_pack[: send_ref.shape[1] - halves * own]


def rows_kernel(cot_ref, x_ref, send_ref):
    n_t = send_ref.shape[0]
    rows = cot_ref.shape[0] // n_t
    grad = dot(cot_ref[...], x_ref[...], None)
    for k in range(n_t):
        for b in range(grad.shape[1] // LANES):
            send_ref[k, b * rows : (b + 1) * rows, :] = grad[
                k * rows : (k + 1) * rows, b * LANES : (b + 1) * LANES
            ]


def sum_kernel(got_ref, held_ref, total_ref, pack_ref, send_ref, scratch, sem):
    n_r = got_ref.shape[0]
    n_t, tall, _ = send_ref.shape
    own, long = total_ref.shape
    ff_win = long // 2
    rows = ff_win // n_t
    got = jnp.sum(got_ref[...], 0)
    pack = got[got.shape[0] - 4 :]
    pack = jnp.concatenate([pack, jnp.zeros_like(pack)], 0)
    pack_ref[...] = pack
    for k in range(n_t):
        scratch[k] = pack
    copy = pltpu.make_async_copy(scratch, send_ref.at[:, pl.ds(tall - SUB, SUB), :], sem)
    copy.start()
    halves = ff_win // LANES if ff_win >= LANES else 1
    width = ff_win // halves
    total = jnp.zeros(total_ref.shape, F32)
    for h in range(halves):
        unit, lane = iota((width, long), 0) + h * width, iota((width, long), 1)
        t, b, a = unit // rows, unit % rows // 4, unit % 4
        move = (lane == b * (SUB * n_t) + t * SUB + a).astype(F32)
        total += dot(got[h * own : (h + 1) * own, :width], move)
    total_ref[...] = total
    copy.wait()


def factor_kernel(n_r, pack_ref, total_ref, send_ref, gram_ref, inverse_ref):
    n_t = pack_ref.shape[0]
    own = total_ref.shape[0]
    rank = gram_ref.shape[0]
    group = own // 4
    pack = pack_ref[...].reshape(n_t * SUB, LANES)
    gram4 = tn(pack, pack)
    gram = sum(gram4[b * rank : (b + 1) * rank, b * rank : (b + 1) * rank] for b in range(4))
    gram_ref[...] = gram
    row, lane = iota((rank, LANES), 0), iota((rank, LANES), 1)
    work = jnp.concatenate([gram, jnp.zeros((rank, LANES - rank), F32)], 1)
    work = jnp.where(lane == row + rank, 1.0, work)
    for j in range(rank):
        pivot = work[j : j + 1, :]
        factor = work[:, j : j + 1] / work[j : j + 1, j : j + 1]
        work = jnp.where(row > j, work - factor * pivot, work)
    diagonal = jnp.sum(jnp.where(lane == row, work, 0.0), 1, keepdims=True)
    inverse = (work * lax.rsqrt(diagonal))[:, rank : 2 * rank]
    inverse_ref[...] = inverse
    inverse16 = jnp.concatenate([inverse] * 4, 0)
    inverse16 = jnp.concatenate([inverse16] * 4, 1)
    total = total_ref[...]
    span = SUB * n_t
    product = jnp.zeros((own, LANES), F32)
    for b in range(4):
        part = dot(total[:, b * span : (b + 1) * span], pack)
        product = jnp.where(iota(part.shape, 1) // rank == b, part, product)
    q4 = nt(product, inverse16) / n_r
    q_pack = fold_rows(q4, group)[:group]
    send_ref[...] = jnp.broadcast_to(q_pack[None], send_ref.shape)


def last_kernel(limit, core_ref, mine_ref, other_ref, basis_ref, weigh_ref, e_ref, g_ref, m_ref, q_ref, error_ref, momentum_ref, approx):
    n_z = mine_ref.shape[0]
    rows = e_ref.shape[0]
    rank = q_ref.shape[0]
    core = core_ref[0]
    wide = 4 * LANES
    square = (LANES, LANES)
    basis4 = basis_ref[...]
    stack = jnp.concatenate(
        [(iota(square, 0) == iota(square, 1)).astype(F32)]
        + [jnp.where(iota(basis4.shape, 1) // rank == b, basis4, 0.0) for b in range(4)],
        0,
    )
    gram = jnp.zeros(square, F32)
    for z in range(n_z):
        for ref, c in ((mine_ref, core), (other_ref, 1 - core)):
            block = ref[z]
            gram += tn(block, block)
            both = nt(stack, block)
            t = 2 * z + c
            for b in range(4):
                at = pl.ds(pl.multiple_of(t * wide + b * LANES, LANES), LANES)
                near = both[LANES + b * rows : LANES + (b + 1) * rows]
                q_ref[:, at] = both[b * rank : (b + 1) * rank]
                approx[:, at] = near
                error_ref[:, at] = e_ref[:, at] + g_ref[t, b * rows : (b + 1) * rows, :] - near
    total = jnp.sum(gram * weigh_ref[...], keepdims=True)
    scale = jnp.minimum(1.0, limit / jnp.sqrt(total))
    momentum_ref[...] = BETA * m_ref[...] + scale * approx[...]


def body(tokens_x, cotangent, weight, error_fb, momentum, q_prev):
    n_t, n_r, n_z = lax.axis_size(T), lax.axis_size(R), lax.axis_size("z")
    t = lax.axis_index(T)[None]
    core = lax.axis_index("core")[None]
    tokens, wide = tokens_x.shape
    rows, width = weight.shape
    rank = q_prev.shape[0]
    ff_win = rows * n_t
    own = wide // n_r
    group = own // 4
    error = error_fb[0]
    halves = ff_win // LANES if ff_win >= LANES else 1

    first, p_error = call(
        first_kernel,
        [((n_t, rows, wide + tokens + rank // rows * tokens), F32), ((rows, rank), F32)],
        [SMEM, VMEM, VMEM, VMEM, VMEM],
        moved=3 * 2**20,
    )(t, tokens_x, cotangent, error, q_prev)
    first = exchange(first, T)

    tall = wide // LANES * rows + SUB
    second, cot_all = call(
        merge_kernel,
        [((n_r, halves * own + 4, LANES), F32), ((ff_win, tokens), BF16)],
        [VMEM] * 4,
        moved=2 * 2**20,
    )(first, tokens_x, cotangent, p_error)
    (third,) = call(
        rows_kernel, [((n_t, tall, LANES), F32)], [VMEM] * 2, flops=2**25, moved=2**20
    )(cot_all, tokens_x)
    second = exchange(second, R)

    total_t, p_pack, third = call(
        sum_kernel,
        [((own, 2 * ff_win), F32), ((SUB, LANES), F32), (third.shape, F32)],
        [VMEM, pl.BlockSpec(memory_space=pl.ANY)],
        [VMEM, VMEM, pl.BlockSpec(memory_space=pl.ANY)],
        moved=2**20,
        scratch_shapes=[pltpu.VMEM((n_t, SUB, LANES), F32), pltpu.SemaphoreType.DMA(())],
        input_output_aliases={1: 2},
    )(second, third)
    third = exchange(third, T)

    q_send, gram, inverse = call(
        functools.partial(factor_kernel, n_r),
        [((n_r * n_z, group, LANES), F32), ((rank, rank), F32), ((rank, rank), F32)],
        [
            pl.BlockSpec((n_t, SUB, LANES), lambda i: (0, tall // SUB - 1, 0)),
            pl.BlockSpec((own, 2 * ff_win), lambda i: (0, 0)),
        ],
        [
            pl.BlockSpec((n_r * n_z, group, LANES), lambda i: (0, 0, 0)),
            pl.BlockSpec((rank, rank), lambda i: (0, 0)),
            pl.BlockSpec((rank, rank), lambda i: (0, 0)),
        ],
        moved=2**20,
        grid=(1,),
    )(third, total_t)
    mine = exchange(q_send, CHIPS)
    basis_gram = dot(dot(inverse, gram), inverse.T)
    p_rows = p_pack[:4].reshape(4, 4, rank).transpose(1, 0, 2).reshape(rows, rank)
    basis4 = jnp.tile(dot(p_rows, inverse.T), (1, 4))
    square = (LANES, LANES)
    weigh = jnp.where(
        iota(square, 0) // rank == iota(square, 1) // rank, jnp.tile(basis_gram, (4, 4)), 0.0
    )
    weight, mine = lax.optimization_barrier((weight, mine))
    w_cols = exchange(weight.reshape(rows, n_t, wide).transpose(1, 0, 2), T).reshape(ff_win, wide)
    other = lax.ppermute(mine, "core", [(0, 1), (1, 0)])
    blocks = (n_z, LANES, LANES)
    limit = CLIPPING * math.sqrt(ff_win * width)
    q_new, error_new, momentum_new = call(
        functools.partial(last_kernel, limit),
        [((rank, width), F32), ((rows, width), F32), ((rows, width), F32)],
        [SMEM] + [VMEM] * 7,
        flops=2**30,
        moved=5 * 2**20,
        scratch_shapes=[pltpu.VMEM((rows, width), F32)],
    )(core, mine.reshape(blocks), other.reshape(blocks), basis4, weigh, error, third, momentum)

    input_grad = tn(cot_all, w_cols, None).astype(BF16)
    return (input_grad, error_new[None], momentum_new, q_new)


def solution(mesh):
    n_r, n_t = mesh.devices.shape
    x = 4 if n_r > 4 else 2
    split = Mesh(mesh.devices.reshape(n_r // x, x, n_t // 2, 2), (*R, *T))
    placed = (P(R, T), P(T, R), P(T, None), P(R, T, None), P(T, None), P())
    return jax.shard_map(
        body,
        mesh=split,
        in_specs=placed,
        out_specs=(P(R, T), P(R, T, None), P(T, None), P()),
        check_vma=False,
    )
```

```python
import functools
import math

import jax
import jax.numpy as jnp
from jax import lax
from jax.experimental import pallas as pl
from jax.experimental.pallas import tpu as pltpu
from jax.sharding import Mesh, PartitionSpec as P

CLIPPING = 0.2
BETA = 0.9
HIGHEST = lax.Precision.HIGHEST
LANES = 128
SUB = 8
F32 = jnp.float32
BF16 = jnp.bfloat16

T = ("z", "core")
R = ("y", "x")
CHIPS = ("z", "y", "x")

VMEM = pl.BlockSpec(memory_space=pltpu.VMEM)
SMEM = pl.BlockSpec(memory_space=pltpu.SMEM)
HBM = pl.BlockSpec(memory_space=pltpu.HBM)


def exchange(parts, axes):
    return lax.all_to_all(parts, axes, 0, 0, tiled=True)


def call(kernel, outs, in_specs=None, out_specs=None, flops=0, moved=0, limit=48, **more):
    outs = [jax.ShapeDtypeStruct(*o) for o in outs]
    return functools.partial(
        pl.pallas_call,
        kernel,
        out_shape=outs,
        out_specs=out_specs or [VMEM] * len(outs),
        cost_estimate=pl.CostEstimate(flops=flops, bytes_accessed=moved, transcendentals=0),
        compiler_params=pltpu.CompilerParams(vmem_limit_bytes=limit and limit * 2**20),
        **more,
    )(in_specs=in_specs)


def iota(shape, axis):
    return lax.broadcasted_iota(jnp.int32, shape, axis)


def nt(a, b, precision=HIGHEST):
    return lax.dot_general(a, b, (((1,), (1,)), ((), ())), precision=precision, preferred_element_type=F32)


def tn(a, b, precision=HIGHEST):
    return lax.dot_general(a, b, (((0,), (0,)), ((), ())), precision=precision, preferred_element_type=F32)


def dot(a, b, precision=HIGHEST):
    return jnp.dot(a, b, precision=precision, preferred_element_type=F32)


def fold_rows(tiled, group):
    n = tiled.shape[0]
    kept = jnp.where(iota(tiled.shape, 0) // group == iota(tiled.shape, 1) // 32, tiled, 0.0)
    out = max(group, SUB)
    pick = (iota((out, n), 1) % group == iota((out, n), 0)).astype(F32)
    return dot(pick, kept)


def first_kernel(t_ref, x_ref, c_ref, e_ref, q_ref, send_ref, x, c, q, sems):
    n_t, rows, _ = send_ref.shape
    tokens, wide = x_ref.shape
    start = pl.multiple_of(t_ref[0] * wide, wide)
    copies = [
        pltpu.make_async_copy(q_ref.at[:, pl.ds(start, wide)], q, sems.at[0]),
        pltpu.make_async_copy(x_ref, x, sems.at[1]),
        pltpu.make_async_copy(c_ref, c, sems.at[2]),
    ]
    for k in range(n_t):
        copies.append(
            pltpu.make_async_copy(
                e_ref.at[:, pl.ds(k * wide, wide)], send_ref.at[k, :, pl.ds(0, wide)], sems.at[3 + k]
            )
        )
    for copy in copies:
        copy.start()
    for copy in copies[:3]:
        copy.wait()
    y = nt(q[...], x[...].astype(F32))
    cot = c[...].astype(F32)
    for k in range(n_t):
        send_ref[k, :, wide : wide + tokens] = cot
        for g in range(y.shape[0] // rows):
            at = wide + tokens + g * tokens
            send_ref[k, :, at : at + tokens] = y[g * rows : (g + 1) * rows]
    for copy in copies[3:]:
        copy.wait()


def project_kernel(e_ref, q_ref, pe_ref):
    pe_ref[...] = nt(e_ref[...], q_ref[...])


def merge_kernel(got_ref, x_ref, c_ref, pe_ref, send_ref, cot_ref):
    n_t, rows, _ = got_ref.shape
    tokens, wide = x_ref.shape
    n_r = send_ref.shape[0]
    group = LANES // n_r
    ff_win = n_t * rows
    cot = got_ref[:, :, wide : wide + tokens].reshape(ff_win, tokens).astype(BF16)
    cot_ref[...] = cot
    y = jnp.sum(got_ref[:, :, wide + tokens :], 0)
    folds = y.shape[1] // tokens
    y = jnp.concatenate([y[:, g * tokens : (g + 1) * tokens] for g in range(folds)], 0)
    rank = y.shape[0]
    y4 = jnp.concatenate([y] * (LANES // rank), 0)
    tile = (iota((rank, LANES), 1) % rank == iota((rank, LANES), 0)).astype(F32)
    p4 = nt(c_ref[...].astype(F32), y4) + dot(pe_ref[...], tile)
    p_pack = fold_rows(p4, rows // 4)

    merged = got_ref[:, :, :wide].reshape(ff_win, wide) + dot(cot, x_ref[...], None)
    out, col = iota((wide, wide), 0), iota((wide, wide), 1)
    own = wide // n_r
    r, b, a = out // own, out % own // group, out % group
    turn = (col == b * LANES + r * group + a).astype(BF16)
    turned = jnp.zeros((wide, ff_win), F32)
    rest = merged
    for _ in range(3):
        piece = rest.astype(BF16)
        turned += nt(turn, piece, None)
        rest -= piece.astype(F32)
    halves = ff_win // LANES if ff_win >= LANES else 1
    width = ff_win // halves
    for k in range(n_r):
        for h in range(halves):
            send_ref[k, h * own : (h + 1) * own, :width] = turned[
                k * own : (k + 1) * own, h * width : (h + 1) * width
            ]
        send_ref[k, halves * own :, :] = p_pack[: send_ref.shape[1] - halves * own]


def rows_kernel(cot_ref, x_ref, send_ref):
    n_t = send_ref.shape[0]
    rows = cot_ref.shape[0] // n_t
    grad = dot(cot_ref[...], x_ref[...], None)
    for k in range(n_t):
        for b in range(grad.shape[1] // LANES):
            send_ref[k, b * rows : (b + 1) * rows, :] = grad[
                k * rows : (k + 1) * rows, b * LANES : (b + 1) * LANES
            ]


def sum_kernel(got_ref, held_ref, total_ref, pack_ref, send_ref, scratch, sem):
    n_r = got_ref.shape[0]
    n_t, tall, _ = send_ref.shape
    own, long = total_ref.shape
    ff_win = long // 2
    rows = ff_win // n_t
    got = jnp.sum(got_ref[...], 0)
    pack = got[got.shape[0] - 4 :]
    pack = jnp.concatenate([pack, jnp.zeros_like(pack)], 0)
    pack_ref[...] = pack
    for k in range(n_t):
        scratch[k] = pack
    copy = pltpu.make_async_copy(scratch, send_ref.at[:, pl.ds(tall - SUB, SUB), :], sem)
    copy.start()
    halves = ff_win // LANES if ff_win >= LANES else 1
    width = ff_win // halves
    total = jnp.zeros(total_ref.shape, F32)
    for h in range(halves):
        unit, lane = iota((width, long), 0) + h * width, iota((width, long), 1)
        t, b, a = unit // rows, unit % rows // 4, unit % 4
        move = (lane == b * (SUB * n_t) + t * SUB + a).astype(F32)
        total += dot(got[h * own : (h + 1) * own, :width], move)
    total_ref[...] = total
    copy.wait()


def factor_kernel(n_r, pack_ref, total_ref, send_ref, gram_ref, inverse_ref):
    n_t = pack_ref.shape[0]
    own = total_ref.shape[0]
    rank = gram_ref.shape[0]
    group = own // 4
    pack = pack_ref[...].reshape(n_t * SUB, LANES)
    gram4 = tn(pack, pack)
    gram = sum(gram4[b * rank : (b + 1) * rank, b * rank : (b + 1) * rank] for b in range(4))
    gram_ref[...] = gram
    row, lane = iota((rank, LANES), 0), iota((rank, LANES), 1)
    work = jnp.concatenate([gram, jnp.zeros((rank, LANES - rank), F32)], 1)
    work = jnp.where(lane == row + rank, 1.0, work)
    for j in range(rank):
        pivot = work[j : j + 1, :]
        factor = work[:, j : j + 1] / work[j : j + 1, j : j + 1]
        work = jnp.where(row > j, work - factor * pivot, work)
    diagonal = jnp.sum(jnp.where(lane == row, work, 0.0), 1, keepdims=True)
    inverse = (work * lax.rsqrt(diagonal))[:, rank : 2 * rank]
    inverse_ref[...] = inverse
    inverse16 = jnp.concatenate([inverse] * 4, 0)
    inverse16 = jnp.concatenate([inverse16] * 4, 1)
    total = total_ref[...]
    span = SUB * n_t
    product = jnp.zeros((own, LANES), F32)
    for b in range(4):
        part = dot(total[:, b * span : (b + 1) * span], pack)
        product = jnp.where(iota(part.shape, 1) // rank == b, part, product)
    q4 = nt(product, inverse16) / n_r
    q_pack = fold_rows(q4, group)[:group]
    send_ref[...] = jnp.broadcast_to(q_pack[None], send_ref.shape)


def last_kernel(limit, core_ref, mine_ref, other_ref, basis_ref, weigh_ref, e_ref, g_ref, m_ref, q_ref, error_ref, momentum_ref, approx):
    n_z = mine_ref.shape[0]
    rows = e_ref.shape[0]
    rank = q_ref.shape[0]
    core = core_ref[0]
    wide = 4 * LANES
    square = (LANES, LANES)
    basis4 = basis_ref[...]
    stack = jnp.concatenate(
        [(iota(square, 0) == iota(square, 1)).astype(F32)]
        + [jnp.where(iota(basis4.shape, 1) // rank == b, basis4, 0.0) for b in range(4)],
        0,
    )
    gram = jnp.zeros(square, F32)
    for z in range(n_z):
        for ref, c in ((mine_ref, core), (other_ref, 1 - core)):
            block = ref[z]
            gram += tn(block, block)
            both = nt(stack, block)
            t = 2 * z + c
            for b in range(4):
                at = pl.ds(pl.multiple_of(t * wide + b * LANES, LANES), LANES)
                near = both[LANES + b * rows : LANES + (b + 1) * rows]
                q_ref[:, at] = both[b * rank : (b + 1) * rank]
                approx[:, at] = near
                error_ref[:, at] = e_ref[:, at] + g_ref[t, b * rows : (b + 1) * rows, :] - near
    total = jnp.sum(gram * weigh_ref[...], keepdims=True)
    scale = jnp.minimum(1.0, limit / jnp.sqrt(total))
    momentum_ref[...] = BETA * m_ref[...] + scale * approx[...]


def body(tokens_x, cotangent, weight, error_fb, momentum, q_prev):
    n_t, n_r, n_z = lax.axis_size(T), lax.axis_size(R), lax.axis_size("z")
    t = lax.axis_index(T)[None]
    core = lax.axis_index("core")[None]
    tokens, wide = tokens_x.shape
    rows, width = weight.shape
    rank = q_prev.shape[0]
    ff_win = rows * n_t
    own = wide // n_r
    group = own // 4
    error = error_fb[0]
    halves = ff_win // LANES if ff_win >= LANES else 1

    (first,) = call(
        first_kernel,
        [((n_t, rows, wide + tokens + rank // rows * tokens), F32)],
        [SMEM] + [HBM] * 4,
        moved=3 * 2**20,
        limit=None,
        scratch_shapes=[
            pltpu.VMEM(tokens_x.shape, BF16),
            pltpu.VMEM(cotangent.shape, BF16),
            pltpu.VMEM((rank, wide), F32),
            pltpu.SemaphoreType.DMA((3 + n_t,)),
        ],
    )(t, tokens_x, cotangent, error, q_prev)
    w_parts = weight.reshape(rows, n_t, wide).transpose(1, 0, 2)
    first, error_late = lax.optimization_barrier((first, error))
    (p_error,) = call(
        project_kernel, [((rows, rank), F32)], [VMEM] * 2, flops=2**27, moved=2 * 2**20
    )(error_late, q_prev)
    first = exchange(first, T)

    tall = wide // LANES * rows + SUB
    second, cot_all = call(
        merge_kernel,
        [((n_r, halves * own + 4, LANES), F32), ((ff_win, tokens), BF16)],
        [VMEM] * 4,
        moved=2 * 2**20,
    )(first, tokens_x, cotangent, p_error)
    (third,) = call(
        rows_kernel, [((n_t, tall, LANES), F32)], [VMEM] * 2, flops=2**25, moved=2**20
    )(cot_all, tokens_x)
    second = exchange(second, R)

    total_t, p_pack, third = call(
        sum_kernel,
        [((own, 2 * ff_win), F32), ((SUB, LANES), F32), (third.shape, F32)],
        [VMEM, pl.BlockSpec(memory_space=pl.ANY)],
        [VMEM, VMEM, pl.BlockSpec(memory_space=pl.ANY)],
        moved=2**20,
        scratch_shapes=[pltpu.VMEM((n_t, SUB, LANES), F32), pltpu.SemaphoreType.DMA(())],
        input_output_aliases={1: 2},
    )(second, third)
    third = exchange(third, T)

    q_send, gram, inverse = call(
        functools.partial(factor_kernel, n_r),
        [((n_r * n_z, group, LANES), F32), ((rank, rank), F32), ((rank, rank), F32)],
        [
            pl.BlockSpec((n_t, SUB, LANES), lambda i: (0, tall // SUB - 1, 0)),
            pl.BlockSpec((own, 2 * ff_win), lambda i: (0, 0)),
        ],
        [
            pl.BlockSpec((n_r * n_z, group, LANES), lambda i: (0, 0, 0)),
            pl.BlockSpec((rank, rank), lambda i: (0, 0)),
            pl.BlockSpec((rank, rank), lambda i: (0, 0)),
        ],
        moved=2**20,
        grid=(1,),
    )(third, total_t)
    mine = exchange(q_send, CHIPS)
    basis_gram = dot(dot(inverse, gram), inverse.T)
    p_rows = p_pack[:4].reshape(4, 4, rank).transpose(1, 0, 2).reshape(rows, rank)
    basis4 = jnp.tile(dot(p_rows, inverse.T), (1, 4))
    square = (LANES, LANES)
    weigh = jnp.where(
        iota(square, 0) // rank == iota(square, 1) // rank, jnp.tile(basis_gram, (4, 4)), 0.0
    )
    w_parts, mine = lax.optimization_barrier((w_parts, mine))
    w_cols = exchange(w_parts, T).reshape(ff_win, wide)
    other = lax.ppermute(mine, "core", [(0, 1), (1, 0)])
    blocks = (n_z, LANES, LANES)
    limit = CLIPPING * math.sqrt(ff_win * width)
    q_new, error_new, momentum_new = call(
        functools.partial(last_kernel, limit),
        [((rank, width), F32), ((rows, width), F32), ((rows, width), F32)],
        [SMEM] + [VMEM] * 7,
        flops=2**30,
        moved=5 * 2**20,
        scratch_shapes=[pltpu.VMEM((rows, width), F32)],
    )(core, mine.reshape(blocks), other.reshape(blocks), basis4, weigh, error, third, momentum)

    cot_all, q_new = lax.optimization_barrier((cot_all, q_new))
    input_grad = tn(cot_all, w_cols, None).astype(BF16)
    return (input_grad, error_new[None], momentum_new, q_new)


def solution(mesh):
    n_r, n_t = mesh.devices.shape
    x = 4 if n_r > 4 else 2
    split = Mesh(mesh.devices.reshape(n_r // x, x, n_t // 2, 2), (*R, *T))
    placed = (P(R, T), P(T, R), P(T, None), P(R, T, None), P(T, None), P())
    return jax.shard_map(
        body,
        mesh=split,
        in_specs=placed,
        out_specs=(P(R, T), P(R, T, None), P(T, None), P()),
        check_vma=False,
    )
```

```python
import functools
import math

import jax
import jax.numpy as jnp
from jax import lax
from jax.experimental import pallas as pl
from jax.experimental.pallas import tpu as pltpu
from jax.sharding import Mesh, PartitionSpec as P

CLIPPING = 0.2
BETA = 0.9
HIGHEST = lax.Precision.HIGHEST
LANES = 128
SUB = 8
F32 = jnp.float32
BF16 = jnp.bfloat16

T = ("z", "core")
R = ("y", "x")
CHIPS = ("z", "y", "x")

VMEM = pl.BlockSpec(memory_space=pltpu.VMEM)
SMEM = pl.BlockSpec(memory_space=pltpu.SMEM)
HBM = pl.BlockSpec(memory_space=pltpu.HBM)


def exchange(parts, axes):
    return lax.all_to_all(parts, axes, 0, 0, tiled=True)


def call(kernel, outs, in_specs=None, out_specs=None, flops=0, moved=0, limit=48, **more):
    outs = [jax.ShapeDtypeStruct(*o) for o in outs]
    return functools.partial(
        pl.pallas_call,
        kernel,
        out_shape=outs,
        out_specs=out_specs or [VMEM] * len(outs),
        cost_estimate=pl.CostEstimate(flops=flops, bytes_accessed=moved, transcendentals=0),
        compiler_params=pltpu.CompilerParams(vmem_limit_bytes=limit and limit * 2**20),
        **more,
    )(in_specs=in_specs)


def iota(shape, axis):
    return lax.broadcasted_iota(jnp.int32, shape, axis)


def nt(a, b, precision=HIGHEST):
    return lax.dot_general(a, b, (((1,), (1,)), ((), ())), precision=precision, preferred_element_type=F32)


def tn(a, b, precision=HIGHEST):
    return lax.dot_general(a, b, (((0,), (0,)), ((), ())), precision=precision, preferred_element_type=F32)


def dot(a, b, precision=HIGHEST):
    return jnp.dot(a, b, precision=precision, preferred_element_type=F32)


def fold_rows(tiled, group):
    n = tiled.shape[0]
    kept = jnp.where(iota(tiled.shape, 0) // group == iota(tiled.shape, 1) // 32, tiled, 0.0)
    out = max(group, SUB)
    pick = (iota((out, n), 1) % group == iota((out, n), 0)).astype(F32)
    return dot(pick, kept)


def cut_kernel(e_ref, send_ref, sems):
    n_t, _, wide = send_ref.shape
    copies = [
        pltpu.make_async_copy(e_ref.at[:, pl.ds(k * wide, wide)], send_ref.at[k], sems.at[k])
        for k in range(n_t)
    ]
    for copy in copies:
        copy.start()
    for copy in copies:
        copy.wait()


def share_kernel(t_ref, x_ref, c_ref, q_ref, send_ref, x, c, q, sems):
    rows, tokens = c_ref.shape
    wide = x_ref.shape[1]
    start = pl.multiple_of(t_ref[0] * wide, wide)
    copies = [
        pltpu.make_async_copy(q_ref.at[:, pl.ds(start, wide)], q, sems.at[0]),
        pltpu.make_async_copy(x_ref, x, sems.at[1]),
        pltpu.make_async_copy(c_ref, c, sems.at[2]),
    ]
    for copy in copies:
        copy.start()
    for copy in copies:
        copy.wait()
    send_ref[:rows] = c[...].astype(F32)
    send_ref[rows:] = nt(q[...], x[...].astype(F32))


def project_kernel(e_ref, q_ref, pe_ref):
    pe_ref[...] = nt(e_ref[...], q_ref[...])


def merge_kernel(got_ref, all_ref, x_ref, c_ref, pe_ref, send_ref, cot_ref):
    n_t, rows, _ = got_ref.shape
    tokens, wide = x_ref.shape
    n_r = send_ref.shape[0]
    group = LANES // n_r
    ff_win = n_t * rows
    cot = all_ref[:, :rows, :].reshape(ff_win, tokens).astype(BF16)
    cot_ref[...] = cot
    y = jnp.sum(all_ref[:, rows:, :], 0)
    rank = y.shape[0]
    y4 = jnp.concatenate([y] * (LANES // rank), 0)
    tile = (iota((rank, LANES), 1) % rank == iota((rank, LANES), 0)).astype(F32)
    p4 = nt(c_ref[...].astype(F32), y4) + dot(pe_ref[...], tile)
    p_pack = fold_rows(p4, rows // 4)

    merged = got_ref[...].reshape(ff_win, wide) + dot(cot, x_ref[...], None)
    out, col = iota((wide, wide), 0), iota((wide, wide), 1)
    own = wide // n_r
    r, b, a = out // own, out % own // group, out % group
    turn = (col == b * LANES + r * group + a).astype(BF16)
    turned = jnp.zeros((wide, ff_win), F32)
    rest = merged
    for _ in range(3):
        piece = rest.astype(BF16)
        turned += nt(turn, piece, None)
        rest -= piece.astype(F32)
    halves = ff_win // LANES if ff_win >= LANES else 1
    width = ff_win // halves
    for k in range(n_r):
        for h in range(halves):
            send_ref[k, h * own : (h + 1) * own, :width] = turned[
                k * own : (k + 1) * own, h * width : (h + 1) * width
            ]
        send_ref[k, halves * own :, :] = p_pack[: send_ref.shape[1] - halves * own]


def rows_kernel(cot_ref, x_ref, w_ref, send_ref):
    n_t, rows, _ = send_ref.shape
    wide = x_ref.shape[1]
    grad = dot(cot_ref[...], x_ref[...], None)
    for k in range(n_t):
        send_ref[k, :, :wide] = grad[k * rows : (k + 1) * rows]
        send_ref[k, :, wide:] = w_ref[:, k * wide : (k + 1) * wide].astype(F32)


def sum_kernel(n_t, got_ref, total_ref, pack_ref):
    own, long = total_ref.shape
    ff_win = long // 2
    rows = ff_win // n_t
    got = jnp.sum(got_ref[...], 0)
    pack = got[got.shape[0] - 4 :]
    pack_ref[...] = jnp.concatenate([pack, jnp.zeros_like(pack)], 0)
    halves = ff_win // LANES if ff_win >= LANES else 1
    width = ff_win // halves
    total = jnp.zeros(total_ref.shape, F32)
    for h in range(halves):
        unit, lane = iota((width, long), 0) + h * width, iota((width, long), 1)
        t, b, a = unit // rows, unit % rows // 4, unit % 4
        move = (lane == b * (SUB * n_t) + t * SUB + a).astype(F32)
        total += dot(got[h * own : (h + 1) * own, :width], move)
    total_ref[...] = total


def factor_kernel(n_r, pack_ref, total_ref, send_ref, gram_ref, inverse_ref):
    span = pack_ref.shape[0]
    own = total_ref.shape[0]
    rank = gram_ref.shape[0]
    group = own // 4
    pack = pack_ref[...]
    gram4 = tn(pack, pack)
    gram = sum(gram4[b * rank : (b + 1) * rank, b * rank : (b + 1) * rank] for b in range(4))
    gram_ref[...] = gram
    row, lane = iota((rank, LANES), 0), iota((rank, LANES), 1)
    work = jnp.concatenate([gram, jnp.zeros((rank, LANES - rank), F32)], 1)
    work = jnp.where(lane == row + rank, 1.0, work)
    for j in range(rank):
        pivot = work[j : j + 1, :]
        factor = work[:, j : j + 1] / work[j : j + 1, j : j + 1]
        work = jnp.where(row > j, work - factor * pivot, work)
    diagonal = jnp.sum(jnp.where(lane == row, work, 0.0), 1, keepdims=True)
    inverse = (work * lax.rsqrt(diagonal))[:, rank : 2 * rank]
    inverse_ref[...] = inverse
    inverse16 = jnp.concatenate([inverse] * 4, 0)
    inverse16 = jnp.concatenate([inverse16] * 4, 1)
    total = total_ref[...]
    product = jnp.zeros((own, LANES), F32)
    for b in range(4):
        part = dot(total[:, b * span : (b + 1) * span], pack)
        product = jnp.where(iota(part.shape, 1) // rank == b, part, product)
    q4 = nt(product, inverse16) / n_r
    q_pack = fold_rows(q4, group)[:group]
    send_ref[...] = jnp.broadcast_to(q_pack[None], send_ref.shape)


def last_kernel(limit, core_ref, mine_ref, other_ref, basis_ref, weigh_ref, e_ref, g_ref, m_ref, q_ref, error_ref, momentum_ref, approx):
    n_z = mine_ref.shape[0]
    rows = e_ref.shape[0]
    rank = q_ref.shape[0]
    core = core_ref[0]
    wide = 4 * LANES
    square = (LANES, LANES)
    basis4 = basis_ref[...]
    stack = jnp.concatenate(
        [(iota(square, 0) == iota(square, 1)).astype(F32)]
        + [jnp.where(iota(basis4.shape, 1) // rank == b, basis4, 0.0) for b in range(4)],
        0,
    )
    gram = jnp.zeros(square, F32)
    for z in range(n_z):
        for ref, c in ((mine_ref, core), (other_ref, 1 - core)):
            block = ref[z]
            gram += tn(block, block)
            both = nt(stack, block)
            t = 2 * z + c
            for b in range(4):
                at = pl.ds(pl.multiple_of(t * wide + b * LANES, LANES), LANES)
                near = both[LANES + b * rows : LANES + (b + 1) * rows]
                q_ref[:, at] = both[b * rank : (b + 1) * rank]
                approx[:, at] = near
                error_ref[:, at] = e_ref[:, at] + g_ref[t, :, b * LANES : (b + 1) * LANES] - near
    total = jnp.sum(gram * weigh_ref[...], keepdims=True)
    scale = jnp.minimum(1.0, limit / jnp.sqrt(total))
    momentum_ref[...] = BETA * m_ref[...] + scale * approx[...]


def body(tokens_x, cotangent, weight, error_fb, momentum, q_prev):
    n_t, n_r, n_z = lax.axis_size(T), lax.axis_size(R), lax.axis_size("z")
    t = lax.axis_index(T)[None]
    core = lax.axis_index("core")[None]
    tokens, wide = tokens_x.shape
    rows, width = weight.shape
    rank = q_prev.shape[0]
    ff_win = rows * n_t
    own = wide // n_r
    group = own // 4
    error = error_fb[0]
    halves = ff_win // LANES if ff_win >= LANES else 1

    (first,) = call(
        cut_kernel,
        [((n_t, rows, wide), F32)],
        [HBM],
        moved=2**20,
        limit=None,
        scratch_shapes=[pltpu.SemaphoreType.DMA((n_t,))],
    )(error)
    (share,) = call(
        share_kernel,
        [((rows + rank, tokens), F32)],
        [SMEM] + [HBM] * 3,
        flops=2**24,
        moved=2**19,
        limit=None,
        scratch_shapes=[
            pltpu.VMEM(tokens_x.shape, BF16),
            pltpu.VMEM(cotangent.shape, BF16),
            pltpu.VMEM((rank, wide), F32),
            pltpu.SemaphoreType.DMA((3,)),
        ],
    )(t, tokens_x, cotangent, q_prev)
    first, error_late = lax.optimization_barrier((first, error))
    (p_error,) = call(
        project_kernel, [((rows, rank), F32)], [VMEM] * 2, flops=2**27, moved=2 * 2**20
    )(error_late, q_prev)
    first = exchange(first, T)
    share = lax.all_gather(share, T)

    second, cot_all = call(
        merge_kernel,
        [((n_r, halves * own + 4, LANES), F32), ((ff_win, tokens), BF16)],
        [VMEM] * 5,
        moved=2 * 2**20,
    )(first, share, tokens_x, cotangent, p_error)
    (third,) = call(
        rows_kernel, [((n_t, rows, 2 * wide), F32)], [VMEM] * 3, flops=2**25, moved=2**20
    )(cot_all, tokens_x, weight)
    second = exchange(second, R)

    second, third = lax.optimization_barrier((second, third))
    third = exchange(third, T)
    total_t, p_pack = call(
        functools.partial(sum_kernel, n_t),
        [((own, 2 * ff_win), F32), ((SUB, LANES), F32)],
        [VMEM],
        moved=2**20,
    )(second)
    p_all = lax.all_gather(p_pack, T, tiled=True)

    q_send, gram, inverse = call(
        functools.partial(factor_kernel, n_r),
        [((n_r * n_z, group, LANES), F32), ((rank, rank), F32), ((rank, rank), F32)],
        [VMEM] * 2,
        flops=2**29,
        moved=2**20,
    )(p_all, total_t)
    q_send, third = lax.optimization_barrier((q_send, third))
    mine = exchange(q_send, CHIPS)
    w_cols = third[:, :, wide:].reshape(ff_win, wide).astype(BF16)
    input_grad = tn(cot_all, w_cols, None).astype(BF16)
    basis_gram = dot(dot(inverse, gram), inverse.T)
    p_rows = p_pack[:4].reshape(4, 4, rank).transpose(1, 0, 2).reshape(rows, rank)
    basis4 = jnp.tile(dot(p_rows, inverse.T), (1, 4))
    square = (LANES, LANES)
    weigh = jnp.where(
        iota(square, 0) // rank == iota(square, 1) // rank, jnp.tile(basis_gram, (4, 4)), 0.0
    )
    other = lax.ppermute(mine, "core", [(0, 1), (1, 0)])
    blocks = (n_z, LANES, LANES)
    limit = CLIPPING * math.sqrt(ff_win * width)
    q_new, error_new, momentum_new = call(
        functools.partial(last_kernel, limit),
        [((rank, width), F32), ((rows, width), F32), ((rows, width), F32)],
        [SMEM] + [VMEM] * 7,
        flops=2**30,
        moved=5 * 2**20,
        scratch_shapes=[pltpu.VMEM((rows, width), F32)],
    )(core, mine.reshape(blocks), other.reshape(blocks), basis4, weigh, error, third, momentum)

    return (input_grad, error_new[None], momentum_new, q_new)


def solution(mesh):
    n_r, n_t = mesh.devices.shape
    x = 4 if n_r > 4 else 2
    split = Mesh(mesh.devices.reshape(n_r // x, x, n_t // 2, 2), (*R, *T))
    placed = (P(R, T), P(T, R), P(T, None), P(R, T, None), P(T, None), P())
    return jax.shard_map(
        body,
        mesh=split,
        in_specs=placed,
        out_specs=(P(R, T), P(R, T, None), P(T, None), P()),
        check_vma=False,
    )
```

```python
import functools
import math

import jax
import jax.numpy as jnp
from jax import lax
from jax.experimental import pallas as pl
from jax.experimental.pallas import tpu as pltpu
from jax.sharding import Mesh, PartitionSpec as P

CLIPPING = 0.2
BETA = 0.9
HIGHEST = lax.Precision.HIGHEST
LANES = 128
SUB = 8
F32 = jnp.float32
BF16 = jnp.bfloat16

T = ("z", "core")
R = ("y", "x")
CHIPS = ("z", "y", "x")

VMEM = pl.BlockSpec(memory_space=pltpu.VMEM)
SMEM = pl.BlockSpec(memory_space=pltpu.SMEM)
HBM = pl.BlockSpec(memory_space=pltpu.HBM)


def exchange(parts, axes):
    return lax.all_to_all(parts, axes, 0, 0, tiled=True)


def call(kernel, outs, in_specs=None, out_specs=None, flops=0, moved=0, limit=48, **more):
    outs = [jax.ShapeDtypeStruct(*o) for o in outs]
    return functools.partial(
        pl.pallas_call,
        kernel,
        out_shape=outs,
        out_specs=out_specs or [VMEM] * len(outs),
        cost_estimate=pl.CostEstimate(flops=flops, bytes_accessed=moved, transcendentals=0),
        compiler_params=pltpu.CompilerParams(vmem_limit_bytes=limit and limit * 2**20),
        **more,
    )(in_specs=in_specs)


def iota(shape, axis):
    return lax.broadcasted_iota(jnp.int32, shape, axis)


def nt(a, b, precision=HIGHEST):
    return lax.dot_general(a, b, (((1,), (1,)), ((), ())), precision=precision, preferred_element_type=F32)


def tn(a, b, precision=HIGHEST):
    return lax.dot_general(a, b, (((0,), (0,)), ((), ())), precision=precision, preferred_element_type=F32)


def dot(a, b, precision=HIGHEST):
    return jnp.dot(a, b, precision=precision, preferred_element_type=F32)


def fold_rows(tiled, group):
    n = tiled.shape[0]
    kept = jnp.where(iota(tiled.shape, 0) // group == iota(tiled.shape, 1) // 32, tiled, 0.0)
    out = max(group, SUB)
    pick = (iota((out, n), 1) % group == iota((out, n), 0)).astype(F32)
    return dot(pick, kept)


def first_kernel(t_ref, x_ref, c_ref, e_ref, q_ref, send_ref, x, c, q, sems):
    n_t, rows, _ = send_ref.shape
    tokens, wide = x_ref.shape
    start = pl.multiple_of(t_ref[0] * wide, wide)
    copies = [
        pltpu.make_async_copy(q_ref.at[:, pl.ds(start, wide)], q, sems.at[0]),
        pltpu.make_async_copy(x_ref, x, sems.at[1]),
        pltpu.make_async_copy(c_ref, c, sems.at[2]),
    ]
    for k in range(n_t):
        copies.append(
            pltpu.make_async_copy(
                e_ref.at[:, pl.ds(k * wide, wide)], send_ref.at[k, :, pl.ds(0, wide)], sems.at[3 + k]
            )
        )
    for copy in copies:
        copy.start()
    for copy in copies[:3]:
        copy.wait()
    y = nt(q[...], x[...].astype(F32))
    cot = c[...].astype(F32)
    for k in range(n_t):
        send_ref[k, :, wide : wide + tokens] = cot
        for g in range(y.shape[0] // rows):
            at = wide + tokens + g * tokens
            send_ref[k, :, at : at + tokens] = y[g * rows : (g + 1) * rows]
    for copy in copies[3:]:
        copy.wait()


def project_kernel(e_ref, q_ref, pe_ref):
    pe_ref[...] = nt(e_ref[...], q_ref[...])


def merge_kernel(got_ref, x_ref, c_ref, pe_ref, send_ref, cot_ref):
    n_t, rows, _ = got_ref.shape
    tokens, wide = x_ref.shape
    n_r = send_ref.shape[0]
    group = LANES // n_r
    ff_win = n_t * rows
    cot = got_ref[:, :, wide : wide + tokens].reshape(ff_win, tokens).astype(BF16)
    cot_ref[...] = cot
    y = jnp.sum(got_ref[:, :, wide + tokens :], 0)
    folds = y.shape[1] // tokens
    y = jnp.concatenate([y[:, g * tokens : (g + 1) * tokens] for g in range(folds)], 0)
    rank = y.shape[0]
    y4 = jnp.concatenate([y] * (LANES // rank), 0)
    tile = (iota((rank, LANES), 1) % rank == iota((rank, LANES), 0)).astype(F32)
    p4 = nt(c_ref[...].astype(F32), y4) + dot(pe_ref[...], tile)
    p_pack = fold_rows(p4, rows // 4)

    merged = got_ref[:, :, :wide].reshape(ff_win, wide) + dot(cot, x_ref[...], None)
    out, col = iota((wide, wide), 0), iota((wide, wide), 1)
    own = wide // n_r
    r, b, a = out // own, out % own // group, out % group
    turn = (col == b * LANES + r * group + a).astype(BF16)
    turned = jnp.zeros((wide, ff_win), F32)
    rest = merged
    for _ in range(3):
        piece = rest.astype(BF16)
        turned += nt(turn, piece, None)
        rest -= piece.astype(F32)
    halves = ff_win // LANES if ff_win >= LANES else 1
    width = ff_win // halves
    for k in range(n_r):
        for h in range(halves):
            send_ref[k, h * own : (h + 1) * own, :width] = turned[
                k * own : (k + 1) * own, h * width : (h + 1) * width
            ]
        send_ref[k, halves * own :, :] = p_pack[: send_ref.shape[1] - halves * own]


def rows_kernel(t_ref, c_ref, cot_ref, got_ref, g_ref, dx_ref, w):
    n_t = got_ref.shape[0]
    rows, tokens = c_ref.shape
    wide = got_ref.shape[2]
    at = pl.ds(pl.multiple_of(tokens + t_ref[0] * rows, rows), rows)
    for k in range(n_t):
        g_ref[:, k * wide : (k + 1) * wide] = dot(c_ref[...], got_ref[k, :tokens, :], None)
        w[k * rows : (k + 1) * rows] = got_ref[k, at, :]
    dx_ref[...] = tn(cot_ref[...], w[...], None).astype(BF16)


def sum_kernel(n_t, got_ref, total_ref, pack_ref):
    own, long = total_ref.shape
    ff_win = long // 2
    rows = ff_win // n_t
    got = jnp.sum(got_ref[...], 0)
    pack = got[got.shape[0] - 4 :]
    pack_ref[...] = jnp.concatenate([pack, jnp.zeros_like(pack)], 0)
    halves = ff_win // LANES if ff_win >= LANES else 1
    width = ff_win // halves
    total = jnp.zeros(total_ref.shape, F32)
    for h in range(halves):
        unit, lane = iota((width, long), 0) + h * width, iota((width, long), 1)
        t, b, a = unit // rows, unit % rows // 4, unit % 4
        move = (lane == b * (SUB * n_t) + t * SUB + a).astype(F32)
        total += dot(got[h * own : (h + 1) * own, :width], move)
    total_ref[...] = total


def factor_kernel(n_r, pack_ref, total_ref, send_ref, gram_ref, inverse_ref):
    span = pack_ref.shape[0]
    own = total_ref.shape[0]
    rank = gram_ref.shape[0]
    group = own // 4
    pack = pack_ref[...]
    gram4 = tn(pack, pack)
    gram = sum(gram4[b * rank : (b + 1) * rank, b * rank : (b + 1) * rank] for b in range(4))
    gram_ref[...] = gram
    row, lane = iota((rank, LANES), 0), iota((rank, LANES), 1)
    work = jnp.concatenate([gram, jnp.zeros((rank, LANES - rank), F32)], 1)
    work = jnp.where(lane == row + rank, 1.0, work)
    for j in range(rank):
        pivot = work[j : j + 1, :]
        factor = work[:, j : j + 1] / work[j : j + 1, j : j + 1]
        work = jnp.where(row > j, work - factor * pivot, work)
    diagonal = jnp.sum(jnp.where(lane == row, work, 0.0), 1, keepdims=True)
    inverse = (work * lax.rsqrt(diagonal))[:, rank : 2 * rank]
    inverse_ref[...] = inverse
    inverse16 = jnp.concatenate([inverse] * 4, 0)
    inverse16 = jnp.concatenate([inverse16] * 4, 1)
    total = total_ref[...]
    product = jnp.zeros((own, LANES), F32)
    for b in range(4):
        part = dot(total[:, b * span : (b + 1) * span], pack)
        product = jnp.where(iota(part.shape, 1) // rank == b, part, product)
    q4 = nt(product, inverse16) / n_r
    q_pack = fold_rows(q4, group)[:group]
    send_ref[...] = jnp.broadcast_to(q_pack[None], send_ref.shape)


def last_kernel(limit, core_ref, mine_ref, other_ref, basis_ref, weigh_ref, e_ref, g_ref, m_ref, q_ref, error_ref, momentum_ref, approx):
    n_z = mine_ref.shape[0]
    rows = e_ref.shape[0]
    rank = q_ref.shape[0]
    core = core_ref[0]
    wide = 4 * LANES
    square = (LANES, LANES)
    basis4 = basis_ref[...]
    stack = jnp.concatenate(
        [(iota(square, 0) == iota(square, 1)).astype(F32)]
        + [jnp.where(iota(basis4.shape, 1) // rank == b, basis4, 0.0) for b in range(4)],
        0,
    )
    gram = jnp.zeros(square, F32)
    for z in range(n_z):
        for ref, c in ((mine_ref, core), (other_ref, 1 - core)):
            block = ref[z]
            gram += tn(block, block)
            both = nt(stack, block)
            t = 2 * z + c
            for b in range(4):
                at = pl.ds(pl.multiple_of(t * wide + b * LANES, LANES), LANES)
                near = both[LANES + b * rows : LANES + (b + 1) * rows]
                q_ref[:, at] = both[b * rank : (b + 1) * rank]
                approx[:, at] = near
                error_ref[:, at] = e_ref[:, at] + g_ref[:, at] - near
    total = jnp.sum(gram * weigh_ref[...], keepdims=True)
    scale = jnp.minimum(1.0, limit / jnp.sqrt(total))
    momentum_ref[...] = BETA * m_ref[...] + scale * approx[...]


def body(tokens_x, cotangent, weight, error_fb, momentum, q_prev):
    n_t, n_r, n_z = lax.axis_size(T), lax.axis_size(R), lax.axis_size("z")
    t = lax.axis_index(T)[None]
    core = lax.axis_index("core")[None]
    tokens, wide = tokens_x.shape
    rows, width = weight.shape
    rank = q_prev.shape[0]
    ff_win = rows * n_t
    own = wide // n_r
    group = own // 4
    error = error_fb[0]
    halves = ff_win // LANES if ff_win >= LANES else 1

    (first,) = call(
        first_kernel,
        [((n_t, rows, wide + tokens + rank // rows * tokens), F32)],
        [SMEM] + [HBM] * 4,
        moved=3 * 2**20,
        limit=None,
        scratch_shapes=[
            pltpu.VMEM(tokens_x.shape, BF16),
            pltpu.VMEM(cotangent.shape, BF16),
            pltpu.VMEM((rank, wide), F32),
            pltpu.SemaphoreType.DMA((3 + n_t,)),
        ],
    )(t, tokens_x, cotangent, error, q_prev)
    w_parts = weight.reshape(rows, n_t, wide).transpose(1, 0, 2)
    first, error_late = lax.optimization_barrier((first, error))
    (p_error,) = call(
        project_kernel, [((rows, rank), F32)], [VMEM] * 2, flops=2**27, moved=2 * 2**20
    )(error_late, q_prev)
    first = exchange(first, T)

    bulk = jnp.concatenate([tokens_x, w_parts.reshape(rows * n_t, wide)], 0)
    first, bulk = lax.optimization_barrier((first, bulk))
    bulk = lax.all_gather(bulk, T)
    second, cot_all = call(
        merge_kernel,
        [((n_r, halves * own + 4, LANES), F32), ((ff_win, tokens), BF16)],
        [VMEM] * 4,
        moved=2 * 2**20,
    )(first, tokens_x, cotangent, p_error)
    second = exchange(second, R)
    total_t, p_pack = call(
        functools.partial(sum_kernel, n_t),
        [((own, 2 * ff_win), F32), ((SUB, LANES), F32)],
        [VMEM],
        moved=2**20,
    )(second)
    p_all = exchange(jnp.broadcast_to(p_pack[None], (n_t, SUB, LANES)), T)

    q_send, gram, inverse = call(
        functools.partial(factor_kernel, n_r),
        [((n_r * n_z, group, LANES), F32), ((rank, rank), F32), ((rank, rank), F32)],
        [VMEM] * 2,
        flops=2**29,
        moved=2**20,
    )(p_all.reshape(n_t * SUB, LANES), total_t)
    q_send, bulk = lax.optimization_barrier((q_send, bulk))
    mine = exchange(q_send, CHIPS)
    grad_rows, input_grad = call(
        rows_kernel,
        [((rows, width), F32), ((tokens, wide), BF16)],
        [SMEM] + [VMEM] * 3,
        flops=2**28,
        moved=8 * 2**20,
        scratch_shapes=[pltpu.VMEM((ff_win, wide), BF16)],
    )(t, cotangent, cot_all, bulk)
    basis_gram = dot(dot(inverse, gram), inverse.T)
    p_rows = p_pack[:4].reshape(4, 4, rank).transpose(1, 0, 2).reshape(rows, rank)
    basis4 = jnp.tile(dot(p_rows, inverse.T), (1, 4))
    square = (LANES, LANES)
    weigh = jnp.where(
        iota(square, 0) // rank == iota(square, 1) // rank, jnp.tile(basis_gram, (4, 4)), 0.0
    )
    other = lax.ppermute(mine, "core", [(0, 1), (1, 0)])
    blocks = (n_z, LANES, LANES)
    limit = CLIPPING * math.sqrt(ff_win * width)
    q_new, error_new, momentum_new = call(
        functools.partial(last_kernel, limit),
        [((rank, width), F32), ((rows, width), F32), ((rows, width), F32)],
        [SMEM] + [VMEM] * 7,
        flops=2**30,
        moved=5 * 2**20,
        scratch_shapes=[pltpu.VMEM((rows, width), F32)],
    )(core, mine.reshape(blocks), other.reshape(blocks), basis4, weigh, error, grad_rows, momentum)

    return (input_grad, error_new[None], momentum_new, q_new)


def solution(mesh):
    n_r, n_t = mesh.devices.shape
    x = 4 if n_r > 4 else 2
    split = Mesh(mesh.devices.reshape(n_r // x, x, n_t // 2, 2), (*R, *T))
    placed = (P(R, T), P(T, R), P(T, None), P(R, T, None), P(T, None), P())
    return jax.shard_map(
        body,
        mesh=split,
        in_specs=placed,
        out_specs=(P(R, T), P(R, T, None), P(T, None), P()),
        check_vma=False,
    )
```

```python
import functools
import math

import jax
import jax.numpy as jnp
from jax import lax
from jax.experimental import pallas as pl
from jax.experimental.pallas import tpu as pltpu
from jax.sharding import Mesh, PartitionSpec as P

CLIPPING = 0.2
BETA = 0.9
HIGHEST = lax.Precision.HIGHEST
LANES = 128
SUB = 8
F32 = jnp.float32
BF16 = jnp.bfloat16

T = ("z", "core")
R = ("y", "x")
CHIPS = ("z", "y", "x")

VMEM = pl.BlockSpec(memory_space=pltpu.VMEM)
SMEM = pl.BlockSpec(memory_space=pltpu.SMEM)
HBM = pl.BlockSpec(memory_space=pltpu.HBM)


def exchange(parts, axes):
    return lax.all_to_all(parts, axes, 0, 0, tiled=True)


def call(kernel, outs, in_specs=None, out_specs=None, flops=0, moved=0, limit=48, **more):
    outs = [jax.ShapeDtypeStruct(*o) for o in outs]
    return functools.partial(
        pl.pallas_call,
        kernel,
        out_shape=outs,
        out_specs=out_specs or [VMEM] * len(outs),
        cost_estimate=pl.CostEstimate(flops=flops, bytes_accessed=moved, transcendentals=0),
        compiler_params=pltpu.CompilerParams(vmem_limit_bytes=limit and limit * 2**20),
        **more,
    )(in_specs=in_specs)


def iota(shape, axis):
    return lax.broadcasted_iota(jnp.int32, shape, axis)


def nt(a, b, precision=HIGHEST):
    return lax.dot_general(a, b, (((1,), (1,)), ((), ())), precision=precision, preferred_element_type=F32)


def tn(a, b, precision=HIGHEST):
    return lax.dot_general(a, b, (((0,), (0,)), ((), ())), precision=precision, preferred_element_type=F32)


def dot(a, b, precision=HIGHEST):
    return jnp.dot(a, b, precision=precision, preferred_element_type=F32)


def fold_rows(tiled, group):
    n = tiled.shape[0]
    kept = jnp.where(iota(tiled.shape, 0) // group == iota(tiled.shape, 1) // 32, tiled, 0.0)
    out = max(group, SUB)
    pick = (iota((out, n), 1) % group == iota((out, n), 0)).astype(F32)
    return dot(pick, kept)


def first_kernel(t_ref, x_ref, c_ref, e_ref, q_ref, send_ref, x, c, q, sems):
    n_t, rows, _ = send_ref.shape
    tokens, wide = x_ref.shape
    start = pl.multiple_of(t_ref[0] * wide, wide)
    copies = [
        pltpu.make_async_copy(q_ref.at[:, pl.ds(start, wide)], q, sems.at[0]),
        pltpu.make_async_copy(x_ref, x, sems.at[1]),
        pltpu.make_async_copy(c_ref, c, sems.at[2]),
    ]
    for k in range(n_t):
        copies.append(
            pltpu.make_async_copy(
                e_ref.at[:, pl.ds(k * wide, wide)], send_ref.at[k, :, pl.ds(0, wide)], sems.at[3 + k]
            )
        )
    for copy in copies:
        copy.start()
    for copy in copies[:3]:
        copy.wait()
    y = nt(q[...], x[...].astype(F32))
    cot = c[...].astype(F32)
    for k in range(n_t):
        send_ref[k, :, wide : wide + tokens] = cot
        for g in range(y.shape[0] // rows):
            at = wide + tokens + g * tokens
            send_ref[k, :, at : at + tokens] = y[g * rows : (g + 1) * rows]
    for copy in copies[3:]:
        copy.wait()


def project_kernel(e_ref, q_ref, pe_ref):
    pe_ref[...] = nt(e_ref[...], q_ref[...])


def merge_kernel(got_ref, x_ref, c_ref, pe_ref, send_ref, cot_ref):
    n_t, rows, _ = got_ref.shape
    tokens, wide = x_ref.shape
    n_r = send_ref.shape[0]
    group = LANES // n_r
    ff_win = n_t * rows
    cot = got_ref[:, :, wide : wide + tokens].reshape(ff_win, tokens).astype(BF16)
    cot_ref[...] = cot
    y = jnp.sum(got_ref[:, :, wide + tokens :], 0)
    folds = y.shape[1] // tokens
    y = jnp.concatenate([y[:, g * tokens : (g + 1) * tokens] for g in range(folds)], 0)
    rank = y.shape[0]
    y4 = jnp.concatenate([y] * (LANES // rank), 0)
    tile = (iota((rank, LANES), 1) % rank == iota((rank, LANES), 0)).astype(F32)
    p4 = nt(c_ref[...].astype(F32), y4) + dot(pe_ref[...], tile)
    p_pack = fold_rows(p4, rows // 4)

    merged = got_ref[:, :, :wide].reshape(ff_win, wide) + dot(cot, x_ref[...], None)
    out, col = iota((wide, wide), 0), iota((wide, wide), 1)
    own = wide // n_r
    r, b, a = out // own, out % own // group, out % group
    turn = (col == b * LANES + r * group + a).astype(BF16)
    turned = jnp.zeros((wide, ff_win), F32)
    rest = merged
    for _ in range(3):
        piece = rest.astype(BF16)
        turned += nt(turn, piece, None)
        rest -= piece.astype(F32)
    halves = ff_win // LANES if ff_win >= LANES else 1
    width = ff_win // halves
    for k in range(n_r):
        for h in range(halves):
            send_ref[k, h * own : (h + 1) * own, :width] = turned[
                k * own : (k + 1) * own, h * width : (h + 1) * width
            ]
        send_ref[k, halves * own :, :] = p_pack[: send_ref.shape[1] - halves * own]


def rows_kernel(t_ref, c_ref, cot_ref, got_ref, g_ref, dx_ref, w):
    n_t = got_ref.shape[0]
    rows, tokens = c_ref.shape
    wide = got_ref.shape[2]
    at = pl.ds(pl.multiple_of(tokens + t_ref[0] * rows, rows), rows)
    for k in range(n_t):
        g_ref[:, k * wide : (k + 1) * wide] = dot(c_ref[...], got_ref[k, :tokens, :], None)
        w[k * rows : (k + 1) * rows] = got_ref[k, at, :]
    dx_ref[...] = tn(cot_ref[...], w[...], None).astype(BF16)


def sum_kernel(n_t, got_ref, total_ref, pack_ref):
    own, long = total_ref.shape
    ff_win = long // 2
    rows = ff_win // n_t
    got = jnp.sum(got_ref[...], 0)
    pack = got[got.shape[0] - 4 :]
    pack_ref[...] = jnp.concatenate([pack, jnp.zeros_like(pack)], 0)
    halves = ff_win // LANES if ff_win >= LANES else 1
    width = ff_win // halves
    total = jnp.zeros(total_ref.shape, F32)
    for h in range(halves):
        unit, lane = iota((width, long), 0) + h * width, iota((width, long), 1)
        t, b, a = unit // rows, unit % rows // 4, unit % 4
        move = (lane == b * (SUB * n_t) + t * SUB + a).astype(F32)
        total += dot(got[h * own : (h + 1) * own, :width], move)
    total_ref[...] = total


def factor_kernel(n_r, pack_ref, total_ref, send_ref, gram_ref, inverse_ref):
    span = pack_ref.shape[0]
    own = total_ref.shape[0]
    rank = gram_ref.shape[0]
    group = own // 4
    pack = pack_ref[...]
    gram4 = tn(pack, pack)
    gram = sum(gram4[b * rank : (b + 1) * rank, b * rank : (b + 1) * rank] for b in range(4))
    gram_ref[...] = gram
    row, lane = iota((rank, LANES), 0), iota((rank, LANES), 1)
    work = jnp.concatenate([gram, jnp.zeros((rank, LANES - rank), F32)], 1)
    work = jnp.where(lane == row + rank, 1.0, work)
    for j in range(rank):
        pivot = work[j : j + 1, :]
        factor = work[:, j : j + 1] / work[j : j + 1, j : j + 1]
        work = jnp.where(row > j, work - factor * pivot, work)
    diagonal = jnp.sum(jnp.where(lane == row, work, 0.0), 1, keepdims=True)
    inverse = (work * lax.rsqrt(diagonal))[:, rank : 2 * rank]
    inverse_ref[...] = inverse
    inverse16 = jnp.concatenate([inverse] * 4, 0)
    inverse16 = jnp.concatenate([inverse16] * 4, 1)
    total = total_ref[...]
    product = jnp.zeros((own, LANES), F32)
    for b in range(4):
        part = dot(total[:, b * span : (b + 1) * span], pack)
        product = jnp.where(iota(part.shape, 1) // rank == b, part, product)
    q4 = nt(product, inverse16) / n_r
    q_pack = fold_rows(q4, group)[:group]
    send_ref[...] = jnp.broadcast_to(q_pack[None], send_ref.shape)


def place_blocks(near_core, blocks_ref, basis_ref, e_ref, g_ref, q_hbm, error_hbm, q, error, sems, approx_ref, gram):
    n_z = blocks_ref.shape[0]
    rows = e_ref.shape[0]
    rank = q.shape[1]
    square = (LANES, LANES)
    basis4 = basis_ref[...]
    stack = jnp.concatenate(
        [(iota(square, 0) == iota(square, 1)).astype(F32)]
        + [jnp.where(iota(basis4.shape, 1) // rank == b, basis4, 0.0) for b in range(4)],
        0,
    )
    copies = []
    for z in range(n_z):
        block = blocks_ref[z]
        gram += tn(block, block)
        both = nt(stack, block)
        start = pl.multiple_of((2 * z + near_core) * 4 * LANES, 4 * LANES)
        for b in range(4):
            near = both[LANES + b * rows : LANES + (b + 1) * rows]
            at = pl.ds(pl.multiple_of(start + b * LANES, LANES), LANES)
            to = slice(b * LANES, (b + 1) * LANES)
            q[z, :, to] = both[b * rank : (b + 1) * rank]
            approx_ref[z, :, to] = near
            error[z, :, to] = e_ref[:, at] + g_ref[:, at] - near
        span = pl.ds(start, 4 * LANES)
        copies.append(pltpu.make_async_copy(q.at[z], q_hbm.at[:, span], sems.at[0, z]))
        copies.append(pltpu.make_async_copy(error.at[z], error_hbm.at[:, span], sems.at[1, z]))
        copies[-2].start()
        copies[-1].start()
    return gram, copies


def near_kernel(core_ref, mine_ref, basis_ref, e_ref, g_ref, q_hbm, error_hbm, approx_ref, gram_ref, q, error, sems):
    gram, copies = place_blocks(
        core_ref[0], mine_ref, basis_ref, e_ref, g_ref, q_hbm, error_hbm, q, error, sems, approx_ref,
        jnp.zeros((LANES, LANES), F32),
    )
    gram_ref[...] = gram
    for copy in copies:
        copy.wait()


def far_kernel(limit, core_ref, other_ref, basis_ref, e_ref, g_ref, gram_ref, approx_ref, weigh_ref, m_ref, q_old, error_old, q_hbm, error_hbm, momentum_ref, q, error, sems, far):
    core = core_ref[0]
    gram, copies = place_blocks(
        1 - core, other_ref, basis_ref, e_ref, g_ref, q_hbm, error_hbm, q, error, sems, far, gram_ref[...]
    )
    total = jnp.sum(gram * weigh_ref[...], keepdims=True)
    scale = jnp.minimum(1.0, limit / jnp.sqrt(total))
    for z in range(other_ref.shape[0]):
        for ref, c in ((approx_ref, core), (far, 1 - core)):
            at = pl.ds(pl.multiple_of((2 * z + c) * 4 * LANES, 4 * LANES), 4 * LANES)
            momentum_ref[:, at] = BETA * m_ref[:, at] + scale * ref[z]
    for copy in copies:
        copy.wait()


def body(tokens_x, cotangent, weight, error_fb, momentum, q_prev):
    n_t, n_r, n_z = lax.axis_size(T), lax.axis_size(R), lax.axis_size("z")
    t = lax.axis_index(T)[None]
    core = lax.axis_index("core")[None]
    tokens, wide = tokens_x.shape
    rows, width = weight.shape
    rank = q_prev.shape[0]
    ff_win = rows * n_t
    own = wide // n_r
    group = own // 4
    error = error_fb[0]
    halves = ff_win // LANES if ff_win >= LANES else 1

    (first,) = call(
        first_kernel,
        [((n_t, rows, wide + tokens + rank // rows * tokens), F32)],
        [SMEM] + [HBM] * 4,
        moved=3 * 2**20,
        limit=None,
        scratch_shapes=[
            pltpu.VMEM(tokens_x.shape, BF16),
            pltpu.VMEM(cotangent.shape, BF16),
            pltpu.VMEM((rank, wide), F32),
            pltpu.SemaphoreType.DMA((3 + n_t,)),
        ],
    )(t, tokens_x, cotangent, error, q_prev)
    w_parts = weight.reshape(rows, n_t, wide).transpose(1, 0, 2)
    first, error_late = lax.optimization_barrier((first, error))
    (p_error,) = call(
        project_kernel, [((rows, rank), F32)], [VMEM] * 2, flops=2**27, moved=2 * 2**20
    )(error_late, q_prev)
    first = exchange(first, T)

    bulk = jnp.concatenate([tokens_x, w_parts.reshape(rows * n_t, wide)], 0)
    first, bulk, p_error = lax.optimization_barrier((first, bulk, p_error))
    bulk = lax.all_gather(bulk, T)
    second, cot_all = call(
        merge_kernel,
        [((n_r, halves * own + 4, LANES), F32), ((ff_win, tokens), BF16)],
        [VMEM] * 4,
        moved=2 * 2**20,
    )(first, tokens_x, cotangent, p_error)
    second = exchange(second, R)
    total_t, p_pack = call(
        functools.partial(sum_kernel, n_t),
        [((own, 2 * ff_win), F32), ((SUB, LANES), F32)],
        [VMEM],
        moved=2**20,
    )(second)
    p_all = exchange(jnp.broadcast_to(p_pack[None], (n_t, SUB, LANES)), T)

    q_send, gram, inverse = call(
        functools.partial(factor_kernel, n_r),
        [((n_r * n_z, group, LANES), F32), ((rank, rank), F32), ((rank, rank), F32)],
        [VMEM] * 2,
        flops=2**29,
        moved=2**20,
    )(p_all.reshape(n_t * SUB, LANES), total_t)
    mine = exchange(q_send, CHIPS)
    grad_rows, input_grad = call(
        rows_kernel,
        [((rows, width), F32), ((tokens, wide), BF16)],
        [SMEM] + [VMEM] * 3,
        flops=2**28,
        moved=8 * 2**20,
        scratch_shapes=[pltpu.VMEM((ff_win, wide), BF16)],
    )(t, cotangent, cot_all, bulk)
    mine, grad_rows = lax.optimization_barrier((mine, grad_rows))
    basis_gram = dot(dot(inverse, gram), inverse.T)
    p_rows = p_pack[:4].reshape(4, 4, rank).transpose(1, 0, 2).reshape(rows, rank)
    basis4 = jnp.tile(dot(p_rows, inverse.T), (1, 4))
    square = (LANES, LANES)
    weigh = jnp.where(
        iota(square, 0) // rank == iota(square, 1) // rank, jnp.tile(basis_gram, (4, 4)), 0.0
    )
    other = lax.ppermute(mine, "core", [(0, 1), (1, 0)])
    blocks = (n_z, LANES, LANES)
    limit = CLIPPING * math.sqrt(ff_win * width)
    scratch = [
        pltpu.VMEM((n_z, rank, wide), F32),
        pltpu.VMEM((n_z, rows, wide), F32),
        pltpu.SemaphoreType.DMA((2, n_z)),
    ]
    whole = [((rank, width), F32), ((rows, width), F32)]
    q_new, error_new, approx, q_gram = call(
        near_kernel,
        [*whole, ((n_z, rows, wide), F32), ((LANES, LANES), F32)],
        [SMEM] + [VMEM] * 4,
        [HBM, HBM, VMEM, VMEM],
        flops=2**30,
        moved=3 * 2**20,
        scratch_shapes=scratch,
    )(core, mine.reshape(blocks), basis4, error, grad_rows)
    q_new, error_new, momentum_new = call(
        functools.partial(far_kernel, limit),
        [*whole, ((rows, width), F32)],
        [SMEM] + [VMEM] * 8 + [HBM, HBM],
        [HBM, HBM, VMEM],
        flops=2**30,
        moved=4 * 2**20,
        scratch_shapes=[*scratch, pltpu.VMEM((n_z, rows, wide), F32)],
        input_output_aliases={9: 0, 10: 1},
    )(core, other.reshape(blocks), basis4, error, grad_rows, q_gram, approx, weigh, momentum, q_new, error_new)
    return (input_grad, error_new[None], momentum_new, q_new)


def solution(mesh):
    n_r, n_t = mesh.devices.shape
    x = 4 if n_r > 4 else 2
    split = Mesh(mesh.devices.reshape(n_r // x, x, n_t // 2, 2), (*R, *T))
    placed = (P(R, T), P(T, R), P(T, None), P(R, T, None), P(T, None), P())
    return jax.shard_map(
        body,
        mesh=split,
        in_specs=placed,
        out_specs=(P(R, T), P(R, T, None), P(T, None), P()),
        check_vma=False,
    )
```

```python
import functools
import math

import jax
import jax.numpy as jnp
from jax import lax
from jax.experimental import pallas as pl
from jax.experimental.pallas import tpu as pltpu
from jax.sharding import Mesh, PartitionSpec as P

CLIPPING = 0.2
BETA = 0.9
HIGHEST = lax.Precision.HIGHEST
LANES = 128
SUB = 8
F32 = jnp.float32
BF16 = jnp.bfloat16

T = ("z", "core")
R = ("y", "x")
CHIPS = ("z", "y", "x")

VMEM = pl.BlockSpec(memory_space=pltpu.VMEM)
SMEM = pl.BlockSpec(memory_space=pltpu.SMEM)
HBM = pl.BlockSpec(memory_space=pltpu.HBM)


def exchange(parts, axes):
    return lax.all_to_all(parts, axes, 0, 0, tiled=True)


def call(kernel, outs, in_specs=None, out_specs=None, flops=0, moved=0, limit=48, **more):
    outs = [jax.ShapeDtypeStruct(*o) for o in outs]
    return functools.partial(
        pl.pallas_call,
        kernel,
        out_shape=outs,
        out_specs=out_specs or [VMEM] * len(outs),
        cost_estimate=pl.CostEstimate(flops=flops, bytes_accessed=moved, transcendentals=0),
        compiler_params=pltpu.CompilerParams(vmem_limit_bytes=limit and limit * 2**20),
        **more,
    )(in_specs=in_specs)


def iota(shape, axis):
    return lax.broadcasted_iota(jnp.int32, shape, axis)


def nt(a, b, precision=HIGHEST):
    return lax.dot_general(a, b, (((1,), (1,)), ((), ())), precision=precision, preferred_element_type=F32)


def tn(a, b, precision=HIGHEST):
    return lax.dot_general(a, b, (((0,), (0,)), ((), ())), precision=precision, preferred_element_type=F32)


def dot(a, b, precision=HIGHEST):
    return jnp.dot(a, b, precision=precision, preferred_element_type=F32)


def lane_halves(ff_win):
    halves = max(ff_win // LANES, 1)
    return halves, ff_win // halves


def fold_rows(tiled, group):
    n = tiled.shape[0]
    kept = jnp.where(iota(tiled.shape, 0) // group == iota(tiled.shape, 1) // 32, tiled, 0.0)
    out = max(group, SUB)
    pick = (iota((out, n), 1) % group == iota((out, n), 0)).astype(F32)
    return dot(pick, kept)


def first_kernel(t_ref, x_ref, c_ref, e_ref, q_ref, send_ref, x, c, q, sems):
    n_t, rows, _ = send_ref.shape
    tokens, wide = x_ref.shape
    start = pl.multiple_of(t_ref[0] * wide, wide)
    copies = [
        pltpu.make_async_copy(q_ref.at[:, pl.ds(start, wide)], q, sems.at[0]),
        pltpu.make_async_copy(x_ref, x, sems.at[1]),
        pltpu.make_async_copy(c_ref, c, sems.at[2]),
    ]
    for k in range(n_t):
        copies.append(
            pltpu.make_async_copy(
                e_ref.at[:, pl.ds(k * wide, wide)], send_ref.at[k, :, pl.ds(0, wide)], sems.at[3 + k]
            )
        )
    for copy in copies:
        copy.start()
    for copy in copies[:3]:
        copy.wait()
    y = nt(q[...], x[...].astype(F32))
    cot = c[...].astype(F32)
    for k in range(n_t):
        send_ref[k, :, wide : wide + tokens] = cot
        for g in range(y.shape[0] // rows):
            at = wide + tokens + g * tokens
            send_ref[k, :, at : at + tokens] = y[g * rows : (g + 1) * rows]
    for copy in copies[3:]:
        copy.wait()


def project_kernel(e_ref, q_ref, pe_ref):
    pe_ref[...] = nt(e_ref[...], q_ref[...])


def merge_kernel(got_ref, x_ref, c_ref, pe_ref, send_ref, cot_ref, turned_ref):
    n_t, rows, _ = got_ref.shape
    tokens, wide = x_ref.shape
    n_r = send_ref.shape[0]
    group = LANES // n_r
    ff_win = n_t * rows
    cot = got_ref[:, :, wide : wide + tokens].reshape(ff_win, tokens).astype(BF16)
    cot_ref[...] = cot
    y = jnp.sum(got_ref[:, :, wide + tokens :], 0)
    folds = y.shape[1] // tokens
    y = jnp.concatenate([y[:, g * tokens : (g + 1) * tokens] for g in range(folds)], 0)
    rank = y.shape[0]
    y4 = jnp.concatenate([y] * (LANES // rank), 0)
    tile = (iota((rank, LANES), 1) % rank == iota((rank, LANES), 0)).astype(F32)
    p4 = nt(c_ref[...].astype(F32), y4) + dot(pe_ref[...], tile)
    p_pack = fold_rows(p4, rows // 4)

    merged = got_ref[:, :, :wide].reshape(ff_win, wide) + dot(cot, x_ref[...], None)
    out, col = iota((wide, wide), 0), iota((wide, wide), 1)
    own = wide // n_r
    r, b, a = out // own, out % own // group, out % group
    turn = (col == b * LANES + r * group + a).astype(BF16)
    turned = jnp.zeros((wide, ff_win), F32)
    rest = merged
    for _ in range(3):
        piece = rest.astype(BF16)
        turned += nt(turn, piece, None)
        rest -= piece.astype(F32)
    turned_ref[...] = turned
    halves, width = lane_halves(ff_win)
    for k in range(n_r):
        for h in range(halves):
            for g in range(own // 4):
                send_ref[k, h * (own // 4) + g, :, :width] = turned_ref[
                    k * own + 4 * g : k * own + 4 * g + 4, h * width : (h + 1) * width
                ]
        send_ref[k, halves * (own // 4)] = p_pack[:4]


def rows_kernel(t_ref, c_ref, cot_ref, got_ref, g_ref, dx_ref, w):
    n_t = got_ref.shape[0]
    rows, tokens = c_ref.shape
    wide = got_ref.shape[2]
    at = pl.ds(pl.multiple_of(tokens + t_ref[0] * rows, rows), rows)
    for k in range(n_t):
        g_ref[:, k * wide : (k + 1) * wide] = dot(c_ref[...], got_ref[k, :tokens, :], None)
        w[k * rows : (k + 1) * rows] = got_ref[k, at, :]
    dx_ref[...] = tn(cot_ref[...], w[...], None).astype(BF16)


def sum_kernel(n_t, got_ref, total_ref, pack_ref, scratch):
    own, long = total_ref.shape
    ff_win = long // 2
    rows = ff_win // n_t
    halves, width = lane_halves(ff_win)
    got = jnp.sum(got_ref[...], 0)
    pack_ref[...] = jnp.broadcast_to(got[-1][None], pack_ref.shape)
    total = jnp.zeros(total_ref.shape, F32)
    for h in range(halves):
        for g in range(own // 4):
            scratch[h, 4 * g : 4 * g + 4, :] = got[h * (own // 4) + g]
        unit, lane = iota((width, long), 0) + h * width, iota((width, long), 1)
        t, b, a = unit // rows, unit % rows // 4, unit % 4
        move = (lane == b * (SUB * n_t) + t * SUB + a).astype(F32)
        total += dot(scratch[h, :, :width], move)
    total_ref[...] = total


def factor_kernel(n_r, pack_ref, total_ref, send_ref, gram_ref, inverse_ref, held):
    span = held.shape[0]
    own = total_ref.shape[0]
    rank = gram_ref.shape[0]
    group = own // 4
    held[...] = jnp.zeros(held.shape, F32)
    for k in range(pack_ref.shape[0]):
        held[k * SUB : k * SUB + 4] = pack_ref[k]
    pack = held[...]
    gram4 = tn(pack, pack)
    gram = sum(gram4[b * rank : (b + 1) * rank, b * rank : (b + 1) * rank] for b in range(4))
    gram_ref[...] = gram
    row, lane = iota((rank, LANES), 0), iota((rank, LANES), 1)
    work = jnp.concatenate([gram, jnp.zeros((rank, LANES - rank), F32)], 1)
    work = jnp.where(lane == row + rank, 1.0, work)
    for first in range(0, rank, 4):
        columns = [jnp.broadcast_to(work[:, first + m : first + m + 1], work.shape) for m in range(4)]
        for m in range(4):
            j = first + m
            factor = jnp.where(row > j, columns[m] * (1.0 / columns[m][j : j + 1, :]), 0.0)
            work -= factor * work[j : j + 1, :]
            for n in range(m + 1, 4):
                columns[n] -= factor * columns[n][j : j + 1, :]
    diagonal = jnp.sum(jnp.where(lane == row, work, 0.0), 1, keepdims=True)
    inverse = (work * lax.rsqrt(diagonal))[:, rank : 2 * rank]
    inverse_ref[...] = inverse
    inverse16 = jnp.concatenate([inverse] * 4, 0)
    inverse16 = jnp.concatenate([inverse16] * 4, 1)
    total = total_ref[...]
    product = jnp.zeros((own, LANES), F32)
    for b in range(4):
        part = dot(total[:, b * span : (b + 1) * span], pack)
        product = jnp.where(iota(part.shape, 1) // rank == b, part, product)
    q4 = nt(product, inverse16) / n_r
    q_pack = fold_rows(q4, group)[:group]
    send_ref[...] = jnp.broadcast_to(q_pack[None], send_ref.shape)


def place_blocks(near_core, blocks_ref, basis_ref, e_ref, g_ref, q_hbm, error_hbm, q, error, sems, approx_ref, gram):
    n_z = blocks_ref.shape[0]
    rows = e_ref.shape[0]
    rank = q.shape[1]
    square = (LANES, LANES)
    basis4 = basis_ref[...]
    stack = jnp.concatenate(
        [(iota(square, 0) == iota(square, 1)).astype(F32)]
        + [jnp.where(iota(basis4.shape, 1) // rank == b, basis4, 0.0) for b in range(4)],
        0,
    )
    copies = []
    blocks = blocks_ref[...].reshape(n_z * LANES, LANES)
    every = nt(stack, blocks)
    for z in range(n_z):
        both = every[:, z * LANES : (z + 1) * LANES]
        start = pl.multiple_of((2 * z + near_core) * 4 * LANES, 4 * LANES)
        for b in range(4):
            near = both[LANES + b * rows : LANES + (b + 1) * rows]
            at = pl.ds(pl.multiple_of(start + b * LANES, LANES), LANES)
            to = slice(b * LANES, (b + 1) * LANES)
            q[z, :, to] = both[b * rank : (b + 1) * rank]
            approx_ref[z, :, to] = near
            error[z, :, to] = e_ref[:, at] + g_ref[:, at] - near
        span = pl.ds(start, 4 * LANES)
        copies.append(pltpu.make_async_copy(q.at[z], q_hbm.at[:, span], sems.at[0, z]))
        copies.append(pltpu.make_async_copy(error.at[z], error_hbm.at[:, span], sems.at[1, z]))
        copies[-2].start()
        copies[-1].start()
    return gram + tn(blocks, blocks), copies


def near_kernel(core_ref, mine_ref, basis_ref, e_ref, g_ref, q_hbm, error_hbm, approx_ref, gram_ref, q, error, sems):
    gram, copies = place_blocks(
        core_ref[0], mine_ref, basis_ref, e_ref, g_ref, q_hbm, error_hbm, q, error, sems, approx_ref,
        jnp.zeros((LANES, LANES), F32),
    )
    gram_ref[...] = gram
    for copy in copies:
        copy.wait()


def far_kernel(limit, core_ref, other_ref, basis_ref, e_ref, g_ref, gram_ref, approx_ref, weigh_ref, m_ref, q_old, error_old, q_hbm, error_hbm, momentum_ref, q, error, sems, far):
    core = core_ref[0]
    gram, copies = place_blocks(
        1 - core, other_ref, basis_ref, e_ref, g_ref, q_hbm, error_hbm, q, error, sems, far, gram_ref[...]
    )
    total = jnp.sum(gram * weigh_ref[...], keepdims=True)
    scale = jnp.minimum(1.0, limit / jnp.sqrt(total))
    for z in range(other_ref.shape[0]):
        for ref, c in ((approx_ref, core), (far, 1 - core)):
            at = pl.ds(pl.multiple_of((2 * z + c) * 4 * LANES, 4 * LANES), 4 * LANES)
            momentum_ref[:, at] = BETA * m_ref[:, at] + scale * ref[z]
    for copy in copies:
        copy.wait()


def body(tokens_x, cotangent, weight, error_fb, momentum, q_prev):
    n_t, n_r, n_z = lax.axis_size(T), lax.axis_size(R), lax.axis_size("z")
    t = lax.axis_index(T)[None]
    core = lax.axis_index("core")[None]
    tokens, wide = tokens_x.shape
    rows, width = weight.shape
    rank = q_prev.shape[0]
    ff_win = rows * n_t
    own = wide // n_r
    group = own // 4
    halves, _ = lane_halves(ff_win)
    error = error_fb[0]

    (first,) = call(
        first_kernel,
        [((n_t, rows, wide + tokens + rank // rows * tokens), F32)],
        [SMEM] + [HBM] * 4,
        moved=3 * 2**20,
        limit=None,
        scratch_shapes=[
            pltpu.VMEM(tokens_x.shape, BF16),
            pltpu.VMEM(cotangent.shape, BF16),
            pltpu.VMEM((rank, wide), F32),
            pltpu.SemaphoreType.DMA((3 + n_t,)),
        ],
    )(t, tokens_x, cotangent, error, q_prev)
    w_parts = weight.reshape(rows, n_t, wide).transpose(1, 0, 2)
    first, error_late = lax.optimization_barrier((first, error))
    (p_error,) = call(
        project_kernel, [((rows, rank), F32)], [VMEM] * 2, flops=2**27, moved=2 * 2**20
    )(error_late, q_prev)
    first = exchange(first, T)

    bulk = jnp.concatenate([tokens_x, w_parts.reshape(rows * n_t, wide)], 0)
    first, bulk, p_error = lax.optimization_barrier((first, bulk, p_error))
    bulk = lax.all_gather(bulk, T)
    second, cot_all = call(
        merge_kernel,
        [((n_r, halves * own // 4 + 1, 4, LANES), F32), ((ff_win, tokens), BF16)],
        [VMEM] * 4,
        moved=2 * 2**20,
        scratch_shapes=[pltpu.VMEM((wide, ff_win), F32)],
    )(first, tokens_x, cotangent, p_error)
    second = exchange(second, R)
    total_t, p_pack = call(
        functools.partial(sum_kernel, n_t),
        [((own, 2 * ff_win), F32), ((n_t, 4, LANES), F32)],
        [VMEM],
        moved=2**20,
        scratch_shapes=[pltpu.VMEM((halves, own, LANES), F32)],
    )(second)
    p_all = exchange(p_pack, T)

    q_send, gram, inverse = call(
        functools.partial(factor_kernel, n_r),
        [((n_r * n_z, group, LANES), F32), ((rank, rank), F32), ((rank, rank), F32)],
        [VMEM] * 2,
        flops=2**29,
        moved=2**20,
        scratch_shapes=[pltpu.VMEM((n_t * SUB, LANES), F32)],
    )(p_all, total_t)
    mine = exchange(q_send, CHIPS)
    grad_rows, input_grad = call(
        rows_kernel,
        [((rows, width), F32), ((tokens, wide), BF16)],
        [SMEM] + [VMEM] * 3,
        flops=2**28,
        moved=8 * 2**20,
        scratch_shapes=[pltpu.VMEM((ff_win, wide), BF16)],
    )(t, cotangent, cot_all, bulk)
    mine, grad_rows = lax.optimization_barrier((mine, grad_rows))
    basis_gram = dot(dot(inverse, gram), inverse.T)
    p_rows = p_pack[0].reshape(4, 4, rank).transpose(1, 0, 2).reshape(rows, rank)
    basis4 = jnp.tile(dot(p_rows, inverse.T), (1, 4))
    square = (LANES, LANES)
    weigh = jnp.where(
        iota(square, 0) // rank == iota(square, 1) // rank, jnp.tile(basis_gram, (4, 4)), 0.0
    )
    other = lax.ppermute(mine, "core", [(0, 1), (1, 0)])
    blocks = (n_z, LANES, LANES)
    limit = CLIPPING * math.sqrt(ff_win * width)
    scratch = [
        pltpu.VMEM((n_z, rank, wide), F32),
        pltpu.VMEM((n_z, rows, wide), F32),
        pltpu.SemaphoreType.DMA((2, n_z)),
    ]
    whole = [((rank, width), F32), ((rows, width), F32)]
    q_new, error_new, approx, q_gram = call(
        near_kernel,
        [*whole, ((n_z, rows, wide), F32), ((LANES, LANES), F32)],
        [SMEM] + [VMEM] * 4,
        [HBM, HBM, VMEM, VMEM],
        flops=2**30,
        moved=3 * 2**20,
        scratch_shapes=scratch,
    )(core, mine.reshape(blocks), basis4, error, grad_rows)
    q_new, error_new, momentum_new = call(
        functools.partial(far_kernel, limit),
        [*whole, ((rows, width), F32)],
        [SMEM] + [VMEM] * 8 + [HBM, HBM],
        [HBM, HBM, VMEM],
        flops=2**30,
        moved=4 * 2**20,
        scratch_shapes=[*scratch, pltpu.VMEM((n_z, rows, wide), F32)],
        input_output_aliases={9: 0, 10: 1},
    )(core, other.reshape(blocks), basis4, error, grad_rows, q_gram, approx, weigh, momentum, q_new, error_new)
    return (input_grad, error_new[None], momentum_new, q_new)


def solution(mesh):
    n_r, n_t = mesh.devices.shape
    x = 4 if n_r > 4 else 2
    split = Mesh(mesh.devices.reshape(n_r // x, x, n_t // 2, 2), (*R, *T))
    placed = (P(R, T), P(T, R), P(T, None), P(R, T, None), P(T, None), P())
    return jax.shard_map(
        body,
        mesh=split,
        in_specs=placed,
        out_specs=(P(R, T), P(R, T, None), P(T, None), P()),
        check_vma=False,
    )
```

```python
import functools
import math

import jax
import jax.numpy as jnp
from jax import lax
from jax.experimental import pallas as pl
from jax.experimental.pallas import tpu as pltpu
from jax.sharding import Mesh, PartitionSpec as P

CLIPPING = 0.2
BETA = 0.9
HIGHEST = lax.Precision.HIGHEST
LANES = 128
SUB = 8
F32 = jnp.float32
BF16 = jnp.bfloat16

T = ("z", "core")
R = ("y", "x")
CHIPS = ("z", "y", "x")

VMEM = pl.BlockSpec(memory_space=pltpu.VMEM)
SMEM = pl.BlockSpec(memory_space=pltpu.SMEM)
HBM = pl.BlockSpec(memory_space=pltpu.HBM)


def exchange(parts, axes):
    return lax.all_to_all(parts, axes, 0, 0, tiled=True)


def call(kernel, outs, in_specs=None, out_specs=None, flops=0, moved=0, limit=48, **more):
    outs = [jax.ShapeDtypeStruct(*o) for o in outs]
    return functools.partial(
        pl.pallas_call,
        kernel,
        out_shape=outs,
        out_specs=out_specs or [VMEM] * len(outs),
        cost_estimate=pl.CostEstimate(flops=flops, bytes_accessed=moved, transcendentals=0),
        compiler_params=pltpu.CompilerParams(vmem_limit_bytes=limit and limit * 2**20),
        **more,
    )(in_specs=in_specs)


def iota(shape, axis):
    return lax.broadcasted_iota(jnp.int32, shape, axis)


def nt(a, b, precision=HIGHEST):
    return lax.dot_general(a, b, (((1,), (1,)), ((), ())), precision=precision, preferred_element_type=F32)


def tn(a, b, precision=HIGHEST):
    return lax.dot_general(a, b, (((0,), (0,)), ((), ())), precision=precision, preferred_element_type=F32)


def dot(a, b, precision=HIGHEST):
    return jnp.dot(a, b, precision=precision, preferred_element_type=F32)


def lane_halves(ff_win):
    halves = max(ff_win // LANES, 1)
    return halves, ff_win // halves


def fold_rows(tiled, group):
    n = tiled.shape[0]
    kept = jnp.where(iota(tiled.shape, 0) // group == iota(tiled.shape, 1) // 32, tiled, 0.0)
    out = max(group, SUB)
    pick = (iota((out, n), 1) % group == iota((out, n), 0)).astype(F32)
    return dot(pick, kept)


def fetch(pairs, sems):
    copies = [pltpu.make_async_copy(src, dst, sems.at[i]) for i, (src, dst) in enumerate(pairs)]
    for copy in copies:
        copy.start()
    return copies


def first_kernel(t_ref, x_ref, c_ref, q_ref, send_ref, x, c, q, sems):
    n_t, rows, _ = send_ref.shape
    tokens, wide = x_ref.shape
    start = pl.multiple_of(t_ref[0] * wide, wide)
    for copy in fetch([(q_ref.at[:, pl.ds(start, wide)], q), (x_ref, x), (c_ref, c)], sems):
        copy.wait()
    y = nt(q[...], x[...].astype(F32))
    cot = c[...].astype(F32)
    for k in range(n_t):
        send_ref[k, :, :tokens] = cot
        for g in range(y.shape[0] // rows):
            at = tokens + g * tokens
            send_ref[k, :, at : at + tokens] = y[g * rows : (g + 1) * rows]


def tiles_kernel(x_ref, e_ref, *refs):
    outs, e, sem = refs[:-2], refs[-2], refs[-1]
    n_t = outs[0].shape[0]
    copy = pltpu.make_async_copy(e_ref, e, sem)
    copy.start()
    copy.wait()
    for d, out in enumerate(outs):
        b = lax.rem(x_ref[0] + d, 4)
        for k in range(n_t):
            out[k] = e[:, pl.ds(pl.multiple_of((4 * k + b) * LANES, LANES), LANES)]


def project_kernel(group, x_ref, e_ref, q_ref, xt_ref, pe_ref, x, e, q, sems):
    copies = fetch([(x_ref, x), (e_ref, e), (q_ref, q)], sems)
    wide = x_ref.shape[1]
    own = 4 * group
    out, col = iota((wide, wide), 0), iota((wide, wide), 1)
    r, b, a = out // own, out % own // group, out % group
    turn = (col == b * LANES + r * group + a).astype(BF16)
    copies[0].wait()
    xt_ref[...] = nt(turn, x[...], None).astype(BF16)
    copies[1].wait()
    copies[2].wait()
    pe_ref[...] = nt(e[...], q[...])


def turn_kernel(a_ref, b_ref, c_ref, d_ref, x_ref, p_ref, out_ref, xt_ref, pe_ref):
    xt_ref[...] = x_ref[...]
    pe_ref[...] = p_ref[...]
    rest = (a_ref[...] + b_ref[...]) + (c_ref[...] + d_ref[...])
    rest = rest.reshape(out_ref.shape[1], LANES)
    same = (iota((LANES, LANES), 0) == iota((LANES, LANES), 1)).astype(BF16)
    turned = jnp.zeros(out_ref.shape, F32)
    for _ in range(3):
        piece = rest.astype(BF16)
        turned += nt(same, piece, None)
        rest -= piece.astype(F32)
    out_ref[...] = turned


def pack_kernel(x_ref, w_ref, out_ref, sems):
    tokens, wide = x_ref.shape
    rows = w_ref.shape[0]
    pairs = [(x_ref, out_ref.at[pl.ds(0, tokens)])]
    for k in range(w_ref.shape[1] // wide):
        pairs.append((w_ref.at[:, pl.ds(k * wide, wide)], out_ref.at[pl.ds(tokens + k * rows, rows)]))
    for copy in fetch(pairs, sems):
        copy.wait()


def merge_kernel(t_ref, got_ref, xt_ref, pe_ref, et_ref, send_ref, cot_ref, turned_ref):
    n_t, rows, _ = got_ref.shape
    wide, tokens = xt_ref.shape
    n_r = send_ref.shape[0]
    group = LANES // n_r
    ff_win = n_t * rows
    cot = got_ref[:, :, :tokens].reshape(ff_win, tokens).astype(BF16)
    cot_ref[...] = cot
    y = jnp.sum(got_ref[:, :, tokens:], 0)
    folds = y.shape[1] // tokens
    y = jnp.concatenate([y[:, g * tokens : (g + 1) * tokens] for g in range(folds)], 0)
    rank = y.shape[0]
    y4 = jnp.concatenate([y] * (LANES // rank), 0)
    tile = (iota((rank, LANES), 1) % rank == iota((rank, LANES), 0)).astype(F32)
    p4 = nt(got_ref[t_ref[0], :, :tokens], y4) + dot(pe_ref[...], tile)
    p_pack = fold_rows(p4, rows // 4)

    own = wide // n_r
    turned_ref[...] = nt(xt_ref[...], cot, None)
    halves, width = lane_halves(ff_win)
    at = halves * (own // 4)
    for k in range(n_r):
        for h in range(halves):
            lanes = slice(h * width, (h + 1) * width)
            for g in range(own // 4):
                row = k * own + 4 * g
                send_ref[k, h * (own // 4) + g, :, :width] = turned_ref[row : row + 4, lanes]
            for g in range(group // 4):
                row = k * group + 4 * g
                send_ref[k, at + 1 + h * (group // 4) + g, :, :width] = et_ref[row : row + 4, lanes]
        send_ref[k, at] = p_pack[:4]


def rows_kernel(t_ref, c_ref, cot_ref, got_ref, g_ref, dx_ref, w):
    n_t = got_ref.shape[0]
    rows, tokens = c_ref.shape
    wide = got_ref.shape[2]
    at = pl.ds(pl.multiple_of(tokens + t_ref[0] * rows, rows), rows)
    for k in range(n_t):
        g_ref[:, k * wide : (k + 1) * wide] = dot(c_ref[...], got_ref[k, :tokens, :], None)
        w[k * rows : (k + 1) * rows] = got_ref[k, at, :]
    dx_ref[...] = tn(cot_ref[...], w[...], None).astype(BF16)


def sum_kernel(got_ref, total_ref, send_ref, scratch, error):
    n_r = got_ref.shape[0]
    n_t = send_ref.shape[0]
    own, long = total_ref.shape
    ff_win = long // 2
    rows = ff_win // n_t
    group = own // 4
    halves, width = lane_halves(ff_win)
    at = halves * (own // 4)
    got = jnp.sum(got_ref[:, : at + 1], 0)
    p_pack = got[at]
    total = jnp.zeros(total_ref.shape, F32)
    for h in range(halves):
        for g in range(own // 4):
            scratch[h, 4 * g : 4 * g + 4, :] = got[h * (own // 4) + g]
        unit, lane = iota((width, long), 0) + h * width, iota((width, long), 1)
        t, b, a = unit // rows, unit % rows // 4, unit % 4
        move = (lane == b * (SUB * n_t) + t * SUB + a).astype(F32)
        total += dot(scratch[h, :, :width], move)
    total_ref[...] = total

    p8 = jnp.concatenate([p_pack, jnp.zeros_like(p_pack)], 0)
    spread = (iota((rows, SUB), 0) % 4 == iota((rows, SUB), 1)).astype(F32)
    p16 = dot(spread, p8)
    p16 = jnp.where(iota(p16.shape, 0) // 4 == iota(p16.shape, 1) // 32, p16, 0.0)
    square = (LANES, LANES)
    p16 = dot(p16, (iota(square, 0) % 32 == iota(square, 1) % 32).astype(F32))
    p_all = jnp.concatenate([p16] * n_t, 0)
    for b in range(4):
        part = sum(got_ref[r, at + 1 :] for r in range(b, n_r, 4))
        for h in range(halves):
            for g in range(group // 4):
                row = b * group + 4 * g
                error[row : row + 4, h * width : (h + 1) * width] = part[h * (group // 4) + g][:, :width]
    pieces = []
    for q in range(n_t // 4):
        mask = iota(p_all.shape, 0) // rows == 4 * q + iota(p_all.shape, 1) // 32
        out = dot(error[...], jnp.where(mask, p_all, 0.0))
        rolled = [out] + [pltpu.roll(out, 32 * d, 1) for d in range(1, 4)]
        row, lane = iota(out.shape, 0) // group, iota(out.shape, 1) // 32
        for s in range(4):
            kept = jnp.zeros(out.shape, F32)
            for b in range(4):
                kept = jnp.where((row == b) & (lane == b), rolled[(b - s) % 4], kept)
            pieces.append(kept)
    every = jnp.concatenate(pieces, 0)
    tall = max(group, SUB)
    pick_row, pick_col = iota((n_t * tall, n_t * own), 0), iota((n_t * tall, n_t * own), 1)
    pick = (pick_row // tall == pick_col // own) & (pick_row % tall == pick_col % group)
    folded = dot(pick.astype(F32), every)
    for k in range(n_t):
        send_ref[k, 0] = p_pack
        for g in range(group // 4):
            send_ref[k, 1 + g] = folded[k * tall + 4 * g : k * tall + 4 * g + 4]


def factor_kernel(n_r, pack_ref, total_ref, send_ref, gram_ref, inverse_ref, held, wide):
    wide[...] = jnp.zeros(wide.shape, F32)
    span = held.shape[0]
    own = total_ref.shape[0]
    rank = gram_ref.shape[0]
    group = own // 4
    held[...] = jnp.zeros(held.shape, F32)
    for k in range(pack_ref.shape[0]):
        held[k * SUB : k * SUB + 4] = pack_ref[k, 0]
    pack = held[...]
    gram4 = tn(pack, pack)
    gram = sum(gram4[b * rank : (b + 1) * rank, b * rank : (b + 1) * rank] for b in range(4))
    gram_ref[...] = gram
    row, lane = iota((rank, LANES), 0), iota((rank, LANES), 1)
    work = jnp.concatenate([gram, jnp.zeros((rank, LANES - rank), F32)], 1)
    work = jnp.where(lane == row + rank, 1.0, work)
    for first in range(0, rank, 4):
        columns = [jnp.broadcast_to(work[:, first + m : first + m + 1], work.shape) for m in range(4)]
        for m in range(4):
            j = first + m
            factor = jnp.where(row > j, columns[m] * (1.0 / columns[m][j : j + 1, :]), 0.0)
            work -= factor * work[j : j + 1, :]
            for n in range(m + 1, 4):
                columns[n] -= factor * columns[n][j : j + 1, :]
    diagonal = jnp.sum(jnp.where(lane == row, work, 0.0), 1, keepdims=True)
    inverse = (work * lax.rsqrt(diagonal))[:, rank : 2 * rank]
    inverse_ref[...] = inverse
    inverse16 = jnp.concatenate([inverse] * 4, 0)
    inverse16 = jnp.concatenate([inverse16] * 4, 1)
    total = total_ref[...]
    product = jnp.zeros((own, LANES), F32)
    for b in range(4):
        part = dot(total[:, b * span : (b + 1) * span], pack)
        product = jnp.where(iota(part.shape, 1) // rank == b, part, product)
    from_error = jnp.sum(pack_ref[:, 1:], 0)
    for g in range(group // 4):
        wide[4 * g : 4 * g + 4] = from_error[g]
    tall = wide.shape[0]
    spread = (iota((own, tall), 0) % group == iota((own, tall), 1)).astype(F32)
    from_error = dot(spread, wide[...])
    product += jnp.where(iota(product.shape, 0) // group == iota(product.shape, 1) // rank, from_error, 0.0)
    q4 = nt(product, inverse16) / n_r
    q_pack = fold_rows(q4, group)[:group]
    send_ref[...] = jnp.broadcast_to(q_pack[None], send_ref.shape)


def place_blocks(near_core, blocks_ref, basis_ref, e_ref, g_ref, q_hbm, error_hbm, q, error, sems, approx_ref, gram):
    n_z = blocks_ref.shape[0]
    rows = e_ref.shape[0]
    rank = q.shape[1]
    square = (LANES, LANES)
    basis4 = basis_ref[...]
    stack = jnp.concatenate(
        [(iota(square, 0) == iota(square, 1)).astype(F32)]
        + [jnp.where(iota(basis4.shape, 1) // rank == b, basis4, 0.0) for b in range(4)],
        0,
    )
    copies = []
    blocks = blocks_ref[...].reshape(n_z * LANES, LANES)
    every = nt(stack, blocks)
    for z in range(n_z):
        both = every[:, z * LANES : (z + 1) * LANES]
        start = pl.multiple_of((2 * z + near_core) * 4 * LANES, 4 * LANES)
        for b in range(4):
            near = both[LANES + b * rows : LANES + (b + 1) * rows]
            at = pl.ds(pl.multiple_of(start + b * LANES, LANES), LANES)
            to = slice(b * LANES, (b + 1) * LANES)
            q[z, :, to] = both[b * rank : (b + 1) * rank]
            approx_ref[z, :, to] = near
            error[z, :, to] = e_ref[:, at] + g_ref[:, at] - near
        span = pl.ds(start, 4 * LANES)
        copies.append(pltpu.make_async_copy(q.at[z], q_hbm.at[:, span], sems.at[0, z]))
        copies.append(pltpu.make_async_copy(error.at[z], error_hbm.at[:, span], sems.at[1, z]))
        copies[-2].start()
        copies[-1].start()
    return gram + tn(blocks, blocks), copies


def near_kernel(core_ref, mine_ref, basis_ref, e_ref, g_ref, q_hbm, error_hbm, approx_ref, gram_ref, q, error, sems):
    gram, copies = place_blocks(
        core_ref[0], mine_ref, basis_ref, e_ref, g_ref, q_hbm, error_hbm, q, error, sems, approx_ref,
        jnp.zeros((LANES, LANES), F32),
    )
    gram_ref[...] = gram
    for copy in copies:
        copy.wait()


def far_kernel(limit, core_ref, other_ref, basis_ref, e_ref, g_ref, gram_ref, approx_ref, weigh_ref, m_ref, q_old, error_old, q_hbm, error_hbm, momentum_ref, q, error, sems, far):
    core = core_ref[0]
    gram, copies = place_blocks(
        1 - core, other_ref, basis_ref, e_ref, g_ref, q_hbm, error_hbm, q, error, sems, far, gram_ref[...]
    )
    total = jnp.sum(gram * weigh_ref[...], keepdims=True)
    scale = jnp.minimum(1.0, limit / jnp.sqrt(total))
    for z in range(other_ref.shape[0]):
        for ref, c in ((approx_ref, core), (far, 1 - core)):
            at = pl.ds(pl.multiple_of((2 * z + c) * 4 * LANES, 4 * LANES), 4 * LANES)
            momentum_ref[:, at] = BETA * m_ref[:, at] + scale * ref[z]
    for copy in copies:
        copy.wait()


def body(tokens_x, cotangent, weight, error_fb, momentum, q_prev):
    n_t, n_r, n_z = lax.axis_size(T), lax.axis_size(R), lax.axis_size("z")
    t = lax.axis_index(T)[None]
    core = lax.axis_index("core")[None]
    tokens, wide = tokens_x.shape
    rows, width = weight.shape
    rank = q_prev.shape[0]
    ff_win = rows * n_t
    own = wide // n_r
    group = own // 4
    halves, _ = lane_halves(ff_win)
    error = error_fb[0]

    (first,) = call(
        first_kernel,
        [((n_t, rows, tokens + rank // rows * tokens), F32)],
        [SMEM] + [HBM] * 3,
        moved=2**20,
        limit=None,
        scratch_shapes=[
            pltpu.VMEM(tokens_x.shape, BF16),
            pltpu.VMEM(cotangent.shape, BF16),
            pltpu.VMEM((rank, wide), F32),
            pltpu.SemaphoreType.DMA((3,)),
        ],
    )(t, tokens_x, cotangent, q_prev)
    first, error_late, x_late = lax.optimization_barrier((first, error, tokens_x))
    tiles = call(
        tiles_kernel,
        [((n_t, rows, LANES), F32)] * 4,
        [SMEM, HBM],
        moved=2**20,
        limit=None,
        scratch_shapes=[pltpu.VMEM(error.shape, F32), pltpu.SemaphoreType.DMA(())],
    )(lax.axis_index("x")[None], error_late)
    tiles = [tiles[0]] + [
        lax.ppermute(tiles[d], "x", [(i, (i + d) % 4) for i in range(4)]) for d in range(1, 4)
    ]
    x_t, p_error = call(
        functools.partial(project_kernel, group),
        [((wide, tokens), BF16), ((rows, rank), F32)],
        [HBM] * 3,
        flops=2**27,
        moved=2 * 2**20,
        limit=None,
        scratch_shapes=[
            pltpu.VMEM(tokens_x.shape, BF16),
            pltpu.VMEM(error.shape, F32),
            pltpu.VMEM(q_prev.shape, F32),
            pltpu.SemaphoreType.DMA((3,)),
        ],
    )(x_late, error_late, q_prev)
    error_t, x_t, p_error = call(
        turn_kernel,
        [((LANES, ff_win), F32), ((wide, tokens), BF16), ((rows, rank), F32)],
        [VMEM] * 6,
        moved=2**20,
    )(*tiles, x_t, p_error)
    (bulk,) = call(
        pack_kernel,
        [((tokens + rows * n_t, wide), BF16)],
        [HBM] * 2,
        [HBM],
        moved=2**20,
        limit=None,
        scratch_shapes=[pltpu.SemaphoreType.DMA((1 + n_t,))],
    )(x_late, weight)
    first = exchange(first, T)
    first, error_t, x_t, p_error, bulk = lax.optimization_barrier((first, error_t, x_t, p_error, bulk))
    bulk = lax.all_gather(bulk, T)
    blocks_g, blocks_e = halves * own // 4, halves * group // 4
    second, cot_all = call(
        merge_kernel,
        [((n_r, blocks_g + 1 + blocks_e, 4, LANES), F32), ((ff_win, tokens), BF16)],
        [SMEM] + [VMEM] * 4,
        moved=2 * 2**20,
        scratch_shapes=[pltpu.VMEM((wide, ff_win), F32)],
    )(t, first, x_t, p_error, error_t)
    second = exchange(second, R)
    total_t, third = call(
        sum_kernel,
        [((own, 2 * ff_win), F32), ((n_t, 1 + group // 4, 4, LANES), F32)],
        [VMEM],
        moved=2**20,
        scratch_shapes=[pltpu.VMEM((halves, own, LANES), F32), pltpu.VMEM((own, ff_win), F32)],
    )(second)
    p_pack = third[0, 0]
    third = exchange(third, T)

    q_send, gram, inverse = call(
        functools.partial(factor_kernel, n_r),
        [((n_r * n_z, group, LANES), F32), ((rank, rank), F32), ((rank, rank), F32)],
        [VMEM] * 2,
        flops=2**29,
        moved=2**20,
        scratch_shapes=[pltpu.VMEM((n_t * SUB, LANES), F32), pltpu.VMEM((max(group, SUB), LANES), F32)],
    )(third, total_t)
    mine = exchange(q_send, CHIPS)
    grad_rows, input_grad = call(
        rows_kernel,
        [((rows, width), F32), ((tokens, wide), BF16)],
        [SMEM] + [VMEM] * 3,
        flops=2**28,
        moved=8 * 2**20,
        scratch_shapes=[pltpu.VMEM((ff_win, wide), BF16)],
    )(t, cotangent, cot_all, bulk)
    basis_gram = dot(dot(inverse, gram), inverse.T)
    p_rows = p_pack.reshape(4, 4, rank).transpose(1, 0, 2).reshape(rows, rank)
    basis4 = jnp.tile(dot(p_rows, inverse.T), (1, 4))
    square = (LANES, LANES)
    weigh = jnp.where(
        iota(square, 0) // rank == iota(square, 1) // rank, jnp.tile(basis_gram, (4, 4)), 0.0
    )
    mine, grad_rows, weigh, basis4 = lax.optimization_barrier((mine, grad_rows, weigh, basis4))
    other = lax.ppermute(mine, "core", [(0, 1), (1, 0)])
    blocks = (n_z, LANES, LANES)
    limit = CLIPPING * math.sqrt(ff_win * width)
    scratch = [
        pltpu.VMEM((n_z, rank, wide), F32),
        pltpu.VMEM((n_z, rows, wide), F32),
        pltpu.SemaphoreType.DMA((2, n_z)),
    ]
    whole = [((rank, width), F32), ((rows, width), F32)]
    q_new, error_new, approx, q_gram = call(
        near_kernel,
        [*whole, ((n_z, rows, wide), F32), ((LANES, LANES), F32)],
        [SMEM] + [VMEM] * 4,
        [HBM, HBM, VMEM, VMEM],
        flops=2**30,
        moved=3 * 2**20,
        scratch_shapes=scratch,
    )(core, mine.reshape(blocks), basis4, error, grad_rows)
    q_new, error_new, momentum_new = call(
        functools.partial(far_kernel, limit),
        [*whole, ((rows, width), F32)],
        [SMEM] + [VMEM] * 8 + [HBM, HBM],
        [HBM, HBM, VMEM],
        flops=2**30,
        moved=4 * 2**20,
        scratch_shapes=[*scratch, pltpu.VMEM((n_z, rows, wide), F32)],
        input_output_aliases={9: 0, 10: 1},
    )(core, other.reshape(blocks), basis4, error, grad_rows, q_gram, approx, weigh, momentum, q_new, error_new)
    return (input_grad, error_new[None], momentum_new, q_new)


def solution(mesh):
    n_r, n_t = mesh.devices.shape
    x = 4
    split = Mesh(mesh.devices.reshape(n_r // x, x, n_t // 2, 2), (*R, *T))
    placed = (P(R, T), P(T, R), P(T, None), P(R, T, None), P(T, None), P())
    return jax.shard_map(
        body,
        mesh=split,
        in_specs=placed,
        out_specs=(P(R, T), P(R, T, None), P(T, None), P()),
        check_vma=False,
    )
```

```python
import functools
import math

import jax
import jax.numpy as jnp
from jax import lax
from jax.experimental import pallas as pl
from jax.experimental.pallas import tpu as pltpu
from jax.sharding import Mesh, PartitionSpec as P

CLIPPING = 0.2
BETA = 0.9
HIGHEST = lax.Precision.HIGHEST
LANES = 128
SUB = 8
F32 = jnp.float32
BF16 = jnp.bfloat16

T = ("z", "core")
R = ("y", "x")
CHIPS = ("z", "y", "x")

VMEM = pl.BlockSpec(memory_space=pltpu.VMEM)
SMEM = pl.BlockSpec(memory_space=pltpu.SMEM)
HBM = pl.BlockSpec(memory_space=pltpu.HBM)


def exchange(parts, axes):
    return lax.all_to_all(parts, axes, 0, 0, tiled=True)


def call(kernel, outs, in_specs=None, out_specs=None, flops=0, moved=0, limit=48, **more):
    outs = [jax.ShapeDtypeStruct(*o) for o in outs]
    return functools.partial(
        pl.pallas_call,
        kernel,
        out_shape=outs,
        out_specs=out_specs or [VMEM] * len(outs),
        cost_estimate=pl.CostEstimate(flops=flops, bytes_accessed=moved, transcendentals=0),
        compiler_params=pltpu.CompilerParams(vmem_limit_bytes=limit and limit * 2**20),
        **more,
    )(in_specs=in_specs)


def iota(shape, axis):
    return lax.broadcasted_iota(jnp.int32, shape, axis)


def nt(a, b, precision=HIGHEST):
    return lax.dot_general(a, b, (((1,), (1,)), ((), ())), precision=precision, preferred_element_type=F32)


def tn(a, b, precision=HIGHEST):
    return lax.dot_general(a, b, (((0,), (0,)), ((), ())), precision=precision, preferred_element_type=F32)


def dot(a, b, precision=HIGHEST):
    return jnp.dot(a, b, precision=precision, preferred_element_type=F32)


def lane_halves(ff_win):
    halves = max(ff_win // LANES, 1)
    return halves, ff_win // halves


def fold_rows(tiled, group):
    n = tiled.shape[0]
    kept = jnp.where(iota(tiled.shape, 0) // group == iota(tiled.shape, 1) // 32, tiled, 0.0)
    out = max(group, SUB)
    pick = (iota((out, n), 1) % group == iota((out, n), 0)).astype(F32)
    return dot(pick, kept)


def fetch(pairs, sems):
    copies = [pltpu.make_async_copy(src, dst, sems.at[i]) for i, (src, dst) in enumerate(pairs)]
    for copy in copies:
        copy.start()
    return copies


def first_kernel(t_ref, x_ref, c_ref, q_ref, send_ref, x, c, q, sems):
    n_t, rows, _ = send_ref.shape
    tokens, wide = x_ref.shape
    start = pl.multiple_of(t_ref[0] * wide, wide)
    for copy in fetch([(q_ref.at[:, pl.ds(start, wide)], q), (x_ref, x), (c_ref, c)], sems):
        copy.wait()
    y = nt(q[...], x[...].astype(F32))
    cot = c[...].astype(F32)
    for k in range(n_t):
        send_ref[k, :, :tokens] = cot
        for g in range(y.shape[0] // rows):
            at = tokens + g * tokens
            send_ref[k, :, at : at + tokens] = y[g * rows : (g + 1) * rows]


def tiles_kernel(x_ref, e_ref, q_ref, *refs):
    outs, pe_ref, (e, q, sems) = refs[:4], refs[4], refs[5:]
    n_t = outs[0].shape[0]
    copies = fetch([(e_ref, e), (q_ref, q)], sems)
    copies[0].wait()
    for d, out in enumerate(outs):
        b = lax.rem(x_ref[0] + d, 4)
        for k in range(n_t):
            out[k] = e[:, pl.ds(pl.multiple_of((4 * k + b) * LANES, LANES), LANES)]
    copies[1].wait()
    pe_ref[...] = nt(e[...], q[...])


def pack_kernel(x_ref, w_ref, out_ref):
    tokens, wide = x_ref.shape
    rows = w_ref.shape[0]
    out_ref[:tokens] = x_ref[...]
    for k in range(w_ref.shape[1] // wide):
        out_ref[tokens + k * rows : tokens + (k + 1) * rows] = w_ref[:, k * wide : (k + 1) * wide]


def turn_kernel(a_ref, b_ref, c_ref, d_ref, p_ref, x_ref, out_ref, pe_ref, near_ref):
    pe_ref[...] = p_ref[...]
    near_ref[...] = x_ref[...]
    rest = (a_ref[...] + b_ref[...]) + (c_ref[...] + d_ref[...])
    rest = rest.reshape(out_ref.shape[1], LANES)
    same = (iota((LANES, LANES), 0) == iota((LANES, LANES), 1)).astype(BF16)
    turned = jnp.zeros(out_ref.shape, F32)
    for _ in range(3):
        piece = rest.astype(BF16)
        turned += nt(same, piece, None)
        rest -= piece.astype(F32)
    out_ref[...] = turned


def merge_kernel(t_ref, got_ref, x_ref, pe_ref, et_ref, send_ref, cot_ref, turned_ref):
    n_t, rows, _ = got_ref.shape
    tokens, wide = x_ref.shape
    n_r = send_ref.shape[0]
    group = LANES // n_r
    ff_win = n_t * rows
    cot = got_ref[:, :, :tokens].reshape(ff_win, tokens).astype(BF16)
    cot_ref[...] = cot
    y = jnp.sum(got_ref[:, :, tokens:], 0)
    folds = y.shape[1] // tokens
    y = jnp.concatenate([y[:, g * tokens : (g + 1) * tokens] for g in range(folds)], 0)
    rank = y.shape[0]
    y4 = jnp.concatenate([y] * (LANES // rank), 0)
    tile = (iota((rank, LANES), 1) % rank == iota((rank, LANES), 0)).astype(F32)
    p4 = nt(got_ref[t_ref[0], :, :tokens], y4) + dot(pe_ref[...], tile)
    p_pack = fold_rows(p4, rows // 4)

    own = wide // n_r
    turned_ref[...] = lax.dot_general(
        x_ref[...], cot, (((0,), (1,)), ((), ())), preferred_element_type=F32
    )
    halves, width = lane_halves(ff_win)
    at = halves * (own // 4)
    for k in range(n_r):
        for h in range(halves):
            lanes = slice(h * width, (h + 1) * width)
            for g in range(own // 4):
                row = 4 * g // group * LANES + k * group + 4 * g % group
                send_ref[k, h * (own // 4) + g, :, :width] = turned_ref[row : row + 4, lanes]
            for g in range(group // 4):
                row = k * group + 4 * g
                send_ref[k, at + 1 + h * (group // 4) + g, :, :width] = et_ref[row : row + 4, lanes]
        send_ref[k, at] = p_pack[:4]


def rows_kernel(t_ref, c_ref, cot_ref, got_ref, g_ref, dx_ref, w):
    n_t = got_ref.shape[0]
    rows, tokens = c_ref.shape
    wide = got_ref.shape[2]
    at = pl.ds(pl.multiple_of(tokens + t_ref[0] * rows, rows), rows)
    for k in range(n_t):
        g_ref[:, k * wide : (k + 1) * wide] = dot(c_ref[...], got_ref[k, :tokens, :], None)
        w[k * rows : (k + 1) * rows] = got_ref[k, at, :]
    dx_ref[...] = tn(cot_ref[...], w[...], None).astype(BF16)


def sum_kernel(got_ref, total_ref, send_ref, scratch, error):
    n_r = got_ref.shape[0]
    n_t = send_ref.shape[0]
    own, long = total_ref.shape
    ff_win = long // 2
    rows = ff_win // n_t
    group = own // 4
    halves, width = lane_halves(ff_win)
    at = halves * (own // 4)
    got = jnp.sum(got_ref[:, : at + 1], 0)
    p_pack = got[at]
    total = jnp.zeros(total_ref.shape, F32)
    for h in range(halves):
        for g in range(own // 4):
            scratch[h, 4 * g : 4 * g + 4, :] = got[h * (own // 4) + g]
        unit, lane = iota((width, long), 0) + h * width, iota((width, long), 1)
        t, b, a = unit // rows, unit % rows // 4, unit % 4
        move = (lane == b * (SUB * n_t) + t * SUB + a).astype(F32)
        total += dot(scratch[h, :, :width], move)
    total_ref[...] = total

    p8 = jnp.concatenate([p_pack, jnp.zeros_like(p_pack)], 0)
    spread = (iota((rows, SUB), 0) % 4 == iota((rows, SUB), 1)).astype(F32)
    p16 = dot(spread, p8)
    p16 = jnp.where(iota(p16.shape, 0) // 4 == iota(p16.shape, 1) // 32, p16, 0.0)
    square = (LANES, LANES)
    p16 = dot(p16, (iota(square, 0) % 32 == iota(square, 1) % 32).astype(F32))
    p_all = jnp.concatenate([p16] * n_t, 0)
    for b in range(4):
        part = sum(got_ref[r, at + 1 :] for r in range(b, n_r, 4))
        for h in range(halves):
            for g in range(group // 4):
                row = b * group + 4 * g
                error[row : row + 4, h * width : (h + 1) * width] = part[h * (group // 4) + g][:, :width]
    pieces = []
    for q in range(n_t // 4):
        mask = iota(p_all.shape, 0) // rows == 4 * q + iota(p_all.shape, 1) // 32
        out = dot(error[...], jnp.where(mask, p_all, 0.0))
        rolled = [out] + [pltpu.roll(out, 32 * d, 1) for d in range(1, 4)]
        row, lane = iota(out.shape, 0) // group, iota(out.shape, 1) // 32
        for s in range(4):
            kept = jnp.zeros(out.shape, F32)
            for b in range(4):
                kept = jnp.where((row == b) & (lane == b), rolled[(b - s) % 4], kept)
            pieces.append(kept)
    every = jnp.concatenate(pieces, 0)
    tall = max(group, SUB)
    pick_row, pick_col = iota((n_t * tall, n_t * own), 0), iota((n_t * tall, n_t * own), 1)
    pick = (pick_row // tall == pick_col // own) & (pick_row % tall == pick_col % group)
    folded = dot(pick.astype(F32), every)
    for k in range(n_t):
        send_ref[k, 0] = p_pack
        for g in range(group // 4):
            send_ref[k, 1 + g] = folded[k * tall + 4 * g : k * tall + 4 * g + 4]


def factor_kernel(n_r, pack_ref, total_ref, send_ref, gram_ref, inverse_ref, held, wide):
    wide[...] = jnp.zeros(wide.shape, F32)
    span = held.shape[0]
    own = total_ref.shape[0]
    rank = gram_ref.shape[0]
    group = own // 4
    held[...] = jnp.zeros(held.shape, F32)
    for k in range(pack_ref.shape[0]):
        held[k * SUB : k * SUB + 4] = pack_ref[k, 0]
    pack = held[...]
    gram4 = tn(pack, pack)
    gram = sum(gram4[b * rank : (b + 1) * rank, b * rank : (b + 1) * rank] for b in range(4))
    gram_ref[...] = gram
    row, lane = iota((rank, LANES), 0), iota((rank, LANES), 1)
    work = jnp.concatenate([gram, jnp.zeros((rank, LANES - rank), F32)], 1)
    work = jnp.where(lane == row + rank, 1.0, work)
    for first in range(0, rank, 4):
        columns = [jnp.broadcast_to(work[:, first + m : first + m + 1], work.shape) for m in range(4)]
        for m in range(4):
            j = first + m
            factor = jnp.where(row > j, columns[m] * (1.0 / columns[m][j : j + 1, :]), 0.0)
            work -= factor * work[j : j + 1, :]
            for n in range(m + 1, 4):
                columns[n] -= factor * columns[n][j : j + 1, :]
    diagonal = jnp.sum(jnp.where(lane == row, work, 0.0), 1, keepdims=True)
    inverse = (work * lax.rsqrt(diagonal))[:, rank : 2 * rank]
    inverse_ref[...] = inverse
    inverse16 = jnp.concatenate([inverse] * 4, 0)
    inverse16 = jnp.concatenate([inverse16] * 4, 1)
    total = total_ref[...]
    product = jnp.zeros((own, LANES), F32)
    for b in range(4):
        part = dot(total[:, b * span : (b + 1) * span], pack)
        product = jnp.where(iota(part.shape, 1) // rank == b, part, product)
    from_error = jnp.sum(pack_ref[:, 1:], 0)
    for g in range(group // 4):
        wide[4 * g : 4 * g + 4] = from_error[g]
    tall = wide.shape[0]
    spread = (iota((own, tall), 0) % group == iota((own, tall), 1)).astype(F32)
    from_error = dot(spread, wide[...])
    product += jnp.where(iota(product.shape, 0) // group == iota(product.shape, 1) // rank, from_error, 0.0)
    q4 = nt(product, inverse16) / n_r
    q_pack = fold_rows(q4, group)[:group]
    send_ref[...] = jnp.broadcast_to(q_pack[None], send_ref.shape)


def place_blocks(near_core, blocks_ref, basis_ref, e_ref, g_ref, q_hbm, error_hbm, q, error, sems, approx_ref, gram):
    n_z = blocks_ref.shape[0]
    rows = e_ref.shape[0]
    rank = q.shape[1]
    square = (LANES, LANES)
    basis4 = basis_ref[...]
    stack = jnp.concatenate(
        [(iota(square, 0) == iota(square, 1)).astype(F32)]
        + [jnp.where(iota(basis4.shape, 1) // rank == b, basis4, 0.0) for b in range(4)],
        0,
    )
    copies = []
    blocks = blocks_ref[...].reshape(n_z * LANES, LANES)
    every = nt(stack, blocks)
    for z in range(n_z):
        both = every[:, z * LANES : (z + 1) * LANES]
        start = pl.multiple_of((2 * z + near_core) * 4 * LANES, 4 * LANES)
        for b in range(4):
            near = both[LANES + b * rows : LANES + (b + 1) * rows]
            at = pl.ds(pl.multiple_of(start + b * LANES, LANES), LANES)
            to = slice(b * LANES, (b + 1) * LANES)
            q[z, :, to] = both[b * rank : (b + 1) * rank]
            approx_ref[z, :, to] = near
            error[z, :, to] = e_ref[:, at] + g_ref[:, at] - near
        span = pl.ds(start, 4 * LANES)
        copies.append(pltpu.make_async_copy(q.at[z], q_hbm.at[:, span], sems.at[0, z]))
        copies.append(pltpu.make_async_copy(error.at[z], error_hbm.at[:, span], sems.at[1, z]))
        copies[-2].start()
        copies[-1].start()
    return gram + tn(blocks, blocks), copies


def near_kernel(core_ref, mine_ref, basis_ref, e_ref, g_ref, q_hbm, error_hbm, approx_ref, gram_ref, q, error, sems):
    gram, copies = place_blocks(
        core_ref[0], mine_ref, basis_ref, e_ref, g_ref, q_hbm, error_hbm, q, error, sems, approx_ref,
        jnp.zeros((LANES, LANES), F32),
    )
    gram_ref[...] = gram
    for copy in copies:
        copy.wait()


def far_kernel(limit, core_ref, other_ref, basis_ref, e_ref, g_ref, gram_ref, approx_ref, weigh_ref, m_ref, q_old, error_old, q_hbm, error_hbm, momentum_ref, q, error, sems, far):
    core = core_ref[0]
    gram, copies = place_blocks(
        1 - core, other_ref, basis_ref, e_ref, g_ref, q_hbm, error_hbm, q, error, sems, far, gram_ref[...]
    )
    total = jnp.sum(gram * weigh_ref[...], keepdims=True)
    scale = jnp.minimum(1.0, limit / jnp.sqrt(total))
    for z in range(other_ref.shape[0]):
        for ref, c in ((approx_ref, core), (far, 1 - core)):
            at = pl.ds(pl.multiple_of((2 * z + c) * 4 * LANES, 4 * LANES), 4 * LANES)
            momentum_ref[:, at] = BETA * m_ref[:, at] + scale * ref[z]
    for copy in copies:
        copy.wait()


def body(tokens_x, cotangent, weight, error_fb, momentum, q_prev):
    n_t, n_r, n_z = lax.axis_size(T), lax.axis_size(R), lax.axis_size("z")
    t = lax.axis_index(T)[None]
    core = lax.axis_index("core")[None]
    tokens, wide = tokens_x.shape
    rows, width = weight.shape
    rank = q_prev.shape[0]
    ff_win = rows * n_t
    own = wide // n_r
    group = own // 4
    halves, _ = lane_halves(ff_win)
    error = error_fb[0]

    (first,) = call(
        first_kernel,
        [((n_t, rows, tokens + rank // rows * tokens), F32)],
        [SMEM] + [HBM] * 3,
        moved=2**20,
        limit=None,
        scratch_shapes=[
            pltpu.VMEM(tokens_x.shape, BF16),
            pltpu.VMEM(cotangent.shape, BF16),
            pltpu.VMEM((rank, wide), F32),
            pltpu.SemaphoreType.DMA((3,)),
        ],
    )(t, tokens_x, cotangent, q_prev)
    first, error_late, x_late = lax.optimization_barrier((first, error, tokens_x))
    *tiles, p_error = call(
        tiles_kernel,
        [((n_t, rows, LANES), F32)] * 4 + [((rows, rank), F32)],
        [SMEM, HBM, HBM],
        flops=2**27,
        moved=3 * 2**20,
        limit=None,
        scratch_shapes=[
            pltpu.VMEM(error.shape, F32),
            pltpu.VMEM(q_prev.shape, F32),
            pltpu.SemaphoreType.DMA((2,)),
        ],
    )(lax.axis_index("x")[None], error_late, q_prev)
    tiles = [tiles[0]] + [
        lax.ppermute(tiles[d], "x", [(i, (i + d) % 4) for i in range(4)]) for d in range(1, 4)
    ]
    error_t, p_error, x_near = call(
        turn_kernel,
        [((LANES, ff_win), F32), ((rows, rank), F32), (tokens_x.shape, BF16)],
        [VMEM] * 6,
        moved=2**20,
    )(*tiles, p_error, x_late)
    (bulk,) = call(
        pack_kernel, [((tokens + rows * n_t, wide), BF16)], [VMEM] * 2, moved=2**20
    )(x_late, weight)
    first = exchange(first, T)
    first, error_t, p_error, x_near, bulk = lax.optimization_barrier((first, error_t, p_error, x_near, bulk))
    bulk = lax.all_gather(bulk, T)
    blocks_g, blocks_e = halves * own // 4, halves * group // 4
    second, cot_all = call(
        merge_kernel,
        [((n_r, blocks_g + 1 + blocks_e, 4, LANES), F32), ((ff_win, tokens), BF16)],
        [SMEM] + [VMEM] * 4,
        moved=2 * 2**20,
        scratch_shapes=[pltpu.VMEM((wide, ff_win), F32)],
    )(t, first, x_near, p_error, error_t)
    second = exchange(second, R)
    total_t, third = call(
        sum_kernel,
        [((own, 2 * ff_win), F32), ((n_t, 1 + group // 4, 4, LANES), F32)],
        [VMEM],
        moved=2**20,
        scratch_shapes=[pltpu.VMEM((halves, own, LANES), F32), pltpu.VMEM((own, ff_win), F32)],
    )(second)
    p_pack = third[0, 0]
    third = exchange(third, T)

    q_send, gram, inverse = call(
        functools.partial(factor_kernel, n_r),
        [((n_r * n_z, group, LANES), F32), ((rank, rank), F32), ((rank, rank), F32)],
        [VMEM] * 2,
        flops=2**29,
        moved=2**20,
        scratch_shapes=[pltpu.VMEM((n_t * SUB, LANES), F32), pltpu.VMEM((max(group, SUB), LANES), F32)],
    )(third, total_t)
    mine = exchange(q_send, CHIPS)
    grad_rows, input_grad = call(
        rows_kernel,
        [((rows, width), F32), ((tokens, wide), BF16)],
        [SMEM] + [VMEM] * 3,
        flops=2**28,
        moved=8 * 2**20,
        scratch_shapes=[pltpu.VMEM((ff_win, wide), BF16)],
    )(t, cotangent, cot_all, bulk)
    basis_gram = dot(dot(inverse, gram), inverse.T)
    p_rows = p_pack.reshape(4, 4, rank).transpose(1, 0, 2).reshape(rows, rank)
    basis4 = jnp.tile(dot(p_rows, inverse.T), (1, 4))
    square = (LANES, LANES)
    weigh = jnp.where(
        iota(square, 0) // rank == iota(square, 1) // rank, jnp.tile(basis_gram, (4, 4)), 0.0
    )
    mine, grad_rows, weigh, basis4 = lax.optimization_barrier((mine, grad_rows, weigh, basis4))
    other = lax.ppermute(mine, "core", [(0, 1), (1, 0)])
    blocks = (n_z, LANES, LANES)
    limit = CLIPPING * math.sqrt(ff_win * width)
    scratch = [
        pltpu.VMEM((n_z, rank, wide), F32),
        pltpu.VMEM((n_z, rows, wide), F32),
        pltpu.SemaphoreType.DMA((2, n_z)),
    ]
    whole = [((rank, width), F32), ((rows, width), F32)]
    q_new, error_new, approx, q_gram = call(
        near_kernel,
        [*whole, ((n_z, rows, wide), F32), ((LANES, LANES), F32)],
        [SMEM] + [VMEM] * 4,
        [HBM, HBM, VMEM, VMEM],
        flops=2**30,
        moved=3 * 2**20,
        scratch_shapes=scratch,
    )(core, mine.reshape(blocks), basis4, error, grad_rows)
    q_new, error_new, momentum_new = call(
        functools.partial(far_kernel, limit),
        [*whole, ((rows, width), F32)],
        [SMEM] + [VMEM] * 8 + [HBM, HBM],
        [HBM, HBM, VMEM],
        flops=2**30,
        moved=4 * 2**20,
        scratch_shapes=[*scratch, pltpu.VMEM((n_z, rows, wide), F32)],
        input_output_aliases={9: 0, 10: 1},
    )(core, other.reshape(blocks), basis4, error, grad_rows, q_gram, approx, weigh, momentum, q_new, error_new)
    return (input_grad, error_new[None], momentum_new, q_new)


def solution(mesh):
    n_r, n_t = mesh.devices.shape
    x = 4
    split = Mesh(mesh.devices.reshape(n_r // x, x, n_t // 2, 2), (*R, *T))
    placed = (P(R, T), P(T, R), P(T, None), P(R, T, None), P(T, None), P())
    return jax.shard_map(
        body,
        mesh=split,
        in_specs=placed,
        out_specs=(P(R, T), P(R, T, None), P(T, None), P()),
        check_vma=False,
    )
```

```python
import functools
import math

import jax
import jax.numpy as jnp
from jax import lax
from jax.experimental import pallas as pl
from jax.experimental.pallas import tpu as pltpu
from jax.sharding import Mesh, PartitionSpec as P

CLIPPING = 0.2
BETA = 0.9
HIGHEST = lax.Precision.HIGHEST
LANES = 128
SUB = 8
F32 = jnp.float32
BF16 = jnp.bfloat16

T = ("z", "core")
R = ("y", "x")
CHIPS = ("z", "y", "x")

VMEM = pl.BlockSpec(memory_space=pltpu.VMEM)
SMEM = pl.BlockSpec(memory_space=pltpu.SMEM)
HBM = pl.BlockSpec(memory_space=pltpu.HBM)


def exchange(parts, axes):
    return lax.all_to_all(parts, axes, 0, 0, tiled=True)


def call(kernel, outs, in_specs=None, out_specs=None, flops=0, moved=0, limit=48, **more):
    outs = [jax.ShapeDtypeStruct(*o) for o in outs]
    return functools.partial(
        pl.pallas_call,
        kernel,
        out_shape=outs,
        out_specs=out_specs or [VMEM] * len(outs),
        cost_estimate=pl.CostEstimate(flops=flops, bytes_accessed=moved, transcendentals=0),
        compiler_params=pltpu.CompilerParams(vmem_limit_bytes=limit and limit * 2**20),
        **more,
    )(in_specs=in_specs)


def iota(shape, axis):
    return lax.broadcasted_iota(jnp.int32, shape, axis)


def nt(a, b, precision=HIGHEST):
    return lax.dot_general(a, b, (((1,), (1,)), ((), ())), precision=precision, preferred_element_type=F32)


def tn(a, b, precision=HIGHEST):
    return lax.dot_general(a, b, (((0,), (0,)), ((), ())), precision=precision, preferred_element_type=F32)


def dot(a, b, precision=HIGHEST):
    return jnp.dot(a, b, precision=precision, preferred_element_type=F32)


def lane_halves(ff_win):
    halves = max(ff_win // LANES, 1)
    return halves, ff_win // halves


def fold_rows(tiled, group):
    n = tiled.shape[0]
    kept = jnp.where(iota(tiled.shape, 0) // group == iota(tiled.shape, 1) // 32, tiled, 0.0)
    out = max(group, SUB)
    pick = (iota((out, n), 1) % group == iota((out, n), 0)).astype(F32)
    return dot(pick, kept)


def fetch(pairs, sems):
    copies = [pltpu.make_async_copy(src, dst, sems.at[i]) for i, (src, dst) in enumerate(pairs)]
    for copy in copies:
        copy.start()
    return copies


def first_kernel(t_ref, x_ref, c_ref, q_ref, send_ref, x, c, q, sems):
    n_t, rows, _ = send_ref.shape
    tokens, wide = x_ref.shape
    start = pl.multiple_of(t_ref[0] * wide, wide)
    for copy in fetch([(q_ref.at[:, pl.ds(start, wide)], q), (x_ref, x), (c_ref, c)], sems):
        copy.wait()
    y = nt(q[...], x[...].astype(F32))
    cot = c[...].astype(F32)
    for k in range(n_t):
        send_ref[k, :, :tokens] = cot
        for g in range(y.shape[0] // rows):
            at = tokens + g * tokens
            send_ref[k, :, at : at + tokens] = y[g * rows : (g + 1) * rows]


def tiles_kernel(x_ref, e_ref, q_ref, *refs):
    outs, pe_ref, (e, q, sems) = refs[:4], refs[4], refs[5:]
    n_t = outs[0].shape[0]
    copies = fetch([(e_ref, e), (q_ref, q)], sems)
    copies[0].wait()
    for d, out in enumerate(outs):
        b = lax.rem(x_ref[0] + d, 4)
        for k in range(n_t):
            out[k] = e[:, pl.ds(pl.multiple_of((4 * k + b) * LANES, LANES), LANES)]
    copies[1].wait()
    pe_ref[...] = nt(e[...], q[...])


def pack_kernel(x_ref, w_ref, a_ref, p_ref, out_ref, near_ref, tile_ref, pe_ref):
    near_ref[...] = x_ref[...]
    tile_ref[...] = a_ref[...]
    pe_ref[...] = p_ref[...]
    tokens, wide = x_ref.shape
    rows = w_ref.shape[0]
    out_ref[:tokens] = x_ref[...]
    for k in range(w_ref.shape[1] // wide):
        out_ref[tokens + k * rows : tokens + (k + 1) * rows] = w_ref[:, k * wide : (k + 1) * wide]


def turn_kernel(a_ref, b_ref, c_ref, d_ref, out_ref):
    rest = (a_ref[...] + b_ref[...]) + (c_ref[...] + d_ref[...])
    rest = rest.reshape(out_ref.shape[1], LANES)
    same = (iota((LANES, LANES), 0) == iota((LANES, LANES), 1)).astype(BF16)
    turned = jnp.zeros(out_ref.shape, F32)
    for _ in range(3):
        piece = rest.astype(BF16)
        turned += nt(same, piece, None)
        rest -= piece.astype(F32)
    out_ref[...] = turned


def merge_kernel(t_ref, got_ref, x_ref, pe_ref, et_ref, send_ref, cot_ref, turned_ref):
    n_t, rows, _ = got_ref.shape
    tokens, wide = x_ref.shape
    n_r = send_ref.shape[0]
    group = LANES // n_r
    ff_win = n_t * rows
    cot = got_ref[:, :, :tokens].reshape(ff_win, tokens).astype(BF16)
    cot_ref[...] = cot
    y = jnp.sum(got_ref[:, :, tokens:], 0)
    folds = y.shape[1] // tokens
    y = jnp.concatenate([y[:, g * tokens : (g + 1) * tokens] for g in range(folds)], 0)
    rank = y.shape[0]
    y4 = jnp.concatenate([y] * (LANES // rank), 0)
    tile = (iota((rank, LANES), 1) % rank == iota((rank, LANES), 0)).astype(F32)
    p4 = nt(got_ref[t_ref[0], :, :tokens], y4) + dot(pe_ref[...], tile)
    p_pack = fold_rows(p4, rows // 4)

    own = wide // n_r
    turned_ref[...] = lax.dot_general(
        x_ref[...], cot, (((0,), (1,)), ((), ())), preferred_element_type=F32
    )
    halves, width = lane_halves(ff_win)
    at = halves * (own // 4)
    for k in range(n_r):
        for h in range(halves):
            lanes = slice(h * width, (h + 1) * width)
            for g in range(own // 4):
                row = 4 * g // group * LANES + k * group + 4 * g % group
                send_ref[k, h * (own // 4) + g, :, :width] = turned_ref[row : row + 4, lanes]
            for g in range(group // 4):
                row = k * group + 4 * g
                send_ref[k, at + 1 + h * (group // 4) + g, :, :width] = et_ref[row : row + 4, lanes]
        send_ref[k, at] = p_pack[:4]


def rows_kernel(t_ref, c_ref, cot_ref, got_ref, g_ref, dx_ref, w):
    n_t = got_ref.shape[0]
    rows, tokens = c_ref.shape
    wide = got_ref.shape[2]
    at = pl.ds(pl.multiple_of(tokens + t_ref[0] * rows, rows), rows)
    for k in range(n_t):
        g_ref[:, k * wide : (k + 1) * wide] = dot(c_ref[...], got_ref[k, :tokens, :], None)
        w[k * rows : (k + 1) * rows] = got_ref[k, at, :]
    dx_ref[...] = tn(cot_ref[...], w[...], None).astype(BF16)


def sum_kernel(got_ref, total_ref, send_ref, scratch, error):
    n_r = got_ref.shape[0]
    n_t = send_ref.shape[0]
    own, long = total_ref.shape
    ff_win = long // 2
    rows = ff_win // n_t
    group = own // 4
    halves, width = lane_halves(ff_win)
    at = halves * (own // 4)
    got = jnp.sum(got_ref[:, : at + 1], 0)
    p_pack = got[at]
    total = jnp.zeros(total_ref.shape, F32)
    for h in range(halves):
        for g in range(own // 4):
            scratch[h, 4 * g : 4 * g + 4, :] = got[h * (own // 4) + g]
        unit, lane = iota((width, long), 0) + h * width, iota((width, long), 1)
        t, b, a = unit // rows, unit % rows // 4, unit % 4
        move = (lane == b * (SUB * n_t) + t * SUB + a).astype(F32)
        total += dot(scratch[h, :, :width], move)
    total_ref[...] = total

    p16 = jnp.concatenate([p_pack] * (rows // 4), 0)
    turns = [p16] + [pltpu.roll(p16, 32 * d, 1) for d in range(1, 4)]
    ahead = (iota(p16.shape, 1) // 32 - iota(p16.shape, 0) // 4) % 4
    for d in range(1, 4):
        p16 = jnp.where(ahead == d, turns[d], p16)
    p_all = jnp.concatenate([p16] * n_t, 0)
    for b in range(4):
        part = sum(got_ref[r, at + 1 :] for r in range(b, n_r, 4))
        for h in range(halves):
            for g in range(group // 4):
                row = b * group + 4 * g
                error[row : row + 4, h * width : (h + 1) * width] = part[h * (group // 4) + g][:, :width]
    for q in range(n_t // 4):
        mask = iota(p_all.shape, 0) // rows == 4 * q + iota(p_all.shape, 1) // 32
        out = dot(error[...], jnp.where(mask, p_all, 0.0))
        turns = [out] + [pltpu.roll(out, 32 * d, 1) for d in range(1, 4)]
        row, lane = iota(out.shape, 0) // group, iota(out.shape, 1) // 32
        for s in range(4):
            kept = jnp.zeros(out.shape, F32)
            for b in range(4):
                kept = jnp.where((row == b) & (lane == b), turns[(b - s) % 4], kept)
            kept = sum(kept[b * group : (b + 1) * group] for b in range(4))
            for g in range(group // 4):
                send_ref[4 * q + s, 1 + g] = kept[4 * g : 4 * g + 4]
    for k in range(n_t):
        send_ref[k, 0] = p_pack


def factor_kernel(n_r, pack_ref, total_ref, send_ref, gram_ref, inverse_ref, held, wide):
    wide[...] = jnp.zeros(wide.shape, F32)
    span = held.shape[0]
    own = total_ref.shape[0]
    rank = gram_ref.shape[0]
    group = own // 4
    held[...] = jnp.zeros(held.shape, F32)
    for k in range(pack_ref.shape[0]):
        held[k * SUB : k * SUB + 4] = pack_ref[k, 0]
    pack = held[...]
    gram4 = tn(pack, pack)
    gram = sum(gram4[b * rank : (b + 1) * rank, b * rank : (b + 1) * rank] for b in range(4))
    gram_ref[...] = gram
    row, lane = iota((rank, LANES), 0), iota((rank, LANES), 1)
    work = jnp.concatenate([gram, jnp.zeros((rank, LANES - rank), F32)], 1)
    work = jnp.where(lane == row + rank, 1.0, work)
    for first in range(0, rank, 4):
        columns = [jnp.broadcast_to(work[:, first + m : first + m + 1], work.shape) for m in range(4)]
        for m in range(4):
            j = first + m
            factor = jnp.where(row > j, columns[m] * (1.0 / columns[m][j : j + 1, :]), 0.0)
            work -= factor * work[j : j + 1, :]
            for n in range(m + 1, 4):
                columns[n] -= factor * columns[n][j : j + 1, :]
    diagonal = jnp.sum(jnp.where(lane == row, work, 0.0), 1, keepdims=True)
    inverse = (work * lax.rsqrt(diagonal))[:, rank : 2 * rank]
    inverse_ref[...] = inverse
    inverse16 = jnp.concatenate([inverse] * 4, 0)
    inverse16 = jnp.concatenate([inverse16] * 4, 1)
    total = total_ref[...]
    product = jnp.zeros((own, LANES), F32)
    for b in range(4):
        part = dot(total[:, b * span : (b + 1) * span], pack)
        product = jnp.where(iota(part.shape, 1) // rank == b, part, product)
    from_error = jnp.sum(pack_ref[:, 1:], 0)
    for g in range(group // 4):
        wide[4 * g : 4 * g + 4] = from_error[g]
    tall = wide.shape[0]
    spread = (iota((own, tall), 0) % group == iota((own, tall), 1)).astype(F32)
    from_error = dot(spread, wide[...])
    product += jnp.where(iota(product.shape, 0) // group == iota(product.shape, 1) // rank, from_error, 0.0)
    q4 = nt(product, inverse16) / n_r
    q_pack = fold_rows(q4, group)[:group]
    send_ref[...] = jnp.broadcast_to(q_pack[None], send_ref.shape)


def place_blocks(near_core, blocks_ref, basis_ref, e_ref, g_ref, q_hbm, error_hbm, q, error, sems, approx_ref, gram):
    n_z = blocks_ref.shape[0]
    rows = e_ref.shape[0]
    rank = q.shape[1]
    square = (LANES, LANES)
    basis4 = basis_ref[...]
    stack = jnp.concatenate(
        [(iota(square, 0) == iota(square, 1)).astype(F32)]
        + [jnp.where(iota(basis4.shape, 1) // rank == b, basis4, 0.0) for b in range(4)],
        0,
    )
    copies = []
    blocks = blocks_ref[...].reshape(n_z * LANES, LANES)
    every = nt(stack, blocks)
    for z in range(n_z):
        both = every[:, z * LANES : (z + 1) * LANES]
        start = pl.multiple_of((2 * z + near_core) * 4 * LANES, 4 * LANES)
        for b in range(4):
            near = both[LANES + b * rows : LANES + (b + 1) * rows]
            at = pl.ds(pl.multiple_of(start + b * LANES, LANES), LANES)
            to = slice(b * LANES, (b + 1) * LANES)
            q[z, :, to] = both[b * rank : (b + 1) * rank]
            approx_ref[z, :, to] = near
            error[z, :, to] = e_ref[:, at] + g_ref[:, at] - near
        span = pl.ds(start, 4 * LANES)
        copies.append(pltpu.make_async_copy(q.at[z], q_hbm.at[:, span], sems.at[0, z]))
        copies.append(pltpu.make_async_copy(error.at[z], error_hbm.at[:, span], sems.at[1, z]))
        copies[-2].start()
        copies[-1].start()
    return gram + tn(blocks, blocks), copies


def near_kernel(core_ref, mine_ref, basis_ref, e_ref, g_ref, q_hbm, error_hbm, approx_ref, gram_ref, q, error, sems):
    gram, copies = place_blocks(
        core_ref[0], mine_ref, basis_ref, e_ref, g_ref, q_hbm, error_hbm, q, error, sems, approx_ref,
        jnp.zeros((LANES, LANES), F32),
    )
    gram_ref[...] = gram
    for copy in copies:
        copy.wait()


def far_kernel(limit, core_ref, other_ref, basis_ref, e_ref, g_ref, gram_ref, approx_ref, weigh_ref, m_ref, q_old, error_old, q_hbm, error_hbm, momentum_ref, q, error, sems, far):
    core = core_ref[0]
    gram, copies = place_blocks(
        1 - core, other_ref, basis_ref, e_ref, g_ref, q_hbm, error_hbm, q, error, sems, far, gram_ref[...]
    )
    total = jnp.sum(gram * weigh_ref[...], keepdims=True)
    scale = jnp.minimum(1.0, limit / jnp.sqrt(total))
    for z in range(other_ref.shape[0]):
        for ref, c in ((approx_ref, core), (far, 1 - core)):
            at = pl.ds(pl.multiple_of((2 * z + c) * 4 * LANES, 4 * LANES), 4 * LANES)
            momentum_ref[:, at] = BETA * m_ref[:, at] + scale * ref[z]
    for copy in copies:
        copy.wait()


def body(tokens_x, cotangent, weight, error_fb, momentum, q_prev):
    n_t, n_r, n_z = lax.axis_size(T), lax.axis_size(R), lax.axis_size("z")
    t = lax.axis_index(T)[None]
    core = lax.axis_index("core")[None]
    tokens, wide = tokens_x.shape
    rows, width = weight.shape
    rank = q_prev.shape[0]
    ff_win = rows * n_t
    own = wide // n_r
    group = own // 4
    halves, _ = lane_halves(ff_win)
    error = error_fb[0]

    (first,) = call(
        first_kernel,
        [((n_t, rows, tokens + rank // rows * tokens), F32)],
        [SMEM] + [HBM] * 3,
        moved=2**20,
        limit=None,
        scratch_shapes=[
            pltpu.VMEM(tokens_x.shape, BF16),
            pltpu.VMEM(cotangent.shape, BF16),
            pltpu.VMEM((rank, wide), F32),
            pltpu.SemaphoreType.DMA((3,)),
        ],
    )(t, tokens_x, cotangent, q_prev)
    first, error_late, x_late = lax.optimization_barrier((first, error, tokens_x))
    *tiles, p_error = call(
        tiles_kernel,
        [((n_t, rows, LANES), F32)] * 4 + [((rows, rank), F32)],
        [SMEM, HBM, HBM],
        flops=2**27,
        moved=3 * 2**20,
        limit=None,
        scratch_shapes=[
            pltpu.VMEM(error.shape, F32),
            pltpu.VMEM(q_prev.shape, F32),
            pltpu.SemaphoreType.DMA((2,)),
        ],
    )(lax.axis_index("x")[None], error_late, q_prev)
    moved = [lax.ppermute(tiles[d], "x", [(i, (i + d) % 4) for i in range(4)]) for d in (2, 1, 3)]
    bulk, x_near, tile, p_error = call(
        pack_kernel,
        [
            ((tokens + rows * n_t, wide), BF16),
            (tokens_x.shape, BF16),
            ((n_t, rows, LANES), F32),
            ((rows, rank), F32),
        ],
        [VMEM] * 4,
        moved=2**20,
    )(x_late, weight, tiles[0], p_error)
    (error_t,) = call(turn_kernel, [((LANES, ff_win), F32)], [VMEM] * 4, moved=2**20)(tile, *moved)
    first = exchange(first, T)
    first, error_t, p_error, x_near, bulk = lax.optimization_barrier((first, error_t, p_error, x_near, bulk))
    bulk = lax.all_gather(bulk, T)
    blocks_g, blocks_e = halves * own // 4, halves * group // 4
    second, cot_all = call(
        merge_kernel,
        [((n_r, blocks_g + 1 + blocks_e, 4, LANES), F32), ((ff_win, tokens), BF16)],
        [SMEM] + [VMEM] * 4,
        moved=2 * 2**20,
        scratch_shapes=[pltpu.VMEM((wide, ff_win), F32)],
    )(t, first, x_near, p_error, error_t)
    second = exchange(second, R)
    total_t, third = call(
        sum_kernel,
        [((own, 2 * ff_win), F32), ((n_t, 1 + group // 4, 4, LANES), F32)],
        [VMEM],
        moved=2**20,
        scratch_shapes=[pltpu.VMEM((halves, own, LANES), F32), pltpu.VMEM((own, ff_win), F32)],
    )(second)
    p_pack = third[0, 0]
    third = exchange(third, T)

    q_send, gram, inverse = call(
        functools.partial(factor_kernel, n_r),
        [((n_r * n_z, group, LANES), F32), ((rank, rank), F32), ((rank, rank), F32)],
        [VMEM] * 2,
        flops=2**29,
        moved=2**20,
        scratch_shapes=[pltpu.VMEM((n_t * SUB, LANES), F32), pltpu.VMEM((max(group, SUB), LANES), F32)],
    )(third, total_t)
    mine = exchange(q_send, CHIPS)
    grad_rows, input_grad = call(
        rows_kernel,
        [((rows, width), F32), ((tokens, wide), BF16)],
        [SMEM] + [VMEM] * 3,
        flops=2**28,
        moved=8 * 2**20,
        scratch_shapes=[pltpu.VMEM((ff_win, wide), BF16)],
    )(t, cotangent, cot_all, bulk)
    basis_gram = dot(dot(inverse, gram), inverse.T)
    p_rows = p_pack.reshape(4, 4, rank).transpose(1, 0, 2).reshape(rows, rank)
    basis4 = jnp.tile(dot(p_rows, inverse.T), (1, 4))
    square = (LANES, LANES)
    weigh = jnp.where(
        iota(square, 0) // rank == iota(square, 1) // rank, jnp.tile(basis_gram, (4, 4)), 0.0
    )
    mine, grad_rows, weigh, basis4 = lax.optimization_barrier((mine, grad_rows, weigh, basis4))
    other = lax.ppermute(mine, "core", [(0, 1), (1, 0)])
    blocks = (n_z, LANES, LANES)
    limit = CLIPPING * math.sqrt(ff_win * width)
    scratch = [
        pltpu.VMEM((n_z, rank, wide), F32),
        pltpu.VMEM((n_z, rows, wide), F32),
        pltpu.SemaphoreType.DMA((2, n_z)),
    ]
    whole = [((rank, width), F32), ((rows, width), F32)]
    q_new, error_new, approx, q_gram = call(
        near_kernel,
        [*whole, ((n_z, rows, wide), F32), ((LANES, LANES), F32)],
        [SMEM] + [VMEM] * 4,
        [HBM, HBM, VMEM, VMEM],
        flops=2**30,
        moved=3 * 2**20,
        scratch_shapes=scratch,
    )(core, mine.reshape(blocks), basis4, error, grad_rows)
    q_new, error_new, momentum_new = call(
        functools.partial(far_kernel, limit),
        [*whole, ((rows, width), F32)],
        [SMEM] + [VMEM] * 8 + [HBM, HBM],
        [HBM, HBM, VMEM],
        flops=2**30,
        moved=4 * 2**20,
        scratch_shapes=[*scratch, pltpu.VMEM((n_z, rows, wide), F32)],
        input_output_aliases={9: 0, 10: 1},
    )(core, other.reshape(blocks), basis4, error, grad_rows, q_gram, approx, weigh, momentum, q_new, error_new)
    return (input_grad, error_new[None], momentum_new, q_new)


def solution(mesh):
    n_r, n_t = mesh.devices.shape
    x = 4
    split = Mesh(mesh.devices.reshape(n_r // x, x, n_t // 2, 2), (*R, *T))
    placed = (P(R, T), P(T, R), P(T, None), P(R, T, None), P(T, None), P())
    return jax.shard_map(
        body,
        mesh=split,
        in_specs=placed,
        out_specs=(P(R, T), P(R, T, None), P(T, None), P()),
        check_vma=False,
    )
```

```python
import functools
import math

import jax
import jax.numpy as jnp
from jax import lax
from jax.experimental import pallas as pl
from jax.experimental.pallas import tpu as pltpu
from jax.sharding import Mesh, PartitionSpec as P

CLIPPING = 0.2
BETA = 0.9
HIGHEST = lax.Precision.HIGHEST
LANES = 128
SUB = 8
F32 = jnp.float32
BF16 = jnp.bfloat16

T = ("z", "core")
R = ("y", "x")
CHIPS = ("z", "y", "x")

VMEM = pl.BlockSpec(memory_space=pltpu.VMEM)
SMEM = pl.BlockSpec(memory_space=pltpu.SMEM)
HBM = pl.BlockSpec(memory_space=pltpu.HBM)


def exchange(parts, axes):
    return lax.all_to_all(parts, axes, 0, 0, tiled=True)


def call(kernel, outs, in_specs=None, out_specs=None, flops=0, moved=0, limit=48, **more):
    outs = [jax.ShapeDtypeStruct(*o) for o in outs]
    return functools.partial(
        pl.pallas_call,
        kernel,
        out_shape=outs,
        out_specs=out_specs or [VMEM] * len(outs),
        cost_estimate=pl.CostEstimate(flops=flops, bytes_accessed=moved, transcendentals=0),
        compiler_params=pltpu.CompilerParams(vmem_limit_bytes=limit and limit * 2**20),
        **more,
    )(in_specs=in_specs)


def iota(shape, axis):
    return lax.broadcasted_iota(jnp.int32, shape, axis)


def nt(a, b, precision=HIGHEST):
    return lax.dot_general(a, b, (((1,), (1,)), ((), ())), precision=precision, preferred_element_type=F32)


def tn(a, b, precision=HIGHEST):
    return lax.dot_general(a, b, (((0,), (0,)), ((), ())), precision=precision, preferred_element_type=F32)


def dot(a, b, precision=HIGHEST):
    return jnp.dot(a, b, precision=precision, preferred_element_type=F32)


def lane_halves(ff_win):
    halves = max(ff_win // LANES, 1)
    return halves, ff_win // halves


def fold_rows(tiled, group):
    n = tiled.shape[0]
    kept = jnp.where(iota(tiled.shape, 0) // group == iota(tiled.shape, 1) // 32, tiled, 0.0)
    out = max(group, SUB)
    pick = (iota((out, n), 1) % group == iota((out, n), 0)).astype(F32)
    return dot(pick, kept)


def fetch(pairs, sems):
    copies = [pltpu.make_async_copy(src, dst, sems.at[i]) for i, (src, dst) in enumerate(pairs)]
    for copy in copies:
        copy.start()
    return copies


def first_kernel(t_ref, x_ref, c_ref, q_ref, send_ref, x, c, q, sems):
    n_t, rows, _ = send_ref.shape
    tokens, wide = x_ref.shape
    start = pl.multiple_of(t_ref[0] * wide, wide)
    for copy in fetch([(q_ref.at[:, pl.ds(start, wide)], q), (x_ref, x), (c_ref, c)], sems):
        copy.wait()
    y = nt(q[...], x[...].astype(F32))
    cot = c[...].astype(F32)
    for k in range(n_t):
        send_ref[k, :, :tokens] = cot
        for g in range(y.shape[0] // rows):
            at = tokens + g * tokens
            send_ref[k, :, at : at + tokens] = y[g * rows : (g + 1) * rows]


def tiles_kernel(x_ref, e_ref, q_ref, keep_ref, send_ref, pe_ref, e, q, sems):
    n_t = keep_ref.shape[1]
    half = x_ref[0] % 2
    copies = fetch([(e_ref, e), (q_ref, q)], sems)
    copies[0].wait()
    for ref, first in ((keep_ref, 2 * half), (send_ref, 2 - 2 * half)):
        for m in range(2):
            for k in range(n_t):
                ref[m, k] = e[:, pl.ds(pl.multiple_of((4 * k + first + m) * LANES, LANES), LANES)]
    copies[1].wait()
    pe_ref[...] = nt(e[...], q[...])


def pack_kernel(x_ref, w_ref, a_ref, p_ref, out_ref, near_ref, tile_ref, pe_ref):
    near_ref[...] = x_ref[...]
    tile_ref[...] = a_ref[...]
    pe_ref[...] = p_ref[...]
    tokens, wide = x_ref.shape
    rows = w_ref.shape[0]
    out_ref[:tokens] = x_ref[...]
    for k in range(w_ref.shape[1] // wide):
        out_ref[tokens + k * rows : tokens + (k + 1) * rows] = w_ref[:, k * wide : (k + 1) * wide]


def turn_kernel(a_ref, b_ref, out_ref):
    same = (iota((LANES, LANES), 0) == iota((LANES, LANES), 1)).astype(BF16)
    for m in range(2):
        rest = (a_ref[m] + b_ref[m]).reshape(out_ref.shape[1], LANES)
        turned = jnp.zeros((LANES, rest.shape[0]), F32)
        for _ in range(3):
            piece = rest.astype(BF16)
            turned += nt(same, piece, None)
            rest -= piece.astype(F32)
        out_ref[m * LANES : (m + 1) * LANES] = turned


def merge_kernel(t_ref, got_ref, x_ref, pe_ref, et_ref, send_ref, cot_ref, turned_ref):
    n_t, rows, _ = got_ref.shape
    tokens, wide = x_ref.shape
    n_r = send_ref.shape[0]
    group = LANES // n_r
    ff_win = n_t * rows
    cot = got_ref[:, :, :tokens].reshape(ff_win, tokens).astype(BF16)
    cot_ref[...] = cot
    y = jnp.sum(got_ref[:, :, tokens:], 0)
    folds = y.shape[1] // tokens
    y = jnp.concatenate([y[:, g * tokens : (g + 1) * tokens] for g in range(folds)], 0)
    rank = y.shape[0]
    y4 = jnp.concatenate([y] * (LANES // rank), 0)
    tile = (iota((rank, LANES), 1) % rank == iota((rank, LANES), 0)).astype(F32)
    p4 = nt(got_ref[t_ref[0], :, :tokens], y4) + dot(pe_ref[...], tile)
    p_pack = fold_rows(p4, rows // 4)

    own = wide // n_r
    turned_ref[...] = lax.dot_general(
        x_ref[...], cot, (((0,), (1,)), ((), ())), preferred_element_type=F32
    )
    halves, width = lane_halves(ff_win)
    at = halves * (own // 4)
    for k in range(n_r):
        for h in range(halves):
            lanes = slice(h * width, (h + 1) * width)
            for g in range(own // 4):
                row = 4 * g // group * LANES + k * group + 4 * g % group
                send_ref[k, h * (own // 4) + g, :, :width] = turned_ref[row : row + 4, lanes]
            for m in range(2):
                for g in range(group // 4):
                    row = m * LANES + k * group + 4 * g
                    block = at + 1 + (m * halves + h) * (group // 4) + g
                    send_ref[k, block, :, :width] = et_ref[row : row + 4, lanes]
        send_ref[k, at] = p_pack[:4]


def rows_kernel(t_ref, c_ref, cot_ref, got_ref, g_ref, dx_ref, w):
    n_t = got_ref.shape[0]
    rows, tokens = c_ref.shape
    wide = got_ref.shape[2]
    at = pl.ds(pl.multiple_of(tokens + t_ref[0] * rows, rows), rows)
    for k in range(n_t):
        g_ref[:, k * wide : (k + 1) * wide] = dot(c_ref[...], got_ref[k, :tokens, :], None)
        w[k * rows : (k + 1) * rows] = got_ref[k, at, :]
    dx_ref[...] = tn(cot_ref[...], w[...], None).astype(BF16)


def sum_kernel(got_ref, total_ref, send_ref, scratch, error):
    n_r = got_ref.shape[0]
    n_t = send_ref.shape[0]
    own, long = total_ref.shape
    ff_win = long // 2
    rows = ff_win // n_t
    group = own // 4
    halves, width = lane_halves(ff_win)
    at = halves * (own // 4)
    got = jnp.sum(got_ref[:, : at + 1], 0)
    p_pack = got[at]
    total = jnp.zeros(total_ref.shape, F32)
    for h in range(halves):
        for g in range(own // 4):
            scratch[h, 4 * g : 4 * g + 4, :] = got[h * (own // 4) + g]
        unit, lane = iota((width, long), 0) + h * width, iota((width, long), 1)
        t, b, a = unit // rows, unit % rows // 4, unit % 4
        move = (lane == b * (SUB * n_t) + t * SUB + a).astype(F32)
        total += dot(scratch[h, :, :width], move)
    total_ref[...] = total

    p16 = jnp.concatenate([p_pack] * (rows // 4), 0)
    turns = [p16] + [pltpu.roll(p16, 32 * d, 1) for d in range(1, 4)]
    ahead = (iota(p16.shape, 1) // 32 - iota(p16.shape, 0) // 4) % 4
    for d in range(1, 4):
        p16 = jnp.where(ahead == d, turns[d], p16)
    p_all = jnp.concatenate([p16] * n_t, 0)
    for b in range(4):
        tiles = halves * (group // 4)
        start = at + 1 + b % 2 * tiles
        part = sum(got_ref[r, start : start + tiles] for r in range(b // 2, n_r, 2))
        for h in range(halves):
            for g in range(group // 4):
                row = b * group + 4 * g
                error[row : row + 4, h * width : (h + 1) * width] = part[h * (group // 4) + g][:, :width]
    for q in range(n_t // 4):
        mask = iota(p_all.shape, 0) // rows == 4 * q + iota(p_all.shape, 1) // 32
        out = dot(error[...], jnp.where(mask, p_all, 0.0))
        turns = [out] + [pltpu.roll(out, 32 * d, 1) for d in range(1, 4)]
        row, lane = iota(out.shape, 0) // group, iota(out.shape, 1) // 32
        for s in range(4):
            kept = jnp.zeros(out.shape, F32)
            for b in range(4):
                kept = jnp.where((row == b) & (lane == b), turns[(b - s) % 4], kept)
            kept = sum(kept[b * group : (b + 1) * group] for b in range(4))
            for g in range(group // 4):
                send_ref[4 * q + s, 1 + g] = kept[4 * g : 4 * g + 4]
    for k in range(n_t):
        send_ref[k, 0] = p_pack


def factor_kernel(n_r, pack_ref, total_ref, send_ref, gram_ref, inverse_ref, held, wide):
    wide[...] = jnp.zeros(wide.shape, F32)
    span = held.shape[0]
    own = total_ref.shape[0]
    rank = gram_ref.shape[0]
    group = own // 4
    held[...] = jnp.zeros(held.shape, F32)
    for k in range(pack_ref.shape[0]):
        held[k * SUB : k * SUB + 4] = pack_ref[k, 0]
    pack = held[...]
    gram4 = tn(pack, pack)
    gram = sum(gram4[b * rank : (b + 1) * rank, b * rank : (b + 1) * rank] for b in range(4))
    gram_ref[...] = gram
    row, lane = iota((rank, LANES), 0), iota((rank, LANES), 1)
    work = jnp.concatenate([gram, jnp.zeros((rank, LANES - rank), F32)], 1)
    work = jnp.where(lane == row + rank, 1.0, work)
    for first in range(0, rank, 4):
        columns = [jnp.broadcast_to(work[:, first + m : first + m + 1], work.shape) for m in range(4)]
        for m in range(4):
            j = first + m
            factor = jnp.where(row > j, columns[m] * (1.0 / columns[m][j : j + 1, :]), 0.0)
            work -= factor * work[j : j + 1, :]
            for n in range(m + 1, 4):
                columns[n] -= factor * columns[n][j : j + 1, :]
    diagonal = jnp.sum(jnp.where(lane == row, work, 0.0), 1, keepdims=True)
    inverse = (work * lax.rsqrt(diagonal))[:, rank : 2 * rank]
    inverse_ref[...] = inverse
    inverse16 = jnp.concatenate([inverse] * 4, 0)
    inverse16 = jnp.concatenate([inverse16] * 4, 1)
    total = total_ref[...]
    product = jnp.zeros((own, LANES), F32)
    for b in range(4):
        part = dot(total[:, b * span : (b + 1) * span], pack)
        product = jnp.where(iota(part.shape, 1) // rank == b, part, product)
    from_error = jnp.sum(pack_ref[:, 1:], 0)
    for g in range(group // 4):
        wide[4 * g : 4 * g + 4] = from_error[g]
    tall = wide.shape[0]
    spread = (iota((own, tall), 0) % group == iota((own, tall), 1)).astype(F32)
    from_error = dot(spread, wide[...])
    product += jnp.where(iota(product.shape, 0) // group == iota(product.shape, 1) // rank, from_error, 0.0)
    q4 = nt(product, inverse16) / n_r
    q_pack = fold_rows(q4, group)[:group]
    send_ref[...] = jnp.broadcast_to(q_pack[None], send_ref.shape)


def place_blocks(near_core, blocks_ref, basis_ref, e_ref, g_ref, q_hbm, error_hbm, q, error, sems, approx_ref, gram):
    n_z = blocks_ref.shape[0]
    rows = e_ref.shape[0]
    rank = q.shape[1]
    square = (LANES, LANES)
    basis4 = basis_ref[...]
    stack = jnp.concatenate(
        [(iota(square, 0) == iota(square, 1)).astype(F32)]
        + [jnp.where(iota(basis4.shape, 1) // rank == b, basis4, 0.0) for b in range(4)],
        0,
    )
    copies = []
    blocks = blocks_ref[...].reshape(n_z * LANES, LANES)
    every = nt(stack, blocks)
    for z in range(n_z):
        both = every[:, z * LANES : (z + 1) * LANES]
        start = pl.multiple_of((2 * z + near_core) * 4 * LANES, 4 * LANES)
        for b in range(4):
            near = both[LANES + b * rows : LANES + (b + 1) * rows]
            at = pl.ds(pl.multiple_of(start + b * LANES, LANES), LANES)
            to = slice(b * LANES, (b + 1) * LANES)
            q[z, :, to] = both[b * rank : (b + 1) * rank]
            approx_ref[z, :, to] = near
            error[z, :, to] = e_ref[:, at] + g_ref[:, at] - near
        span = pl.ds(start, 4 * LANES)
        copies.append(pltpu.make_async_copy(q.at[z], q_hbm.at[:, span], sems.at[0, z]))
        copies.append(pltpu.make_async_copy(error.at[z], error_hbm.at[:, span], sems.at[1, z]))
        copies[-2].start()
        copies[-1].start()
    return gram + tn(blocks, blocks), copies


def near_kernel(core_ref, mine_ref, basis_ref, e_ref, g_ref, q_hbm, error_hbm, approx_ref, gram_ref, q, error, sems):
    gram, copies = place_blocks(
        core_ref[0], mine_ref, basis_ref, e_ref, g_ref, q_hbm, error_hbm, q, error, sems, approx_ref,
        jnp.zeros((LANES, LANES), F32),
    )
    gram_ref[...] = gram
    for copy in copies:
        copy.wait()


def far_kernel(limit, core_ref, other_ref, basis_ref, e_ref, g_ref, gram_ref, approx_ref, weigh_ref, m_ref, q_old, error_old, q_hbm, error_hbm, momentum_ref, q, error, sems, far):
    core = core_ref[0]
    gram, copies = place_blocks(
        1 - core, other_ref, basis_ref, e_ref, g_ref, q_hbm, error_hbm, q, error, sems, far, gram_ref[...]
    )
    total = jnp.sum(gram * weigh_ref[...], keepdims=True)
    scale = jnp.minimum(1.0, limit / jnp.sqrt(total))
    for z in range(other_ref.shape[0]):
        for ref, c in ((approx_ref, core), (far, 1 - core)):
            at = pl.ds(pl.multiple_of((2 * z + c) * 4 * LANES, 4 * LANES), 4 * LANES)
            momentum_ref[:, at] = BETA * m_ref[:, at] + scale * ref[z]
    for copy in copies:
        copy.wait()


def body(tokens_x, cotangent, weight, error_fb, momentum, q_prev):
    n_t, n_r, n_z = lax.axis_size(T), lax.axis_size(R), lax.axis_size("z")
    t = lax.axis_index(T)[None]
    core = lax.axis_index("core")[None]
    tokens, wide = tokens_x.shape
    rows, width = weight.shape
    rank = q_prev.shape[0]
    ff_win = rows * n_t
    own = wide // n_r
    group = own // 4
    halves, _ = lane_halves(ff_win)
    error = error_fb[0]

    (first,) = call(
        first_kernel,
        [((n_t, rows, tokens + rank // rows * tokens), F32)],
        [SMEM] + [HBM] * 3,
        moved=2**20,
        limit=None,
        scratch_shapes=[
            pltpu.VMEM(tokens_x.shape, BF16),
            pltpu.VMEM(cotangent.shape, BF16),
            pltpu.VMEM((rank, wide), F32),
            pltpu.SemaphoreType.DMA((3,)),
        ],
    )(t, tokens_x, cotangent, q_prev)
    first, error_late, x_late = lax.optimization_barrier((first, error, tokens_x))
    kept, given, p_error = call(
        tiles_kernel,
        [((2, n_t, rows, LANES), F32)] * 2 + [((rows, rank), F32)],
        [SMEM, HBM, HBM],
        flops=2**27,
        moved=3 * 2**20,
        limit=None,
        scratch_shapes=[
            pltpu.VMEM(error.shape, F32),
            pltpu.VMEM(q_prev.shape, F32),
            pltpu.SemaphoreType.DMA((2,)),
        ],
    )(lax.axis_index("x")[None], error_late, q_prev)
    moved = lax.ppermute(given, "x", [(i, i ^ 1) for i in range(4)])
    bulk, x_near, kept, p_error = call(
        pack_kernel,
        [
            ((tokens + rows * n_t, wide), BF16),
            (tokens_x.shape, BF16),
            (kept.shape, F32),
            ((rows, rank), F32),
        ],
        [VMEM] * 4,
        moved=2**20,
    )(x_late, weight, kept, p_error)
    (error_t,) = call(turn_kernel, [((2 * LANES, ff_win), F32)], [VMEM] * 2, moved=2**20)(kept, moved)
    first = exchange(first, T)
    first, error_t, p_error, x_near, bulk = lax.optimization_barrier((first, error_t, p_error, x_near, bulk))
    bulk = lax.all_gather(bulk, T)
    blocks_g, blocks_e = halves * own // 4, halves * group // 2
    second, cot_all = call(
        merge_kernel,
        [((n_r, blocks_g + 1 + blocks_e, 4, LANES), F32), ((ff_win, tokens), BF16)],
        [SMEM] + [VMEM] * 4,
        moved=2 * 2**20,
        scratch_shapes=[pltpu.VMEM((wide, ff_win), F32)],
    )(t, first, x_near, p_error, error_t)
    second = exchange(second, R)
    total_t, third = call(
        sum_kernel,
        [((own, 2 * ff_win), F32), ((n_t, 1 + group // 4, 4, LANES), F32)],
        [VMEM],
        moved=2**20,
        scratch_shapes=[pltpu.VMEM((halves, own, LANES), F32), pltpu.VMEM((own, ff_win), F32)],
    )(second)
    p_pack = third[0, 0]
    third = exchange(third, T)

    q_send, gram, inverse = call(
        functools.partial(factor_kernel, n_r),
        [((n_r * n_z, group, LANES), F32), ((rank, rank), F32), ((rank, rank), F32)],
        [VMEM] * 2,
        flops=2**29,
        moved=2**20,
        scratch_shapes=[pltpu.VMEM((n_t * SUB, LANES), F32), pltpu.VMEM((max(group, SUB), LANES), F32)],
    )(third, total_t)
    mine = exchange(q_send, CHIPS)
    grad_rows, input_grad = call(
        rows_kernel,
        [((rows, width), F32), ((tokens, wide), BF16)],
        [SMEM] + [VMEM] * 3,
        flops=2**28,
        moved=8 * 2**20,
        scratch_shapes=[pltpu.VMEM((ff_win, wide), BF16)],
    )(t, cotangent, cot_all, bulk)
    basis_gram = dot(dot(inverse, gram), inverse.T)
    p_rows = p_pack.reshape(4, 4, rank).transpose(1, 0, 2).reshape(rows, rank)
    basis4 = jnp.tile(dot(p_rows, inverse.T), (1, 4))
    square = (LANES, LANES)
    weigh = jnp.where(
        iota(square, 0) // rank == iota(square, 1) // rank, jnp.tile(basis_gram, (4, 4)), 0.0
    )
    mine, grad_rows, weigh, basis4 = lax.optimization_barrier((mine, grad_rows, weigh, basis4))
    other = lax.ppermute(mine, "core", [(0, 1), (1, 0)])
    blocks = (n_z, LANES, LANES)
    limit = CLIPPING * math.sqrt(ff_win * width)
    scratch = [
        pltpu.VMEM((n_z, rank, wide), F32),
        pltpu.VMEM((n_z, rows, wide), F32),
        pltpu.SemaphoreType.DMA((2, n_z)),
    ]
    whole = [((rank, width), F32), ((rows, width), F32)]
    q_new, error_new, approx, q_gram = call(
        near_kernel,
        [*whole, ((n_z, rows, wide), F32), ((LANES, LANES), F32)],
        [SMEM] + [VMEM] * 4,
        [HBM, HBM, VMEM, VMEM],
        flops=2**30,
        moved=3 * 2**20,
        scratch_shapes=scratch,
    )(core, mine.reshape(blocks), basis4, error, grad_rows)
    q_new, error_new, momentum_new = call(
        functools.partial(far_kernel, limit),
        [*whole, ((rows, width), F32)],
        [SMEM] + [VMEM] * 8 + [HBM, HBM],
        [HBM, HBM, VMEM],
        flops=2**30,
        moved=4 * 2**20,
        scratch_shapes=[*scratch, pltpu.VMEM((n_z, rows, wide), F32)],
        input_output_aliases={9: 0, 10: 1},
    )(core, other.reshape(blocks), basis4, error, grad_rows, q_gram, approx, weigh, momentum, q_new, error_new)
    return (input_grad, error_new[None], momentum_new, q_new)


def solution(mesh):
    n_r, n_t = mesh.devices.shape
    x = 4
    split = Mesh(mesh.devices.reshape(n_r // x, x, n_t // 2, 2), (*R, *T))
    placed = (P(R, T), P(T, R), P(T, None), P(R, T, None), P(T, None), P())
    return jax.shard_map(
        body,
        mesh=split,
        in_specs=placed,
        out_specs=(P(R, T), P(R, T, None), P(T, None), P()),
        check_vma=False,
    )
```

```python
import functools
import math

import jax
import jax.numpy as jnp
from jax import lax
from jax.experimental import pallas as pl
from jax.experimental.pallas import tpu as pltpu
from jax.sharding import Mesh, PartitionSpec as P

CLIPPING = 0.2
BETA = 0.9
HIGHEST = lax.Precision.HIGHEST
LANES = 128
SUB = 8
F32 = jnp.float32
BF16 = jnp.bfloat16

T = ("z", "core")
R = ("y", "x")
CHIPS = ("z", "y", "x")

VMEM = pl.BlockSpec(memory_space=pltpu.VMEM)
SMEM = pl.BlockSpec(memory_space=pltpu.SMEM)
HBM = pl.BlockSpec(memory_space=pltpu.HBM)


def exchange(parts, axes):
    return lax.all_to_all(parts, axes, 0, 0, tiled=True)


def call(kernel, outs, in_specs=None, out_specs=None, flops=0, moved=0, limit=48, **more):
    outs = [jax.ShapeDtypeStruct(*o) for o in outs]
    return functools.partial(
        pl.pallas_call,
        kernel,
        out_shape=outs,
        out_specs=out_specs or [VMEM] * len(outs),
        cost_estimate=pl.CostEstimate(flops=flops, bytes_accessed=moved, transcendentals=0),
        compiler_params=pltpu.CompilerParams(vmem_limit_bytes=limit and limit * 2**20),
        **more,
    )(in_specs=in_specs)


def iota(shape, axis):
    return lax.broadcasted_iota(jnp.int32, shape, axis)


def nt(a, b, precision=HIGHEST):
    return lax.dot_general(a, b, (((1,), (1,)), ((), ())), precision=precision, preferred_element_type=F32)


def tn(a, b, precision=HIGHEST):
    return lax.dot_general(a, b, (((0,), (0,)), ((), ())), precision=precision, preferred_element_type=F32)


def dot(a, b, precision=HIGHEST):
    return jnp.dot(a, b, precision=precision, preferred_element_type=F32)


def lane_halves(ff_win):
    halves = max(ff_win // LANES, 1)
    return halves, ff_win // halves


def fold_rows(tiled, group):
    n = tiled.shape[0]
    kept = jnp.where(iota(tiled.shape, 0) // group == iota(tiled.shape, 1) // 32, tiled, 0.0)
    out = max(group, SUB)
    pick = (iota((out, n), 1) % group == iota((out, n), 0)).astype(F32)
    return dot(pick, kept)


def fetch(pairs, sems):
    copies = [pltpu.make_async_copy(src, dst, sems.at[i]) for i, (src, dst) in enumerate(pairs)]
    for copy in copies:
        copy.start()
    return copies


def first_kernel(t_ref, x_ref, c_ref, q_ref, send_ref, x, c, q, sems):
    n_t, rows, _ = send_ref.shape
    tokens, wide = x_ref.shape
    start = pl.multiple_of(t_ref[0] * wide, wide)
    for copy in fetch([(q_ref.at[:, pl.ds(start, wide)], q), (x_ref, x), (c_ref, c)], sems):
        copy.wait()
    y = nt(q[...], x[...].astype(F32))
    cot = c[...].astype(F32)
    for k in range(n_t):
        send_ref[k, :, :tokens] = cot
        for g in range(y.shape[0] // rows):
            at = tokens + g * tokens
            send_ref[k, :, at : at + tokens] = y[g * rows : (g + 1) * rows]


def tiles_kernel(x_ref, e_ref, keep_ref, send_ref, e, sem):
    n_t = keep_ref.shape[1]
    half = x_ref[0] % 2
    copy = pltpu.make_async_copy(e_ref, e, sem)
    copy.start()
    copy.wait()
    for ref, first in ((keep_ref, 2 * half), (send_ref, 2 - 2 * half)):
        for m in range(2):
            for k in range(n_t):
                ref[m, k] = e[:, pl.ds(pl.multiple_of((4 * k + first + m) * LANES, LANES), LANES)]


def project_kernel(e_ref, q_ref, pe_ref, e, q, sems):
    for copy in fetch([(e_ref, e), (q_ref, q)], sems):
        copy.wait()
    pe_ref[...] = nt(e[...], q[...])


def pack_kernel(x_ref, w_ref, a_ref, p_ref, out_ref, near_ref, tile_ref, pe_ref):
    near_ref[...] = x_ref[...]
    tile_ref[...] = a_ref[...]
    pe_ref[...] = p_ref[...]
    tokens, wide = x_ref.shape
    rows = w_ref.shape[0]
    out_ref[:tokens] = x_ref[...]
    for k in range(w_ref.shape[1] // wide):
        out_ref[tokens + k * rows : tokens + (k + 1) * rows] = w_ref[:, k * wide : (k + 1) * wide]


def turn_kernel(a_ref, b_ref, out_ref):
    same = (iota((LANES, LANES), 0) == iota((LANES, LANES), 1)).astype(BF16)
    for m in range(2):
        rest = (a_ref[m] + b_ref[m]).reshape(out_ref.shape[1], LANES)
        turned = jnp.zeros((LANES, rest.shape[0]), F32)
        for _ in range(3):
            piece = rest.astype(BF16)
            turned += nt(same, piece, None)
            rest -= piece.astype(F32)
        out_ref[m * LANES : (m + 1) * LANES] = turned


def merge_kernel(t_ref, got_ref, x_ref, pe_ref, et_ref, send_ref, cot_ref, turned_ref):
    n_t, rows, _ = got_ref.shape
    tokens, wide = x_ref.shape
    n_r = send_ref.shape[0]
    group = LANES // n_r
    ff_win = n_t * rows
    cot = got_ref[:, :, :tokens].reshape(ff_win, tokens).astype(BF16)
    cot_ref[...] = cot
    y = jnp.sum(got_ref[:, :, tokens:], 0)
    folds = y.shape[1] // tokens
    y = jnp.concatenate([y[:, g * tokens : (g + 1) * tokens] for g in range(folds)], 0)
    rank = y.shape[0]
    y4 = jnp.concatenate([y] * (LANES // rank), 0)
    tile = (iota((rank, LANES), 1) % rank == iota((rank, LANES), 0)).astype(F32)
    p4 = nt(got_ref[t_ref[0], :, :tokens], y4) + dot(pe_ref[...], tile)
    p_pack = fold_rows(p4, rows // 4)

    own = wide // n_r
    turned_ref[...] = lax.dot_general(
        x_ref[...], cot, (((0,), (1,)), ((), ())), preferred_element_type=F32
    )
    halves, width = lane_halves(ff_win)
    at = halves * (own // 4)
    for k in range(n_r):
        for h in range(halves):
            lanes = slice(h * width, (h + 1) * width)
            for g in range(own // 4):
                row = 4 * g // group * LANES + k * group + 4 * g % group
                send_ref[k, h * (own // 4) + g, :, :width] = turned_ref[row : row + 4, lanes]
            for m in range(2):
                for g in range(group // 4):
                    row = m * LANES + k * group + 4 * g
                    block = at + 1 + (m * halves + h) * (group // 4) + g
                    send_ref[k, block, :, :width] = et_ref[row : row + 4, lanes]
        send_ref[k, at] = p_pack[:4]


def rows_kernel(t_ref, c_ref, cot_ref, got_ref, g_ref, dx_ref, w):
    n_t = got_ref.shape[0]
    rows, tokens = c_ref.shape
    wide = got_ref.shape[2]
    at = pl.ds(pl.multiple_of(tokens + t_ref[0] * rows, rows), rows)
    for k in range(n_t):
        g_ref[:, k * wide : (k + 1) * wide] = dot(c_ref[...], got_ref[k, :tokens, :], None)
        w[k * rows : (k + 1) * rows] = got_ref[k, at, :]
    dx_ref[...] = tn(cot_ref[...], w[...], None).astype(BF16)


def sum_kernel(got_ref, total_ref, send_ref, scratch, error):
    n_r = got_ref.shape[0]
    n_t = send_ref.shape[0]
    own, long = total_ref.shape
    ff_win = long // 2
    rows = ff_win // n_t
    group = own // 4
    halves, width = lane_halves(ff_win)
    at = halves * (own // 4)
    got = jnp.sum(got_ref[:, : at + 1], 0)
    p_pack = got[at]
    total = jnp.zeros(total_ref.shape, F32)
    for h in range(halves):
        for g in range(own // 4):
            scratch[h, 4 * g : 4 * g + 4, :] = got[h * (own // 4) + g]
        unit, lane = iota((width, long), 0) + h * width, iota((width, long), 1)
        t, b, a = unit // rows, unit % rows // 4, unit % 4
        move = (lane == b * (SUB * n_t) + t * SUB + a).astype(F32)
        total += dot(scratch[h, :, :width], move)
    total_ref[...] = total

    p16 = jnp.concatenate([p_pack] * (rows // 4), 0)
    turns = [p16] + [pltpu.roll(p16, 32 * d, 1) for d in range(1, 4)]
    ahead = (iota(p16.shape, 1) // 32 - iota(p16.shape, 0) // 4) % 4
    for d in range(1, 4):
        p16 = jnp.where(ahead == d, turns[d], p16)
    p_all = jnp.concatenate([p16] * n_t, 0)
    for b in range(4):
        tiles = halves * (group // 4)
        start = at + 1 + b % 2 * tiles
        part = sum(got_ref[r, start : start + tiles] for r in range(b // 2, n_r, 2))
        for h in range(halves):
            for g in range(group // 4):
                row = b * group + 4 * g
                error[row : row + 4, h * width : (h + 1) * width] = part[h * (group // 4) + g][:, :width]
    for q in range(n_t // 4):
        mask = iota(p_all.shape, 0) // rows == 4 * q + iota(p_all.shape, 1) // 32
        out = dot(error[...], jnp.where(mask, p_all, 0.0))
        turns = [out] + [pltpu.roll(out, 32 * d, 1) for d in range(1, 4)]
        row, lane = iota(out.shape, 0) // group, iota(out.shape, 1) // 32
        for s in range(4):
            kept = jnp.zeros(out.shape, F32)
            for b in range(4):
                kept = jnp.where((row == b) & (lane == b), turns[(b - s) % 4], kept)
            kept = sum(kept[b * group : (b + 1) * group] for b in range(4))
            for g in range(group // 4):
                send_ref[4 * q + s, 1 + g] = kept[4 * g : 4 * g + 4]
    for k in range(n_t):
        send_ref[k, 0] = p_pack


def factor_kernel(n_r, pack_ref, total_ref, send_ref, gram_ref, inverse_ref, held, wide):
    wide[...] = jnp.zeros(wide.shape, F32)
    span = held.shape[0]
    own = total_ref.shape[0]
    rank = gram_ref.shape[0]
    group = own // 4
    held[...] = jnp.zeros(held.shape, F32)
    for k in range(pack_ref.shape[0]):
        held[k * SUB : k * SUB + 4] = pack_ref[k, 0]
    pack = held[...]
    gram4 = tn(pack, pack)
    gram = sum(gram4[b * rank : (b + 1) * rank, b * rank : (b + 1) * rank] for b in range(4))
    gram_ref[...] = gram
    row, lane = iota((rank, LANES), 0), iota((rank, LANES), 1)
    work = jnp.concatenate([gram, jnp.zeros((rank, LANES - rank), F32)], 1)
    work = jnp.where(lane == row + rank, 1.0, work)
    for first in range(0, rank, 8):
        columns = [jnp.broadcast_to(work[:, first + m : first + m + 1], work.shape) for m in range(8)]
        for m in range(8):
            j = first + m
            factor = jnp.where(row > j, columns[m] * (1.0 / columns[m][j : j + 1, :]), 0.0)
            work -= factor * work[j : j + 1, :]
            for n in range(m + 1, 8):
                columns[n] -= factor * columns[n][j : j + 1, :]
    diagonal = jnp.sum(jnp.where(lane == row, work, 0.0), 1, keepdims=True)
    inverse = (work * lax.rsqrt(diagonal))[:, rank : 2 * rank]
    inverse_ref[...] = inverse
    inverse16 = jnp.concatenate([inverse] * 4, 0)
    inverse16 = jnp.concatenate([inverse16] * 4, 1)
    total = total_ref[...]
    product = jnp.zeros((own, LANES), F32)
    for b in range(4):
        part = dot(total[:, b * span : (b + 1) * span], pack)
        product = jnp.where(iota(part.shape, 1) // rank == b, part, product)
    from_error = jnp.sum(pack_ref[:, 1:], 0)
    for g in range(group // 4):
        wide[4 * g : 4 * g + 4] = from_error[g]
    tall = wide.shape[0]
    spread = (iota((own, tall), 0) % group == iota((own, tall), 1)).astype(F32)
    from_error = dot(spread, wide[...])
    product += jnp.where(iota(product.shape, 0) // group == iota(product.shape, 1) // rank, from_error, 0.0)
    q4 = nt(product, inverse16) / n_r
    q_pack = fold_rows(q4, group)[:group]
    send_ref[...] = jnp.broadcast_to(q_pack[None], send_ref.shape)


def place_blocks(near_core, blocks_ref, basis_ref, e_ref, g_ref, q_hbm, error_hbm, q, error, sems, approx_ref, gram):
    n_z = blocks_ref.shape[0]
    rows = e_ref.shape[0]
    rank = q.shape[1]
    square = (LANES, LANES)
    basis4 = basis_ref[...]
    stack = jnp.concatenate(
        [(iota(square, 0) == iota(square, 1)).astype(F32)]
        + [jnp.where(iota(basis4.shape, 1) // rank == b, basis4, 0.0) for b in range(4)],
        0,
    )
    copies = []
    blocks = blocks_ref[...].reshape(n_z * LANES, LANES)
    every = nt(stack, blocks)
    for z in range(n_z):
        both = every[:, z * LANES : (z + 1) * LANES]
        start = pl.multiple_of((2 * z + near_core) * 4 * LANES, 4 * LANES)
        for b in range(4):
            near = both[LANES + b * rows : LANES + (b + 1) * rows]
            at = pl.ds(pl.multiple_of(start + b * LANES, LANES), LANES)
            to = slice(b * LANES, (b + 1) * LANES)
            q[z, :, to] = both[b * rank : (b + 1) * rank]
            approx_ref[z, :, to] = near
            error[z, :, to] = e_ref[:, at] + g_ref[:, at] - near
        span = pl.ds(start, 4 * LANES)
        copies.append(pltpu.make_async_copy(q.at[z], q_hbm.at[:, span], sems.at[0, z]))
        copies.append(pltpu.make_async_copy(error.at[z], error_hbm.at[:, span], sems.at[1, z]))
        copies[-2].start()
        copies[-1].start()
    return gram + tn(blocks, blocks), copies


def near_kernel(core_ref, mine_ref, basis_ref, e_ref, g_ref, q_hbm, error_hbm, approx_ref, gram_ref, q, error, sems):
    gram, copies = place_blocks(
        core_ref[0], mine_ref, basis_ref, e_ref, g_ref, q_hbm, error_hbm, q, error, sems, approx_ref,
        jnp.zeros((LANES, LANES), F32),
    )
    gram_ref[...] = gram
    for copy in copies:
        copy.wait()


def far_kernel(limit, core_ref, other_ref, basis_ref, e_ref, g_ref, gram_ref, approx_ref, weigh_ref, m_ref, q_old, error_old, q_hbm, error_hbm, momentum_hbm, q, error, sems, far, out, out_sems):
    core = core_ref[0]
    gram, copies = place_blocks(
        1 - core, other_ref, basis_ref, e_ref, g_ref, q_hbm, error_hbm, q, error, sems, far, gram_ref[...]
    )
    total = jnp.sum(gram * weigh_ref[...], keepdims=True)
    scale = jnp.minimum(1.0, limit / jnp.sqrt(total))
    for z in range(other_ref.shape[0]):
        for i, ref, c in ((0, approx_ref, core), (1, far, 1 - core)):
            at = pl.ds(pl.multiple_of((2 * z + c) * 4 * LANES, 4 * LANES), 4 * LANES)
            out[i, z] = BETA * m_ref[:, at] + scale * ref[z]
            copies.append(pltpu.make_async_copy(out.at[i, z], momentum_hbm.at[:, at], out_sems.at[i, z]))
            copies[-1].start()
    for copy in copies:
        copy.wait()


def body(tokens_x, cotangent, weight, error_fb, momentum, q_prev):
    n_t, n_r, n_z = lax.axis_size(T), lax.axis_size(R), lax.axis_size("z")
    t = lax.axis_index(T)[None]
    core = lax.axis_index("core")[None]
    tokens, wide = tokens_x.shape
    rows, width = weight.shape
    rank = q_prev.shape[0]
    ff_win = rows * n_t
    own = wide // n_r
    group = own // 4
    halves, _ = lane_halves(ff_win)
    error = error_fb[0]

    (first,) = call(
        first_kernel,
        [((n_t, rows, tokens + rank // rows * tokens), F32)],
        [SMEM] + [HBM] * 3,
        moved=2**20,
        limit=None,
        scratch_shapes=[
            pltpu.VMEM(tokens_x.shape, BF16),
            pltpu.VMEM(cotangent.shape, BF16),
            pltpu.VMEM((rank, wide), F32),
            pltpu.SemaphoreType.DMA((3,)),
        ],
    )(t, tokens_x, cotangent, q_prev)
    first, error_late, x_late = lax.optimization_barrier((first, error, tokens_x))
    kept, given = call(
        tiles_kernel,
        [((2, n_t, rows, LANES), F32)] * 2,
        [SMEM, HBM],
        moved=2 * 2**20,
        limit=None,
        scratch_shapes=[pltpu.VMEM(error.shape, F32), pltpu.SemaphoreType.DMA(())],
    )(lax.axis_index("x")[None], error_late)
    kept, given, error_late = lax.optimization_barrier((kept, given, error_late))
    moved = lax.ppermute(given, "x", [(i, i ^ 1) for i in range(4)])
    (p_error,) = call(
        project_kernel,
        [((rows, rank), F32)],
        [HBM, HBM],
        flops=2**27,
        moved=2 * 2**20,
        limit=None,
        scratch_shapes=[
            pltpu.VMEM(error.shape, F32),
            pltpu.VMEM(q_prev.shape, F32),
            pltpu.SemaphoreType.DMA((2,)),
        ],
    )(error_late, q_prev)
    bulk, x_near, kept, p_error = call(
        pack_kernel,
        [
            ((tokens + rows * n_t, wide), BF16),
            (tokens_x.shape, BF16),
            (kept.shape, F32),
            ((rows, rank), F32),
        ],
        [VMEM] * 4,
        moved=2**20,
    )(x_late, weight, kept, p_error)
    (error_t,) = call(turn_kernel, [((2 * LANES, ff_win), F32)], [VMEM] * 2, moved=2**20)(kept, moved)
    first = exchange(first, T)
    first, error_t, p_error, x_near, bulk = lax.optimization_barrier((first, error_t, p_error, x_near, bulk))
    bulk = lax.all_gather(bulk, T)
    blocks_g, blocks_e = halves * own // 4, halves * group // 2
    second, cot_all = call(
        merge_kernel,
        [((n_r, blocks_g + 1 + blocks_e, 4, LANES), F32), ((ff_win, tokens), BF16)],
        [SMEM] + [VMEM] * 4,
        moved=2 * 2**20,
        scratch_shapes=[pltpu.VMEM((wide, ff_win), F32)],
    )(t, first, x_near, p_error, error_t)
    second = exchange(second, R)
    total_t, third = call(
        sum_kernel,
        [((own, 2 * ff_win), F32), ((n_t, 1 + group // 4, 4, LANES), F32)],
        [VMEM],
        moved=2**20,
        scratch_shapes=[pltpu.VMEM((halves, own, LANES), F32), pltpu.VMEM((own, ff_win), F32)],
    )(second)
    p_pack = third[0, 0]
    third = exchange(third, T)

    q_send, gram, inverse = call(
        functools.partial(factor_kernel, n_r),
        [((n_r * n_z, group, LANES), F32), ((rank, rank), F32), ((rank, rank), F32)],
        [VMEM] * 2,
        flops=2**29,
        moved=2**20,
        scratch_shapes=[pltpu.VMEM((n_t * SUB, LANES), F32), pltpu.VMEM((max(group, SUB), LANES), F32)],
    )(third, total_t)
    mine = exchange(q_send, CHIPS)
    grad_rows, input_grad = call(
        rows_kernel,
        [((rows, width), F32), ((tokens, wide), BF16)],
        [SMEM] + [VMEM] * 3,
        flops=2**28,
        moved=8 * 2**20,
        scratch_shapes=[pltpu.VMEM((ff_win, wide), BF16)],
    )(t, cotangent, cot_all, bulk)
    basis_gram = dot(dot(inverse, gram), inverse.T)
    p_rows = p_pack.reshape(4, 4, rank).transpose(1, 0, 2).reshape(rows, rank)
    basis4 = jnp.tile(dot(p_rows, inverse.T), (1, 4))
    square = (LANES, LANES)
    weigh = jnp.where(
        iota(square, 0) // rank == iota(square, 1) // rank, jnp.tile(basis_gram, (4, 4)), 0.0
    )
    mine, grad_rows, weigh, basis4 = lax.optimization_barrier((mine, grad_rows, weigh, basis4))
    other = lax.ppermute(mine, "core", [(0, 1), (1, 0)])
    blocks = (n_z, LANES, LANES)
    limit = CLIPPING * math.sqrt(ff_win * width)
    scratch = [
        pltpu.VMEM((n_z, rank, wide), F32),
        pltpu.VMEM((n_z, rows, wide), F32),
        pltpu.SemaphoreType.DMA((2, n_z)),
    ]
    whole = [((rank, width), F32), ((rows, width), F32)]
    q_new, error_new, approx, q_gram = call(
        near_kernel,
        [*whole, ((n_z, rows, wide), F32), ((LANES, LANES), F32)],
        [SMEM] + [VMEM] * 4,
        [HBM, HBM, VMEM, VMEM],
        flops=2**30,
        moved=3 * 2**20,
        scratch_shapes=scratch,
    )(core, mine.reshape(blocks), basis4, error, grad_rows)
    q_new, error_new, momentum_new = call(
        functools.partial(far_kernel, limit),
        [*whole, ((rows, width), F32)],
        [SMEM] + [VMEM] * 8 + [HBM, HBM],
        [HBM] * 3,
        flops=2**30,
        moved=4 * 2**20,
        scratch_shapes=[
            *scratch,
            pltpu.VMEM((n_z, rows, wide), F32),
            pltpu.VMEM((2, n_z, rows, wide), F32),
            pltpu.SemaphoreType.DMA((2, n_z)),
        ],
        input_output_aliases={9: 0, 10: 1},
    )(core, other.reshape(blocks), basis4, error, grad_rows, q_gram, approx, weigh, momentum, q_new, error_new)
    return (input_grad, error_new[None], momentum_new, q_new)


def solution(mesh):
    n_r, n_t = mesh.devices.shape
    x = 4
    split = Mesh(mesh.devices.reshape(n_r // x, x, n_t // 2, 2), (*R, *T))
    placed = (P(R, T), P(T, R), P(T, None), P(R, T, None), P(T, None), P())
    return jax.shard_map(
        body,
        mesh=split,
        in_specs=placed,
        out_specs=(P(R, T), P(R, T, None), P(T, None), P()),
        check_vma=False,
    )
```

```python
import functools
import math

import jax
import jax.numpy as jnp
from jax import lax
from jax.experimental import pallas as pl
from jax.experimental.pallas import tpu as pltpu
from jax.sharding import Mesh, PartitionSpec as P

CLIPPING = 0.2
BETA = 0.9
HIGHEST = lax.Precision.HIGHEST
LANES = 128
SUB = 8
F32 = jnp.float32
BF16 = jnp.bfloat16

T = ("z", "core")
R = ("y", "x")
OWNERS = ("x", "y")
CHIPS = ("z", *OWNERS)

VMEM = pl.BlockSpec(memory_space=pltpu.VMEM)
SMEM = pl.BlockSpec(memory_space=pltpu.SMEM)
HBM = pl.BlockSpec(memory_space=pltpu.HBM)


def exchange(parts, axes):
    return lax.all_to_all(parts, axes, 0, 0, tiled=True)


def call(kernel, outs, in_specs=None, out_specs=None, flops=0, moved=0, limit=48, **more):
    outs = [jax.ShapeDtypeStruct(*o) for o in outs]
    return functools.partial(
        pl.pallas_call,
        kernel,
        out_shape=outs,
        out_specs=out_specs or [VMEM] * len(outs),
        cost_estimate=pl.CostEstimate(flops=flops, bytes_accessed=moved, transcendentals=0),
        compiler_params=pltpu.CompilerParams(vmem_limit_bytes=limit and limit * 2**20),
        **more,
    )(in_specs=in_specs)


def iota(shape, axis):
    return lax.broadcasted_iota(jnp.int32, shape, axis)


def nt(a, b, precision=HIGHEST):
    return lax.dot_general(a, b, (((1,), (1,)), ((), ())), precision=precision, preferred_element_type=F32)


def tn(a, b, precision=HIGHEST):
    return lax.dot_general(a, b, (((0,), (0,)), ((), ())), precision=precision, preferred_element_type=F32)


def dot(a, b, precision=HIGHEST):
    return jnp.dot(a, b, precision=precision, preferred_element_type=F32)


def lane_halves(ff_win):
    halves = max(ff_win // LANES, 1)
    return halves, ff_win // halves


def fold_rows(tiled, group):
    n = tiled.shape[0]
    kept = jnp.where(iota(tiled.shape, 0) // group == iota(tiled.shape, 1) // 32, tiled, 0.0)
    out = max(group, SUB)
    pick = (iota((out, n), 1) % group == iota((out, n), 0)).astype(F32)
    return dot(pick, kept)


def fetch(pairs, sems):
    copies = [pltpu.make_async_copy(src, dst, sems.at[i]) for i, (src, dst) in enumerate(pairs)]
    for copy in copies:
        copy.start()
    return copies


def first_kernel(t_ref, x_ref, c_ref, q_ref, send_ref, x, c, q, sems):
    n_t, rows, _ = send_ref.shape
    tokens, wide = x_ref.shape
    start = pl.multiple_of(t_ref[0] * wide, wide)
    for copy in fetch([(q_ref.at[:, pl.ds(start, wide)], q), (x_ref, x), (c_ref, c)], sems):
        copy.wait()
    rest, pieces = q[...], []
    for _ in range(3):
        pieces.append(rest.astype(BF16))
        rest -= pieces[-1].astype(F32)
    rank = rest.shape[0]
    y = nt(jnp.concatenate(pieces, 0), x[...], None)
    y = y[:rank] + (y[rank : 2 * rank] + y[2 * rank :])
    cot = c[...].astype(F32)
    for k in range(n_t):
        send_ref[k, :, :tokens] = cot
        for g in range(y.shape[0] // rows):
            at = tokens + g * tokens
            send_ref[k, :, at : at + tokens] = y[g * rows : (g + 1) * rows]


def tiles_kernel(x_ref, e_ref, keep_ref, send_ref, e, sem):
    n_t = keep_ref.shape[1]
    half = x_ref[0] % 2
    copy = pltpu.make_async_copy(e_ref, e, sem)
    copy.start()
    copy.wait()
    for ref, first in ((keep_ref, 2 * half), (send_ref, 2 - 2 * half)):
        for m in range(2):
            for k in range(n_t):
                ref[m, k] = e[:, pl.ds(pl.multiple_of((4 * k + first + m) * LANES, LANES), LANES)]


def project_kernel(e_ref, q_ref, pe_ref, e, q, sems):
    for copy in fetch([(e_ref, e), (q_ref, q)], sems):
        copy.wait()
    pe_ref[...] = nt(e[...], q[...])


def pack_kernel(x_ref, w_ref, a_ref, p_ref, out_ref, near_ref, tile_ref, pe_ref):
    near_ref[...] = x_ref[...]
    tile_ref[...] = a_ref[...]
    pe_ref[...] = p_ref[...]
    tokens, wide = x_ref.shape
    rows = w_ref.shape[0]
    out_ref[:tokens] = x_ref[...]
    for k in range(w_ref.shape[1] // wide):
        out_ref[tokens + k * rows : tokens + (k + 1) * rows] = w_ref[:, k * wide : (k + 1) * wide]


def turn_kernel(a_ref, b_ref, out_ref):
    same = (iota((LANES, LANES), 0) == iota((LANES, LANES), 1)).astype(BF16)
    for m in range(2):
        rest = (a_ref[m] + b_ref[m]).reshape(out_ref.shape[1], LANES)
        turned = jnp.zeros((LANES, rest.shape[0]), F32)
        for _ in range(3):
            piece = rest.astype(BF16)
            turned += nt(same, piece, None)
            rest -= piece.astype(F32)
        out_ref[m * LANES : (m + 1) * LANES] = turned


def merge_kernel(t_ref, got_ref, x_ref, pe_ref, et_ref, send_ref, cot_ref, turned_ref):
    n_t, rows, _ = got_ref.shape
    tokens, wide = x_ref.shape
    n_r = send_ref.shape[0]
    group = LANES // n_r
    ff_win = n_t * rows
    cot = got_ref[:, :, :tokens].reshape(ff_win, tokens).astype(BF16)
    cot_ref[...] = cot
    y = jnp.sum(got_ref[:, :, tokens:], 0)
    folds = y.shape[1] // tokens
    y = jnp.concatenate([y[:, g * tokens : (g + 1) * tokens] for g in range(folds)], 0)
    rank = y.shape[0]
    y4 = jnp.concatenate([y] * (LANES // rank), 0)
    tile = (iota((rank, LANES), 1) % rank == iota((rank, LANES), 0)).astype(F32)
    p4 = nt(got_ref[t_ref[0], :, :tokens], y4) + dot(pe_ref[...], tile)
    p_pack = fold_rows(p4, rows // 4)

    own = wide // n_r
    turned_ref[...] = lax.dot_general(
        x_ref[...], cot, (((0,), (1,)), ((), ())), preferred_element_type=F32
    )
    halves, width = lane_halves(ff_win)
    at = halves * (own // 4)
    for k in range(n_r):
        for h in range(halves):
            lanes = slice(h * width, (h + 1) * width)
            for g in range(own // 4):
                row = 4 * g // group * LANES + k * group + 4 * g % group
                send_ref[k, h * (own // 4) + g, :, :width] = turned_ref[row : row + 4, lanes]
            for m in range(2):
                for g in range(group // 4):
                    row = m * LANES + k * group + 4 * g
                    block = at + 1 + (m * halves + h) * (group // 4) + g
                    send_ref[k, block, :, :width] = et_ref[row : row + 4, lanes]
        send_ref[k, at] = p_pack[:4]


def rows_kernel(t_ref, c_ref, cot_ref, got_ref, g_ref, dx_ref, w):
    n_t = got_ref.shape[0]
    rows, tokens = c_ref.shape
    wide = got_ref.shape[2]
    at = pl.ds(pl.multiple_of(tokens + t_ref[0] * rows, rows), rows)
    for k in range(n_t):
        g_ref[:, k * wide : (k + 1) * wide] = dot(c_ref[...], got_ref[k, :tokens, :], None)
        w[k * rows : (k + 1) * rows] = got_ref[k, at, :]
    dx_ref[...] = tn(cot_ref[...], w[...], None).astype(BF16)


def sum_kernel(got_ref, total_ref, send_ref, scratch, error):
    n_r = got_ref.shape[0]
    n_t = send_ref.shape[0]
    own, long = total_ref.shape
    ff_win = long // 2
    rows = ff_win // n_t
    group = own // 4
    halves, width = lane_halves(ff_win)
    at = halves * (own // 4)
    got = jnp.sum(got_ref[:, : at + 1], 0)
    p_pack = got[at]
    total = jnp.zeros(total_ref.shape, F32)
    for h in range(halves):
        for g in range(own // 4):
            scratch[h, 4 * g : 4 * g + 4, :] = got[h * (own // 4) + g]
        unit, lane = iota((width, long), 0) + h * width, iota((width, long), 1)
        t, b, a = unit // rows, unit % rows // 4, unit % 4
        move = (lane == b * (SUB * n_t) + t * SUB + a).astype(F32)
        total += dot(scratch[h, :, :width], move)
    total_ref[...] = total

    p16 = jnp.concatenate([p_pack] * (rows // 4), 0)
    turns = [p16] + [pltpu.roll(p16, 32 * d, 1) for d in range(1, 4)]
    ahead = (iota(p16.shape, 1) // 32 - iota(p16.shape, 0) // 4) % 4
    for d in range(1, 4):
        p16 = jnp.where(ahead == d, turns[d], p16)
    p_all = jnp.concatenate([p16] * n_t, 0)
    for b in range(4):
        tiles = halves * (group // 4)
        start = at + 1 + b % 2 * tiles
        part = sum(got_ref[r, start : start + tiles] for r in range(n_r) if r // (n_r // 4) % 2 == b // 2)
        for h in range(halves):
            for g in range(group // 4):
                row = b * group + 4 * g
                error[row : row + 4, h * width : (h + 1) * width] = part[h * (group // 4) + g][:, :width]
    for q in range(n_t // 4):
        mask = iota(p_all.shape, 0) // rows == 4 * q + iota(p_all.shape, 1) // 32
        out = dot(error[...], jnp.where(mask, p_all, 0.0))
        turns = [out] + [pltpu.roll(out, 32 * d, 1) for d in range(1, 4)]
        row, lane = iota(out.shape, 0) // group, iota(out.shape, 1) // 32
        for s in range(4):
            kept = jnp.zeros(out.shape, F32)
            for b in range(4):
                kept = jnp.where((row == b) & (lane == b), turns[(b - s) % 4], kept)
            kept = sum(kept[b * group : (b + 1) * group] for b in range(4))
            for g in range(group // 4):
                send_ref[4 * q + s, 1 + g] = kept[4 * g : 4 * g + 4]
    for k in range(n_t):
        send_ref[k, 0] = p_pack


def factor_kernel(n_r, pack_ref, total_ref, send_ref, inverse_ref, held, wide):
    wide[...] = jnp.zeros(wide.shape, F32)
    span = held.shape[0]
    own = total_ref.shape[0]
    rank = inverse_ref.shape[0]
    group = own // 4
    held[...] = jnp.zeros(held.shape, F32)
    for k in range(pack_ref.shape[0]):
        held[k * SUB : k * SUB + 4] = pack_ref[k, 0]
    pack = held[...]
    gram4 = tn(pack, pack)
    gram = sum(gram4[b * rank : (b + 1) * rank, b * rank : (b + 1) * rank] for b in range(4))
    row, lane = iota((rank, LANES), 0), iota((rank, LANES), 1)
    work = jnp.concatenate([gram, jnp.zeros((rank, LANES - rank), F32)], 1)
    work = jnp.where(lane == row + rank, 1.0, work)
    for first in range(0, rank, 8):
        columns = [jnp.broadcast_to(work[:, first + m : first + m + 1], work.shape) for m in range(8)]
        for m in range(8):
            j = first + m
            factor = jnp.where(row > j, columns[m] * (1.0 / columns[m][j : j + 1, :]), 0.0)
            work -= factor * work[j : j + 1, :]
            for n in range(m + 1, 8):
                columns[n] -= factor * columns[n][j : j + 1, :]
    diagonal = jnp.sum(jnp.where(lane == row, work, 0.0), 1, keepdims=True)
    inverse = (work * lax.rsqrt(diagonal))[:, rank : 2 * rank]
    inverse_ref[...] = inverse
    inverse16 = jnp.concatenate([inverse] * 4, 0)
    inverse16 = jnp.concatenate([inverse16] * 4, 1)
    total = total_ref[...]
    product = jnp.zeros((own, LANES), F32)
    for b in range(4):
        part = dot(total[:, b * span : (b + 1) * span], pack)
        product = jnp.where(iota(part.shape, 1) // rank == b, part, product)
    from_error = jnp.sum(pack_ref[:, 1:], 0)
    for g in range(group // 4):
        wide[4 * g : 4 * g + 4] = from_error[g]
    tall = wide.shape[0]
    spread = (iota((own, tall), 0) % group == iota((own, tall), 1)).astype(F32)
    from_error = dot(spread, wide[...])
    product += jnp.where(iota(product.shape, 0) // group == iota(product.shape, 1) // rank, from_error, 0.0)
    q4 = nt(product, inverse16) / n_r
    q_pack = fold_rows(q4, group)[:group]
    send_ref[...] = jnp.broadcast_to(q_pack[None], send_ref.shape)


def place_blocks(near_core, blocks_ref, basis_ref, e_ref, g_ref, q_hbm, error_hbm, q, error, sems, approx_ref, gram):
    n_z = blocks_ref.shape[0]
    rows = e_ref.shape[0]
    rank = q.shape[1]
    square = (LANES, LANES)
    basis4 = basis_ref[...]
    stack = jnp.concatenate(
        [(iota(square, 0) == iota(square, 1)).astype(F32)]
        + [jnp.where(iota(basis4.shape, 1) // rank == b, basis4, 0.0) for b in range(4)],
        0,
    )
    copies = []
    blocks = blocks_ref[...].reshape(n_z * LANES, LANES)
    every = nt(stack, blocks)
    for z in range(n_z):
        both = every[:, z * LANES : (z + 1) * LANES]
        start = pl.multiple_of((2 * z + near_core) * 4 * LANES, 4 * LANES)
        for b in range(4):
            near = both[LANES + b * rows : LANES + (b + 1) * rows]
            at = pl.ds(pl.multiple_of(start + b * LANES, LANES), LANES)
            to = slice(b * LANES, (b + 1) * LANES)
            q[z, :, to] = both[b * rank : (b + 1) * rank]
            approx_ref[z, :, to] = near
            error[z, :, to] = e_ref[:, at] + g_ref[:, at] - near
        span = pl.ds(start, 4 * LANES)
        copies.append(pltpu.make_async_copy(q.at[z], q_hbm.at[:, span], sems.at[0, z]))
        copies.append(pltpu.make_async_copy(error.at[z], error_hbm.at[:, span], sems.at[1, z]))
        copies[-2].start()
        copies[-1].start()
    return gram + tn(blocks, blocks), copies


def near_kernel(core_ref, mine_ref, basis_ref, e_ref, g_ref, q_hbm, error_hbm, approx_ref, gram_ref, q, error, sems):
    gram, copies = place_blocks(
        core_ref[0], mine_ref, basis_ref, e_ref, g_ref, q_hbm, error_hbm, q, error, sems, approx_ref,
        jnp.zeros((LANES, LANES), F32),
    )
    gram_ref[...] = gram
    for copy in copies:
        copy.wait()


def far_kernel(limit, core_ref, other_ref, basis_ref, e_ref, g_ref, gram_ref, approx_ref, weigh_ref, m_ref, q_old, error_old, q_hbm, error_hbm, momentum_hbm, q, error, sems, far, out, out_sems):
    core = core_ref[0]
    gram, copies = place_blocks(
        1 - core, other_ref, basis_ref, e_ref, g_ref, q_hbm, error_hbm, q, error, sems, far, gram_ref[...]
    )
    total = jnp.sum(gram * weigh_ref[...], keepdims=True)
    scale = jnp.minimum(1.0, limit / jnp.sqrt(total))
    for z in range(other_ref.shape[0]):
        for i, ref, c in ((0, approx_ref, core), (1, far, 1 - core)):
            at = pl.ds(pl.multiple_of((2 * z + c) * 4 * LANES, 4 * LANES), 4 * LANES)
            out[i, z] = BETA * m_ref[:, at] + scale * ref[z]
            copies.append(pltpu.make_async_copy(out.at[i, z], momentum_hbm.at[:, at], out_sems.at[i, z]))
            copies[-1].start()
    for copy in copies:
        copy.wait()


def body(tokens_x, cotangent, weight, error_fb, momentum, q_prev):
    n_t, n_r, n_z = lax.axis_size(T), lax.axis_size(R), lax.axis_size("z")
    t = lax.axis_index(T)[None]
    core = lax.axis_index("core")[None]
    tokens, wide = tokens_x.shape
    rows, width = weight.shape
    rank = q_prev.shape[0]
    ff_win = rows * n_t
    own = wide // n_r
    group = own // 4
    halves, _ = lane_halves(ff_win)
    error = error_fb[0]

    (first,) = call(
        first_kernel,
        [((n_t, rows, tokens + rank // rows * tokens), F32)],
        [SMEM] + [HBM] * 3,
        moved=2**20,
        limit=None,
        scratch_shapes=[
            pltpu.VMEM(tokens_x.shape, BF16),
            pltpu.VMEM(cotangent.shape, BF16),
            pltpu.VMEM((rank, wide), F32),
            pltpu.SemaphoreType.DMA((3,)),
        ],
    )(t, tokens_x, cotangent, q_prev)
    first, error_late, x_late = lax.optimization_barrier((first, error, tokens_x))
    kept, given = call(
        tiles_kernel,
        [((2, n_t, rows, LANES), F32)] * 2,
        [SMEM, HBM],
        moved=2 * 2**20,
        limit=None,
        scratch_shapes=[pltpu.VMEM(error.shape, F32), pltpu.SemaphoreType.DMA(())],
    )(lax.axis_index("x")[None], error_late)
    kept, given, error_late = lax.optimization_barrier((kept, given, error_late))
    moved = lax.ppermute(given, "x", [(i, i ^ 1) for i in range(4)])
    (p_error,) = call(
        project_kernel,
        [((rows, rank), F32)],
        [HBM, HBM],
        flops=2**27,
        moved=2 * 2**20,
        limit=None,
        scratch_shapes=[
            pltpu.VMEM(error.shape, F32),
            pltpu.VMEM(q_prev.shape, F32),
            pltpu.SemaphoreType.DMA((2,)),
        ],
    )(error_late, q_prev)
    bulk, x_near, kept, p_error = call(
        pack_kernel,
        [
            ((tokens + rows * n_t, wide), BF16),
            (tokens_x.shape, BF16),
            (kept.shape, F32),
            ((rows, rank), F32),
        ],
        [VMEM] * 4,
        moved=2**20,
    )(x_late, weight, kept, p_error)
    (error_t,) = call(turn_kernel, [((2 * LANES, ff_win), F32)], [VMEM] * 2, moved=2**20)(kept, moved)
    first = exchange(first, T)
    first, error_t, p_error, x_near, bulk = lax.optimization_barrier((first, error_t, p_error, x_near, bulk))
    bulk = lax.all_gather(bulk, T)
    blocks_g, blocks_e = halves * own // 4, halves * group // 2
    second, cot_all = call(
        merge_kernel,
        [((n_r, blocks_g + 1 + blocks_e, 4, LANES), F32), ((ff_win, tokens), BF16)],
        [SMEM] + [VMEM] * 4,
        moved=2 * 2**20,
        scratch_shapes=[pltpu.VMEM((wide, ff_win), F32)],
    )(t, first, x_near, p_error, error_t)
    second = exchange(second, OWNERS)
    total_t, third = call(
        sum_kernel,
        [((own, 2 * ff_win), F32), ((n_t, 1 + group // 4, 4, LANES), F32)],
        [VMEM],
        moved=2**20,
        scratch_shapes=[pltpu.VMEM((halves, own, LANES), F32), pltpu.VMEM((own, ff_win), F32)],
    )(second)
    p_pack = third[0, 0]
    third = exchange(third, T)

    q_send, inverse = call(
        functools.partial(factor_kernel, n_r),
        [((n_r * n_z, group, LANES), F32), ((rank, rank), F32)],
        [VMEM] * 2,
        flops=2**29,
        moved=2**20,
        scratch_shapes=[pltpu.VMEM((n_t * SUB, LANES), F32), pltpu.VMEM((max(group, SUB), LANES), F32)],
    )(third, total_t)
    mine = exchange(q_send, CHIPS)
    grad_rows, input_grad = call(
        rows_kernel,
        [((rows, width), F32), ((tokens, wide), BF16)],
        [SMEM] + [VMEM] * 3,
        flops=2**28,
        moved=8 * 2**20,
        scratch_shapes=[pltpu.VMEM((ff_win, wide), BF16)],
    )(t, cotangent, cot_all, bulk)
    basis = dot(third[:, 0].reshape(ff_win, rank), inverse.T)
    basis_gram = tn(basis, basis)
    p_rows = p_pack.reshape(4, 4, rank).transpose(1, 0, 2).reshape(rows, rank)
    basis4 = jnp.tile(dot(p_rows, inverse.T), (1, 4))
    square = (LANES, LANES)
    weigh = jnp.where(
        iota(square, 0) // rank == iota(square, 1) // rank, jnp.tile(basis_gram, (4, 4)), 0.0
    )
    mine, grad_rows, weigh, basis4 = lax.optimization_barrier((mine, grad_rows, weigh, basis4))
    other = lax.ppermute(mine, "core", [(0, 1), (1, 0)])
    blocks = (n_z, LANES, LANES)
    limit = CLIPPING * math.sqrt(ff_win * width)
    scratch = [
        pltpu.VMEM((n_z, rank, wide), F32),
        pltpu.VMEM((n_z, rows, wide), F32),
        pltpu.SemaphoreType.DMA((2, n_z)),
    ]
    whole = [((rank, width), F32), ((rows, width), F32)]
    q_new, error_new, approx, q_gram = call(
        near_kernel,
        [*whole, ((n_z, rows, wide), F32), ((LANES, LANES), F32)],
        [SMEM] + [VMEM] * 4,
        [HBM, HBM, VMEM, VMEM],
        flops=2**30,
        moved=3 * 2**20,
        scratch_shapes=scratch,
    )(core, mine.reshape(blocks), basis4, error, grad_rows)
    q_new, error_new, momentum_new = call(
        functools.partial(far_kernel, limit),
        [*whole, ((rows, width), F32)],
        [SMEM] + [VMEM] * 8 + [HBM, HBM],
        [HBM] * 3,
        flops=2**30,
        moved=4 * 2**20,
        scratch_shapes=[
            *scratch,
            pltpu.VMEM((n_z, rows, wide), F32),
            pltpu.VMEM((2, n_z, rows, wide), F32),
            pltpu.SemaphoreType.DMA((2, n_z)),
        ],
        input_output_aliases={9: 0, 10: 1},
    )(core, other.reshape(blocks), basis4, error, grad_rows, q_gram, approx, weigh, momentum, q_new, error_new)
    return (input_grad, error_new[None], momentum_new, q_new)


def solution(mesh):
    n_r, n_t = mesh.devices.shape
    x = 4
    split = Mesh(mesh.devices.reshape(n_r // x, x, n_t // 2, 2), (*R, *T))
    placed = (P(R, T), P(T, R), P(T, None), P(R, T, None), P(T, None), P())
    return jax.shard_map(
        body,
        mesh=split,
        in_specs=placed,
        out_specs=(P(R, T), P(R, T, None), P(T, None), P()),
        check_vma=False,
    )
```

```python
import functools
import math

import jax
import jax.numpy as jnp
from jax import lax
from jax.experimental import pallas as pl
from jax.experimental.pallas import tpu as pltpu
from jax.sharding import Mesh, PartitionSpec as P

CLIPPING = 0.2
BETA = 0.9
HIGHEST = lax.Precision.HIGHEST
LANES = 128
SUB = 8
F32 = jnp.float32
BF16 = jnp.bfloat16

T = ("z", "core")
R = ("y", "x")
CHIPS = ("y", "x", "z")

VMEM = pl.BlockSpec(memory_space=pltpu.VMEM)
SMEM = pl.BlockSpec(memory_space=pltpu.SMEM)
HBM = pl.BlockSpec(memory_space=pltpu.HBM)


def exchange(parts, axes):
    return lax.all_to_all(parts, axes, 0, 0, tiled=True)


def call(kernel, outs, in_specs=None, out_specs=None, flops=0, moved=0, limit=48, **more):
    outs = [jax.ShapeDtypeStruct(*o) for o in outs]
    return functools.partial(
        pl.pallas_call,
        kernel,
        out_shape=outs,
        out_specs=out_specs or [VMEM] * len(outs),
        cost_estimate=pl.CostEstimate(flops=flops, bytes_accessed=moved, transcendentals=0),
        compiler_params=pltpu.CompilerParams(vmem_limit_bytes=limit and limit * 2**20),
        **more,
    )(in_specs=in_specs)


def iota(shape, axis):
    return lax.broadcasted_iota(jnp.int32, shape, axis)


def nt(a, b, precision=HIGHEST):
    return lax.dot_general(a, b, (((1,), (1,)), ((), ())), precision=precision, preferred_element_type=F32)


def tn(a, b, precision=HIGHEST):
    return lax.dot_general(a, b, (((0,), (0,)), ((), ())), precision=precision, preferred_element_type=F32)


def dot(a, b, precision=HIGHEST):
    return jnp.dot(a, b, precision=precision, preferred_element_type=F32)


def lane_halves(ff_win):
    halves = max(ff_win // LANES, 1)
    return halves, ff_win // halves


def fold_rows(tiled, group):
    n = tiled.shape[0]
    kept = jnp.where(iota(tiled.shape, 0) // group == iota(tiled.shape, 1) // 32, tiled, 0.0)
    out = max(group, SUB)
    pick = (iota((out, n), 1) % group == iota((out, n), 0)).astype(F32)
    return dot(pick, kept)


def fetch(pairs, sems):
    copies = [pltpu.make_async_copy(src, dst, sems.at[i]) for i, (src, dst) in enumerate(pairs)]
    for copy in copies:
        copy.start()
    return copies


def first_kernel(t_ref, x_ref, c_ref, q_ref, send_ref, x, c, q, sems):
    n_t, rows, _ = send_ref.shape
    tokens, wide = x_ref.shape
    start = pl.multiple_of(t_ref[0] * wide, wide)
    for copy in fetch([(q_ref.at[:, pl.ds(start, wide)], q), (x_ref, x), (c_ref, c)], sems):
        copy.wait()
    rest, pieces = q[...], []
    for _ in range(3):
        pieces.append(rest.astype(BF16))
        rest -= pieces[-1].astype(F32)
    rank = rest.shape[0]
    y = nt(jnp.concatenate(pieces, 0), x[...], None)
    y = y[:rank] + (y[rank : 2 * rank] + y[2 * rank :])
    cot = c[...].astype(F32)
    for k in range(n_t):
        send_ref[k, :, :tokens] = cot
        for g in range(y.shape[0] // rows):
            at = tokens + g * tokens
            send_ref[k, :, at : at + tokens] = y[g * rows : (g + 1) * rows]


def tiles_kernel(x_ref, e_ref, keep_ref, send_ref, e, sem):
    n_t = keep_ref.shape[1]
    half = x_ref[0] % 2
    copy = pltpu.make_async_copy(e_ref, e, sem)
    copy.start()
    copy.wait()
    for ref, first in ((keep_ref, 2 * half), (send_ref, 2 - 2 * half)):
        for m in range(2):
            for k in range(n_t):
                ref[m, k] = e[:, pl.ds(pl.multiple_of((4 * k + first + m) * LANES, LANES), LANES)]


def project_kernel(e_ref, q_ref, pe_ref, e, q, sems):
    for copy in fetch([(e_ref, e), (q_ref, q)], sems):
        copy.wait()
    pe_ref[...] = nt(e[...], q[...])


def pack_kernel(x_ref, w_ref, a_ref, p_ref, out_ref, near_ref, tile_ref, pe_ref):
    near_ref[...] = x_ref[...]
    tile_ref[...] = a_ref[...]
    pe_ref[...] = p_ref[...]
    tokens, wide = x_ref.shape
    rows = w_ref.shape[0]
    out_ref[:tokens] = x_ref[...]
    for k in range(w_ref.shape[1] // wide):
        out_ref[tokens + k * rows : tokens + (k + 1) * rows] = w_ref[:, k * wide : (k + 1) * wide]


def turn_kernel(a_ref, b_ref, out_ref):
    same = (iota((LANES, LANES), 0) == iota((LANES, LANES), 1)).astype(BF16)
    for m in range(2):
        rest = (a_ref[m] + b_ref[m]).reshape(out_ref.shape[1], LANES)
        turned = jnp.zeros((LANES, rest.shape[0]), F32)
        for _ in range(3):
            piece = rest.astype(BF16)
            turned += nt(same, piece, None)
            rest -= piece.astype(F32)
        out_ref[m * LANES : (m + 1) * LANES] = turned


def merge_kernel(t_ref, got_ref, x_ref, pe_ref, et_ref, send_ref, cot_ref, turned_ref):
    n_t, rows, _ = got_ref.shape
    tokens, wide = x_ref.shape
    n_r = send_ref.shape[0]
    group = LANES // n_r
    ff_win = n_t * rows
    cot = got_ref[:, :, :tokens].reshape(ff_win, tokens).astype(BF16)
    cot_ref[...] = cot
    y = jnp.sum(got_ref[:, :, tokens:], 0)
    folds = y.shape[1] // tokens
    y = jnp.concatenate([y[:, g * tokens : (g + 1) * tokens] for g in range(folds)], 0)
    rank = y.shape[0]
    y4 = jnp.concatenate([y] * (LANES // rank), 0)
    tile = (iota((rank, LANES), 1) % rank == iota((rank, LANES), 0)).astype(F32)
    p4 = nt(got_ref[t_ref[0], :, :tokens], y4) + dot(pe_ref[...], tile)
    p_pack = fold_rows(p4, rows // 4)

    own = wide // n_r
    turned_ref[...] = lax.dot_general(
        x_ref[...], cot, (((0,), (1,)), ((), ())), preferred_element_type=F32
    )
    halves, width = lane_halves(ff_win)
    at = halves * (own // 4)
    for k in range(n_r):
        for h in range(halves):
            lanes = slice(h * width, (h + 1) * width)
            for g in range(own // 4):
                row = 4 * g // group * LANES + k * group + 4 * g % group
                send_ref[k, h * (own // 4) + g, :, :width] = turned_ref[row : row + 4, lanes]
            for m in range(2):
                for g in range(group // 4):
                    row = m * LANES + k * group + 4 * g
                    block = at + 1 + (m * halves + h) * (group // 4) + g
                    send_ref[k, block, :, :width] = et_ref[row : row + 4, lanes]
        send_ref[k, at] = p_pack[:4]


def rows_kernel(t_ref, c_ref, cot_ref, got_ref, g_ref, dx_ref, w):
    n_t = got_ref.shape[0]
    rows, tokens = c_ref.shape
    wide = got_ref.shape[2]
    at = pl.ds(pl.multiple_of(tokens + t_ref[0] * rows, rows), rows)
    for k in range(n_t):
        g_ref[:, k * wide : (k + 1) * wide] = dot(c_ref[...], got_ref[k, :tokens, :], None)
        w[k * rows : (k + 1) * rows] = got_ref[k, at, :]
    dx_ref[...] = tn(cot_ref[...], w[...], None).astype(BF16)


def sum_kernel(got_ref, total_ref, send_ref, scratch, error):
    n_r = got_ref.shape[0]
    n_t = send_ref.shape[0]
    own, long = total_ref.shape
    ff_win = long // 2
    rows = ff_win // n_t
    group = own // 4
    halves, width = lane_halves(ff_win)
    at = halves * (own // 4)
    got = jnp.sum(got_ref[:, : at + 1], 0)
    p_pack = got[at]
    total = jnp.zeros(total_ref.shape, F32)
    for h in range(halves):
        for g in range(own // 4):
            scratch[h, 4 * g : 4 * g + 4, :] = got[h * (own // 4) + g]
        unit, lane = iota((width, long), 0) + h * width, iota((width, long), 1)
        t, b, a = unit // rows, unit % rows // 4, unit % 4
        move = (lane == b * (SUB * n_t) + t * SUB + a).astype(F32)
        total += dot(scratch[h, :, :width], move)
    total_ref[...] = total

    p16 = jnp.concatenate([p_pack] * (rows // 4), 0)
    turns = [p16] + [pltpu.roll(p16, 32 * d, 1) for d in range(1, 4)]
    ahead = (iota(p16.shape, 1) // 32 - iota(p16.shape, 0) // 4) % 4
    for d in range(1, 4):
        p16 = jnp.where(ahead == d, turns[d], p16)
    p_all = jnp.concatenate([p16] * n_t, 0)
    for b in range(4):
        tiles = halves * (group // 4)
        start = at + 1 + b % 2 * tiles
        part = sum(got_ref[r, start : start + tiles] for r in range(b // 2, n_r, 2))
        for h in range(halves):
            for g in range(group // 4):
                row = b * group + 4 * g
                error[row : row + 4, h * width : (h + 1) * width] = part[h * (group // 4) + g][:, :width]
    for q in range(n_t // 4):
        mask = iota(p_all.shape, 0) // rows == 4 * q + iota(p_all.shape, 1) // 32
        out = dot(error[...], jnp.where(mask, p_all, 0.0))
        turns = [out] + [pltpu.roll(out, 32 * d, 1) for d in range(1, 4)]
        row, lane = iota(out.shape, 0) // group, iota(out.shape, 1) // 32
        for s in range(4):
            kept = jnp.zeros(out.shape, F32)
            for b in range(4):
                kept = jnp.where((row == b) & (lane == b), turns[(b - s) % 4], kept)
            kept = sum(kept[b * group : (b + 1) * group] for b in range(4))
            for g in range(group // 4):
                send_ref[4 * q + s, 1 + g] = kept[4 * g : 4 * g + 4]
    for k in range(n_t):
        send_ref[k, 0] = p_pack


def factor_kernel(n_r, pack_ref, total_ref, send_ref, gram_ref, inverse_ref, held, wide):
    wide[...] = jnp.zeros(wide.shape, F32)
    span = held.shape[0]
    own = total_ref.shape[0]
    rank = gram_ref.shape[0]
    group = own // 4
    held[...] = jnp.zeros(held.shape, F32)
    for k in range(pack_ref.shape[0]):
        held[k * SUB : k * SUB + 4] = pack_ref[k, 0]
    pack = held[...]
    gram4 = tn(pack, pack)
    gram = sum(gram4[b * rank : (b + 1) * rank, b * rank : (b + 1) * rank] for b in range(4))
    gram_ref[...] = gram
    row, lane = iota((rank, LANES), 0), iota((rank, LANES), 1)
    work = jnp.concatenate([gram, jnp.zeros((rank, LANES - rank), F32)], 1)
    work = jnp.where(lane == row + rank, 1.0, work)
    for first in range(0, rank, 8):
        columns = [jnp.broadcast_to(work[:, first + m : first + m + 1], work.shape) for m in range(8)]
        for m in range(8):
            j = first + m
            factor = jnp.where(row > j, columns[m] * (1.0 / columns[m][j : j + 1, :]), 0.0)
            work -= factor * work[j : j + 1, :]
            for n in range(m + 1, 8):
                columns[n] -= factor * columns[n][j : j + 1, :]
    diagonal = jnp.sum(jnp.where(lane == row, work, 0.0), 1, keepdims=True)
    inverse = (work * lax.rsqrt(diagonal))[:, rank : 2 * rank]
    inverse_ref[...] = inverse
    inverse16 = jnp.concatenate([inverse] * 4, 0)
    inverse16 = jnp.concatenate([inverse16] * 4, 1)
    total = total_ref[...]
    product = jnp.zeros((own, LANES), F32)
    for b in range(4):
        part = dot(total[:, b * span : (b + 1) * span], pack)
        product = jnp.where(iota(part.shape, 1) // rank == b, part, product)
    from_error = jnp.sum(pack_ref[:, 1:], 0)
    for g in range(group // 4):
        wide[4 * g : 4 * g + 4] = from_error[g]
    tall = wide.shape[0]
    spread = (iota((own, tall), 0) % group == iota((own, tall), 1)).astype(F32)
    from_error = dot(spread, wide[...])
    product += jnp.where(iota(product.shape, 0) // group == iota(product.shape, 1) // rank, from_error, 0.0)
    q4 = nt(product, inverse16) / n_r
    q_pack = fold_rows(q4, group)[:group]
    send_ref[...] = jnp.broadcast_to(q_pack[None], send_ref.shape)


def place_blocks(near_core, blocks_ref, near, basis_ref, e_ref, g_ref, q_hbm, error_hbm, q, error, sems, approx_ref, gram):
    n_r, n_z, group, _ = blocks_ref.shape
    for z in range(n_z):
        for r in range(n_r):
            row = z * LANES + r * group
            near[row : row + group] = blocks_ref[r, z]
    rows = e_ref.shape[0]
    rank = q.shape[1]
    square = (LANES, LANES)
    basis4 = basis_ref[...]
    stack = jnp.concatenate(
        [(iota(square, 0) == iota(square, 1)).astype(F32)]
        + [jnp.where(iota(basis4.shape, 1) // rank == b, basis4, 0.0) for b in range(4)],
        0,
    )
    copies = []
    blocks = near[...]
    every = nt(stack, blocks)
    for z in range(n_z):
        both = every[:, z * LANES : (z + 1) * LANES]
        start = pl.multiple_of((2 * z + near_core) * 4 * LANES, 4 * LANES)
        for b in range(4):
            close = both[LANES + b * rows : LANES + (b + 1) * rows]
            at = pl.ds(pl.multiple_of(start + b * LANES, LANES), LANES)
            to = slice(b * LANES, (b + 1) * LANES)
            q[z, :, to] = both[b * rank : (b + 1) * rank]
            approx_ref[z, :, to] = close
            error[z, :, to] = e_ref[:, at] + g_ref[:, at] - close
        span = pl.ds(start, 4 * LANES)
        copies.append(pltpu.make_async_copy(q.at[z], q_hbm.at[:, span], sems.at[0, z]))
        copies.append(pltpu.make_async_copy(error.at[z], error_hbm.at[:, span], sems.at[1, z]))
        copies[-2].start()
        copies[-1].start()
    return gram + tn(blocks, blocks), copies


def near_kernel(core_ref, mine_ref, basis_ref, e_ref, g_ref, q_hbm, error_hbm, approx_ref, gram_ref, q, error, sems, near):
    gram, copies = place_blocks(
        core_ref[0], mine_ref, near, basis_ref, e_ref, g_ref, q_hbm, error_hbm, q, error, sems, approx_ref,
        jnp.zeros((LANES, LANES), F32),
    )
    gram_ref[...] = gram
    for copy in copies:
        copy.wait()


def far_kernel(limit, core_ref, other_ref, basis_ref, e_ref, g_ref, gram_ref, approx_ref, weigh_ref, m_ref, q_old, error_old, q_hbm, error_hbm, momentum_hbm, q, error, sems, near, far, out, out_sems):
    core = core_ref[0]
    gram, copies = place_blocks(
        1 - core, other_ref, near, basis_ref, e_ref, g_ref, q_hbm, error_hbm, q, error, sems, far, gram_ref[...]
    )
    total = jnp.sum(gram * weigh_ref[...], keepdims=True)
    scale = jnp.minimum(1.0, limit / jnp.sqrt(total))
    for z in range(other_ref.shape[1]):
        for i, ref, c in ((0, approx_ref, core), (1, far, 1 - core)):
            at = pl.ds(pl.multiple_of((2 * z + c) * 4 * LANES, 4 * LANES), 4 * LANES)
            out[i, z] = BETA * m_ref[:, at] + scale * ref[z]
            copies.append(pltpu.make_async_copy(out.at[i, z], momentum_hbm.at[:, at], out_sems.at[i, z]))
            copies[-1].start()
    for copy in copies:
        copy.wait()


def body(tokens_x, cotangent, weight, error_fb, momentum, q_prev):
    n_t, n_r, n_z = lax.axis_size(T), lax.axis_size(R), lax.axis_size("z")
    t = lax.axis_index(T)[None]
    core = lax.axis_index("core")[None]
    tokens, wide = tokens_x.shape
    rows, width = weight.shape
    rank = q_prev.shape[0]
    ff_win = rows * n_t
    own = wide // n_r
    group = own // 4
    halves, _ = lane_halves(ff_win)
    error = error_fb[0]

    (first,) = call(
        first_kernel,
        [((n_t, rows, tokens + rank // rows * tokens), F32)],
        [SMEM] + [HBM] * 3,
        moved=2**20,
        limit=None,
        scratch_shapes=[
            pltpu.VMEM(tokens_x.shape, BF16),
            pltpu.VMEM(cotangent.shape, BF16),
            pltpu.VMEM((rank, wide), F32),
            pltpu.SemaphoreType.DMA((3,)),
        ],
    )(t, tokens_x, cotangent, q_prev)
    first, error_late, x_late = lax.optimization_barrier((first, error, tokens_x))
    kept, given = call(
        tiles_kernel,
        [((2, n_t, rows, LANES), F32)] * 2,
        [SMEM, HBM],
        moved=2 * 2**20,
        limit=None,
        scratch_shapes=[pltpu.VMEM(error.shape, F32), pltpu.SemaphoreType.DMA(())],
    )(lax.axis_index("x")[None], error_late)
    kept, given, error_late = lax.optimization_barrier((kept, given, error_late))
    moved = lax.ppermute(given, "x", [(i, i ^ 1) for i in range(4)])
    (p_error,) = call(
        project_kernel,
        [((rows, rank), F32)],
        [HBM, HBM],
        flops=2**27,
        moved=2 * 2**20,
        limit=None,
        scratch_shapes=[
            pltpu.VMEM(error.shape, F32),
            pltpu.VMEM(q_prev.shape, F32),
            pltpu.SemaphoreType.DMA((2,)),
        ],
    )(error_late, q_prev)
    bulk, x_near, kept, p_error = call(
        pack_kernel,
        [
            ((tokens + rows * n_t, wide), BF16),
            (tokens_x.shape, BF16),
            (kept.shape, F32),
            ((rows, rank), F32),
        ],
        [VMEM] * 4,
        moved=2**20,
    )(x_late, weight, kept, p_error)
    (error_t,) = call(turn_kernel, [((2 * LANES, ff_win), F32)], [VMEM] * 2, moved=2**20)(kept, moved)
    first = exchange(first, T)
    first, error_t, p_error, x_near, bulk = lax.optimization_barrier((first, error_t, p_error, x_near, bulk))
    bulk = lax.all_gather(bulk, T)
    blocks_g, blocks_e = halves * own // 4, halves * group // 2
    second, cot_all = call(
        merge_kernel,
        [((n_r, blocks_g + 1 + blocks_e, 4, LANES), F32), ((ff_win, tokens), BF16)],
        [SMEM] + [VMEM] * 4,
        moved=2 * 2**20,
        scratch_shapes=[pltpu.VMEM((wide, ff_win), F32)],
    )(t, first, x_near, p_error, error_t)
    second = exchange(second, R)
    total_t, third = call(
        sum_kernel,
        [((own, 2 * ff_win), F32), ((n_t, 1 + group // 4, 4, LANES), F32)],
        [VMEM],
        moved=2**20,
        scratch_shapes=[pltpu.VMEM((halves, own, LANES), F32), pltpu.VMEM((own, ff_win), F32)],
    )(second)
    p_pack = third[0, 0]
    third = exchange(third, T)

    q_send, gram, inverse = call(
        functools.partial(factor_kernel, n_r),
        [((n_r * n_z, group, LANES), F32), ((rank, rank), F32), ((rank, rank), F32)],
        [VMEM] * 2,
        flops=2**29,
        moved=2**20,
        scratch_shapes=[pltpu.VMEM((n_t * SUB, LANES), F32), pltpu.VMEM((max(group, SUB), LANES), F32)],
    )(third, total_t)
    mine = exchange(q_send, CHIPS)
    grad_rows, input_grad = call(
        rows_kernel,
        [((rows, width), F32), ((tokens, wide), BF16)],
        [SMEM] + [VMEM] * 3,
        flops=2**28,
        moved=8 * 2**20,
        scratch_shapes=[pltpu.VMEM((ff_win, wide), BF16)],
    )(t, cotangent, cot_all, bulk)
    basis_gram = dot(dot(inverse, gram), inverse.T)
    p_rows = p_pack.reshape(4, 4, rank).transpose(1, 0, 2).reshape(rows, rank)
    basis4 = jnp.tile(dot(p_rows, inverse.T), (1, 4))
    square = (LANES, LANES)
    weigh = jnp.where(
        iota(square, 0) // rank == iota(square, 1) // rank, jnp.tile(basis_gram, (4, 4)), 0.0
    )
    mine, grad_rows, weigh, basis4 = lax.optimization_barrier((mine, grad_rows, weigh, basis4))
    other = lax.ppermute(mine, "core", [(0, 1), (1, 0)])
    blocks = (n_r, n_z, group, LANES)
    limit = CLIPPING * math.sqrt(ff_win * width)
    scratch = [
        pltpu.VMEM((n_z, rank, wide), F32),
        pltpu.VMEM((n_z, rows, wide), F32),
        pltpu.SemaphoreType.DMA((2, n_z)),
        pltpu.VMEM((n_z * LANES, LANES), F32),
    ]
    whole = [((rank, width), F32), ((rows, width), F32)]
    q_new, error_new, approx, q_gram = call(
        near_kernel,
        [*whole, ((n_z, rows, wide), F32), ((LANES, LANES), F32)],
        [SMEM] + [VMEM] * 4,
        [HBM, HBM, VMEM, VMEM],
        flops=2**30,
        moved=3 * 2**20,
        scratch_shapes=scratch,
    )(core, mine.reshape(blocks), basis4, error, grad_rows)
    q_new, error_new, momentum_new = call(
        functools.partial(far_kernel, limit),
        [*whole, ((rows, width), F32)],
        [SMEM] + [VMEM] * 8 + [HBM, HBM],
        [HBM] * 3,
        flops=2**30,
        moved=4 * 2**20,
        scratch_shapes=[
            *scratch,
            pltpu.VMEM((n_z, rows, wide), F32),
            pltpu.VMEM((2, n_z, rows, wide), F32),
            pltpu.SemaphoreType.DMA((2, n_z)),
        ],
        input_output_aliases={9: 0, 10: 1},
    )(core, other.reshape(blocks), basis4, error, grad_rows, q_gram, approx, weigh, momentum, q_new, error_new)
    return (input_grad, error_new[None], momentum_new, q_new)


def solution(mesh):
    n_r, n_t = mesh.devices.shape
    x = 4
    split = Mesh(mesh.devices.reshape(n_r // x, x, n_t // 2, 2), (*R, *T))
    placed = (P(R, T), P(T, R), P(T, None), P(R, T, None), P(T, None), P())
    return jax.shard_map(
        body,
        mesh=split,
        in_specs=placed,
        out_specs=(P(R, T), P(R, T, None), P(T, None), P()),
        check_vma=False,
    )
```
